32 devices in a mesh: fsdp: 32 (over z, y, x, core).
Axes of the slice: x: 2, y: 2, z: 4, core: 2. Of those that a mesh axis runs over, the one named last changes fastest.
Arguments:
- hidden_in: bfloat16 [16384, 1536], P('fsdp'), may hold values from -12 to 12
- lengths: int32 [32, 4], P('fsdp'), may hold values from 1 to 384, 512 in all within a row
- routes: int32 [16384, 8], P('fsdp'), may hold values from 0 to 15, all different within a row; in each aligned block of 512 rows (0 to 511, 512 to 1023, ...) at most 320 rows name the same one
- norm_attn: bfloat16 [1536], P('fsdp'), may hold values from 0.5 to 1.5
- w_query: bfloat16 [1536, 1536], P('fsdp'), may hold values from -0.625 to 0.625
- w_key: bfloat16 [1536, 512], P('fsdp'), may hold values from -0.625 to 0.625
- w_value: bfloat16 [1536, 512], P('fsdp'), may hold values from -0.15625 to 0.15625
- w_out: bfloat16 [1536, 1536], P('fsdp'), may hold values from -2 to 2
- norm_moe: bfloat16 [1536], P('fsdp'), may hold values from 0.5 to 1.5
- w_router: bfloat16 [1536, 16], P('fsdp'), may hold values from -0.078125 to 0.078125
- w_gate: bfloat16 [16, 1536, 512], P(None, 'fsdp'), may hold values from -0.15625 to 0.15625
- w_up: bfloat16 [16, 1536, 512], P(None, 'fsdp'), may hold values from -0.15625 to 0.15625
- w_down: bfloat16 [16, 512, 1536], P(None, 'fsdp'), may hold values from -6 to 6
- cotangent: bfloat16 [16384, 1536], P('fsdp'), may hold values from -12 to 12
Outputs:
- mixed: bfloat16 [16384, 1536], P('fsdp')
- grad_input: float32 [16384, 1536], P('fsdp')
- grad_norm_attn: float32 [1536], P('fsdp')
- grad_query: float32 [1536, 1536], P('fsdp')
- grad_key: float32 [1536, 512], P('fsdp')
- grad_value: float32 [1536, 512], P('fsdp')
- grad_out: float32 [1536, 1536], P('fsdp')
- grad_norm_moe: float32 [1536], P('fsdp')
- grad_router: float32 [1536, 16], P('fsdp')
- grad_gate: float32 [16, 1536, 512], P(None, 'fsdp')
- grad_up: float32 [16, 1536, 512], P(None, 'fsdp')
- grad_down: float32 [16, 512, 1536], P(None, 'fsdp')
The draws below stay inside these ranges and needn't reach their ends.
Inputs may be any that keep to these rules, and one draw needn't show every extreme that they name: Each device's 4 lengths sum to 512. `routes`: each row names 8 different experts; the rows of one device name no expert more than 320 times.
All inputs are finite; a program needn't handle non-finite values.
Results may differ from the reference program's by a relative error of at most 0.015.
The reference program's roundings to bfloat16 on the way count: a program that leaves them out, or rounds other values in their place, can miss the bound.
Values may be sent and summed in bfloat16 or wider, within the bound.
No kernel may reach another device: no remote copies, remote signals or barrier semaphores. Data moves between devices by JAX's collectives and lax.ppermute only.
A program may use at most 512 MiB of HBM per device.

```python
import math
import jax
import jax.numpy as jnp
import numpy as np
from jax import lax

D = 1536
HQ = 24
HK = 8
HD = 64
FE = 512
TOPK = 8
E = 16
SEQ_DEV = 4
TOK_DEV = 512
MAXLEN = 384
CAP = 320
TOKENS = 16384
N_FSDP = 32


def strengthened(drawn, key, source, target, shards_of, factor):
    owner, partner = [(jnp.arange(drawn.shape[dim]) // (drawn.shape[dim] // shards_of)).reshape([-1 if axis == dim else 1 for axis in range(drawn.ndim)]) for dim in (source, target)]
    chosen = jax.random.permutation(key, shards_of)[partner]
    strong = (owner == chosen) | (owner == (partner + shards_of // 2) % shards_of)
    return jnp.where(strong, factor * drawn, drawn)


def shard_levels(own_key, extent, cuts, least, largest):
    loudness, own = 1.0, jax.random.fold_in(own_key, 6)
    for dim, blocks in cuts:
        steps = jnp.exp(jax.random.uniform(jax.random.fold_in(own, dim), (blocks,), jnp.float32, least / len(cuts), largest / len(cuts)))
        loudness = loudness * jnp.repeat(steps, extent[dim] // blocks).reshape([-1 if axis == dim else 1 for axis in range(len(extent))])
    return loudness


def split_up(amount, total, reach, slope):
    loads = [(1 << 20) // math.isqrt(standing ** slope) + 1 for standing in range(2, amount + 1)]
    rest, holding = total - reach - (amount - 1), [1] * (amount - 1)
    while rest > 0:
        candidates = [i for i in range(amount - 1) if holding[i] < reach]
        mass, remaining = sum([loads[i] for i in candidates]), rest
        for i in candidates:
            extra = min(reach - holding[i], max(1, remaining * loads[i] // mass), rest)
            holding[i] = holding[i] + extra
            rest = rest - extra
    return np.array([reach] + holding)


def uneven_parts(rng, amount, total, reach, lean):
    if amount == 2:
        one = jax.random.randint(rng, (), max(1, total - reach), min(reach, total - 1) + 1)
        return jnp.stack([one, total - one])
    tallies = jnp.asarray(split_up(amount, total, reach, lean), jnp.int32)
    couples = (amount - 1) // 2
    giver, receiver = tallies[1:1 + 2 * couples:2], tallies[2:2 + 2 * couples:2]
    margin = jnp.minimum(giver - 1, reach - receiver)
    moved = jax.random.randint(jax.random.fold_in(rng, 1), (couples,), 0, 1 << 20) % (margin + 1)
    tallies = tallies.at[1:1 + 2 * couples:2].set(giver - moved).at[2:2 + 2 * couples:2].set(receiver + moved)
    return tallies[jax.random.permutation(jax.random.fold_in(rng, 2), amount)]


def assign_block(rng, own, number, rows, number_of, top, reach, lean):
    ranking = jax.random.permutation(rng, number_of)
    heavy_load, ordinary = shares(number_of, rows * top, reach, lean, True), shares(number_of, rows * top, reach, lean, False)
    places = jnp.arange(number_of)

    def named(sizes, turn):
        used = int((sizes > 0).sum())
        fixed = max(1, used // 4)
        shifted = fixed + (places - fixed + turn * (used - fixed)) % max(1, number_of - fixed)
        return jnp.zeros((number_of,), jnp.int32).at[ranking[jnp.where(places < fixed, places, shifted)]].set(jnp.asarray(sizes, jnp.int32))

    sizes = jnp.where(number % 4 == 0, named(heavy_load, number // 4), named(ordinary, number - number // 4 - 1))
    mixed = jax.random.permutation(jax.random.fold_in(own, 3), number_of)
    donor, receiver = mixed[0:number_of // 2 * 2:2], mixed[1:number_of // 2 * 2:2]
    room = jnp.minimum(sizes[donor] - 1, reach - sizes[receiver]) // 2
    room = jnp.where((donor == ranking[0]) | (receiver == ranking[0]) | (sizes[receiver] == 0), 0, jnp.maximum(room, 0))
    shifted = jax.random.randint(jax.random.fold_in(own, 4), (number_of // 2,), 0, 1 << 20) % (room + 1)
    sizes = sizes.at[donor].add(-shifted).at[receiver].add(shifted)
    items = jnp.searchsorted(jnp.cumsum(sizes), jnp.arange(rows * top), side="right").astype(jnp.int32)
    table = items.reshape(top, rows).T
    table = table[jax.random.permutation(jax.random.fold_in(own, 1), rows)]
    turn = jax.random.randint(jax.random.fold_in(own, 2), (rows, 1), 0, top)
    return jnp.take_along_axis(table, (jnp.arange(top)[None, :] + turn) % top, axis=1)


def shares(number_of, total, reach, slope, full):
    weights = [(1 << 20) // math.isqrt(standing ** slope) + 1 for standing in range(1, number_of + 1)]
    largest = reach if full else min(reach, max(-(-total // number_of), total * weights[0] // sum(weights)))
    least = 1 if total - largest >= number_of - 1 else 0
    counts, spare = [largest] + [least] * (number_of - 1), total - largest - least * (number_of - 1)
    while spare > 0:
        candidates = [i for i in range(1, number_of) if counts[i] < largest] or [i for i in range(1, number_of) if counts[i] < reach]
        pool, remaining = sum([weights[i] for i in candidates]), spare
        for i in candidates:
            more = min(reach - counts[i], max(1, remaining * weights[i] // pool), spare)
            counts[i] = counts[i] + more
            spare = spare - more
    return np.array(counts)


def centred(stream_key, dims, spread, bound, cuts=(), kind=jnp.bfloat16):
    values = spread * jax.random.normal(stream_key, dims, jnp.float32)
    if cuts:
        values = values * shard_levels(stream_key, dims, cuts, -0.22, 0.18)
    return jnp.clip(values, -bound, bound).astype(kind)


def heavy_noise(stream_key, dims, scale, most, cuts, heavy, kind=jnp.bfloat16):
    drawn = scale * jax.random.normal(stream_key, dims, jnp.float32)
    if cuts:
        drawn = drawn * shard_levels(stream_key, dims, cuts, -0.22, 0.18)
    return jnp.clip(strengthened(drawn, jax.random.fold_in(stream_key, 3), *heavy), -most, most).astype(kind)


def setup_inputs(seed: int = 0) -> dict:
    streams_of = jax.random.split(jax.random.key(seed), 15)
    hidden_in = heavy_noise(streams_of[0], (TOKENS, D), 1.0, 12.0, ((0, 32),), (0, 1, 32, 2.75))
    lengths = jax.vmap(lambda own: uneven_parts(own, SEQ_DEV, TOK_DEV, MAXLEN, 2))(jax.random.split(streams_of[1], N_FSDP)).reshape((N_FSDP, SEQ_DEV)).astype(jnp.int32)
    routes_keys = jax.random.split(jax.random.fold_in(streams_of[2], 1), TOKENS // TOK_DEV)
    routes_turns = jax.random.permutation(jax.random.fold_in(streams_of[2], 3), TOKENS // TOK_DEV)
    routes = jax.vmap(lambda own, number: assign_block(jax.random.fold_in(streams_of[2], 2), own, number, TOK_DEV, E, TOPK, CAP, 1))(routes_keys, routes_turns).reshape((TOKENS, TOPK))
    norm_attn = jnp.clip(1.0 + 0.1 * jax.random.normal(streams_of[3], (D,), jnp.float32), 0.5, 1.5).astype(jnp.bfloat16)
    w_query = centred(streams_of[4], (D, HQ * HD), (D // 16) ** -0.5, 0.625, ((0, 32),))
    w_key = centred(streams_of[5], (D, HK * HD), (D // 16) ** -0.5, 0.625, ((0, 32),))
    w_value = centred(streams_of[6], (D, HK * HD), D ** -0.5, 0.15625, ((0, 32),))
    w_out = centred(streams_of[7], (HQ * HD, D), 8 ** -0.5, 2.0, ((0, 32),))
    norm_moe = jnp.clip(1.0 + 0.1 * jax.random.normal(streams_of[8], (D,), jnp.float32), 0.5, 1.5).astype(jnp.bfloat16)
    w_router = centred(streams_of[9], (D, E), (4 * D) ** -0.5, 0.078125, ((0, 32),))
    w_gate = centred(streams_of[10], (E, D, FE), D ** -0.5, 0.15625, ((1, 32),))
    w_up = centred(streams_of[11], (E, D, FE), D ** -0.5, 0.15625, ((1, 32),))
    w_down = centred(streams_of[12], (E, FE, D), 1 ** -0.5, 6.0, ((1, 32),))
    cotangent = heavy_noise(streams_of[13], (TOKENS, D), 1.0, 12.0, ((0, 32),), (0, 1, 32, 2.75))
    return {"hidden_in": hidden_in, "lengths": lengths, "routes": routes, "norm_attn": norm_attn, "w_query": w_query, "w_key": w_key, "w_value": w_value, "w_out": w_out, "norm_moe": norm_moe, "w_router": w_router, "w_gate": w_gate, "w_up": w_up, "w_down": w_down, "cotangent": cotangent}


@jax.custom_vjp
def low(v):
    return lax.optimization_barrier(v.astype(jnp.bfloat16)).astype(jnp.float32)

@jax.custom_vjp
def low_back(v):
    return v

def low_keep(v):
    return (low(v), None)

def low_pass(kept, grad):
    return (grad,)

def back_keep(v):
    return (v, None)

def back_low(kept, grad):
    return (low(grad),)
low.defvjp(low_keep, low_pass)
low_back.defvjp(back_keep, back_low)
norm_eps = 1e-06
resid_scale = 0.22
score_scale = 0.015625
rope_base = 10000.0
masked_score = -1e+30

def matmul(left, right):
    return jnp.dot(left, right, precision=lax.Precision.HIGHEST, preferred_element_type=jnp.float32)

def rms_norm(values, gain):
    return values * lax.rsqrt(lax.optimization_barrier(jnp.mean(values * values, axis=-1, keepdims=True)) + norm_eps) * gain

def layout(seq_lengths, row_count):
    seq_ends = jnp.cumsum(seq_lengths).astype(jnp.int32)
    starts = (seq_ends - seq_lengths).astype(jnp.int32)
    places = jnp.arange(row_count, dtype=jnp.int32)
    member = (places[:, None] >= starts[None, :]) & (places[:, None] < seq_ends[None, :])
    labels = jnp.arange(seq_lengths.shape[0], dtype=jnp.int32)
    segment = lax.optimization_barrier(jnp.sum(jnp.where(member, labels[None, :], 0), axis=1)).astype(jnp.int32)
    offset = lax.optimization_barrier(jnp.sum(jnp.where(member, starts[None, :], 0), axis=1)).astype(jnp.int32)
    return (segment, (places - offset).astype(jnp.int32))

def rotate(values, position, turn_sign):
    row_count = values.shape[0]
    head_count = values.shape[1] // HD
    half_dim = HD // 2
    split_heads = values.reshape(row_count, head_count, HD)
    inv_freq = jnp.exp(-(jnp.arange(half_dim, dtype=jnp.float32) * (2.0 / HD)) * math.log(rope_base))
    angles = position.astype(jnp.float32)[:, None] * inv_freq[None, :]
    cosine = jnp.cos(angles)[:, None, :]
    sine_val = turn_sign * jnp.sin(angles)[:, None, :]
    lower_half = split_heads[..., :half_dim]
    upper_half = split_heads[..., half_dim:]
    turned = jnp.concatenate([lower_half * cosine - upper_half * sine_val, upper_half * cosine + lower_half * sine_val], axis=-1)
    return turned.reshape(row_count, head_count * HD)

def key_mask(segment, row_start, block_size):
    row_count = segment.shape[0]
    query_at = row_start + jnp.arange(block_size, dtype=jnp.int32)
    key_at = jnp.arange(row_count, dtype=jnp.int32)
    same_seq = segment[row_start:row_start + block_size][:, None] == segment[None, :]
    return same_seq & (key_at[None, :] <= query_at[:, None])

def attend(queries, keys_rot, values_b, segment):
    row_count = queries.shape[0]
    group_size = HQ // HK
    q_heads = queries.reshape(row_count, HK, group_size, HD).transpose(1, 0, 2, 3)
    k_heads = keys_rot.reshape(row_count, HK, HD).transpose(1, 0, 2)
    v_heads = values_b.reshape(row_count, HK, HD).transpose(1, 0, 2)

    def one_group(packed):
        q_group, k_group, v_group = packed
        block_size = min(512, row_count)
        pieces = []
        for row_start in range(0, row_count, block_size):
            q_block = q_group[row_start:row_start + block_size]
            scores = jnp.einsum('qgd,kd->gqk', q_block, k_group, precision=lax.Precision.HIGHEST) * score_scale
            scores = low_back(scores)
            visible = key_mask(segment, row_start, block_size)
            scores = jnp.where(visible[None], scores, masked_score)
            peak_val = lax.optimization_barrier(jnp.max(scores, axis=-1, keepdims=True))
            expo_val = jnp.exp(scores - peak_val)
            prob_low = low(expo_val / lax.optimization_barrier(jnp.sum(expo_val, axis=-1, keepdims=True)))
            pieces.append(jnp.einsum('gqk,kd->qgd', prob_low, v_group, precision=lax.Precision.HIGHEST))
        return jnp.concatenate(pieces, axis=0)
    attended = lax.map(jax.checkpoint(one_group), (q_heads, k_heads, v_heads))
    return attended.transpose(1, 0, 2, 3).reshape(row_count, HQ * HD)

def slot_tables(route_ids):
    flat_ids = route_ids.reshape(-1)
    row_total = flat_ids.shape[0]
    onehot = (flat_ids[:, None] == jnp.arange(E, dtype=jnp.int32)[None, :]).astype(jnp.int32)
    earlier = (jnp.cumsum(onehot, axis=0) - onehot).astype(jnp.int32)
    slot_at = lax.optimization_barrier(jnp.sum(earlier * onehot, axis=1)).astype(jnp.int32)
    places = (flat_ids * CAP + slot_at).astype(jnp.int32)
    source = jnp.zeros((E * CAP,), jnp.int32).at[places].set(jnp.arange(row_total, dtype=jnp.int32))
    filled = jnp.zeros((E * CAP,), jnp.float32).at[places].set(1.0)
    return (source.reshape(E, CAP), filled.reshape(E, CAP))

def route_gates(logits, route_ids):
    picked = route_ids[:, :, None] == jnp.arange(E, dtype=jnp.int32)[None, None, :]
    chosen = lax.optimization_barrier(jnp.sum(jnp.where(picked, logits[:, None, :], 0.0), axis=-1))
    peak_val = lax.optimization_barrier(jnp.max(chosen, axis=-1, keepdims=True))
    expo_val = jnp.exp(chosen - peak_val)
    return (expo_val / lax.optimization_barrier(jnp.sum(expo_val, axis=-1, keepdims=True)), picked)

def experts(inner_b, route_ids, w_router, w_gate, w_up, w_down):
    logits = low_back(matmul(inner_b, w_router))
    gate_mix, picked = route_gates(logits, route_ids)
    source, filled = slot_tables(route_ids)
    token_ids = source // TOPK
    slot_gate = gate_mix.reshape(-1)[source] * filled

    def expert_step(totals, packed):
        gate_weight, up_weight, down_weight, token_row, gate_row = packed
        rows_in = inner_b[token_row]
        gate_proj = low_back(matmul(rows_in, gate_weight))
        up_proj = low_back(matmul(rows_in, up_weight))
        mid_low = low(gate_proj * jax.nn.sigmoid(gate_proj) * up_proj)
        out_rows = low_back(matmul(mid_low, down_weight))
        return (totals.at[token_row].add(gate_row[:, None] * out_rows), None)
    totals, unused = lax.scan(jax.checkpoint(expert_step), jnp.zeros_like(inner_b), (w_gate, w_up, w_down, token_ids, slot_gate))
    return totals

def device_layer(hidden_f32, seq_lengths, route_ids, weights):
    norm_attn, w_query, w_key, w_value, w_out, norm_moe, w_router, w_gate, w_up, w_down = weights
    row_count = hidden_f32.shape[0]
    segment, position = layout(seq_lengths, row_count)
    normed = low(rms_norm(hidden_f32, norm_attn))
    queries = low(rotate(low_back(matmul(normed, w_query)), position, 1.0))
    keys_rot = low(rotate(low_back(matmul(normed, w_key)), position, 1.0))
    values_b = low(low_back(matmul(normed, w_value)))
    attn_out = low(low_back(attend(queries, keys_rot, values_b, segment)))
    middle = hidden_f32 + resid_scale * low_back(matmul(attn_out, w_out))
    inner_b = low(rms_norm(middle, norm_moe))
    return middle + resid_scale * experts(inner_b, route_ids, w_router, w_gate, w_up, w_down)

def reference(hidden_in, lengths, routes, norm_attn, w_query, w_key, w_value, w_out, norm_moe, w_router, w_gate, w_up, w_down, cotangent):
    weights = tuple((weight_arr.astype(jnp.float32) for weight_arr in (norm_attn, w_query, w_key, w_value, w_out, norm_moe, w_router, w_gate, w_up, w_down)))
    blocks_in = hidden_in.astype(jnp.float32).reshape(N_FSDP, TOK_DEV, D)
    route_blocks = routes.reshape(N_FSDP, TOK_DEV, TOPK)

    def forward(inputs_all, *params):

        def device_step(packed):
            return device_layer(packed[0], packed[1], packed[2], params)
        return lax.map(jax.checkpoint(device_step), (inputs_all, lengths, route_blocks))
    result, pullback = jax.vjp(forward, blocks_in, *weights)
    grads = pullback(cotangent.astype(jnp.float32).reshape(N_FSDP, TOK_DEV, D))
    return (result.reshape(TOKENS, D).astype(jnp.bfloat16), grads[0].reshape(TOKENS, D), grads[1], grads[2], grads[3], grads[4], grads[5], grads[6], grads[7], grads[8], grads[9], grads[10])
```

```python
import functools
import math

import jax
import jax.numpy as jnp
from jax import lax
from jax.experimental import pallas as pl
from jax.experimental.pallas import tpu as pltpu
from jax.sharding import PartitionSpec as P

HQ = 24
HK = 8
HD = 64
E = 16
GROUP = 8
PAIR_E = E // GROUP
LANES = 128
HEADS_STEP = 6

norm_eps = 1e-06
resid_scale = 0.22
score_scale = 0.015625
rope_base = 10000.0
masked_score = -1e30

f32 = jnp.float32
bf16 = jnp.bfloat16


def matmul(left, right):
    return jnp.dot(left, right, preferred_element_type=f32)


def contract_rows(left, right):
    return lax.dot_general(left, right, (((0,), (0,)), ((), ())), preferred_element_type=f32)


def contract_last(left, right):
    return lax.dot_general(left, right, (((1,), (1,)), ((), ())), preferred_element_type=f32)


def norm_back(values, rinv, gain, grad):
    scaled = gain * grad
    return rinv * scaled - values * rinv * rinv * rinv * jnp.mean(
        scaled * values, axis=-1, keepdims=True
    )


def layout(seq_lengths, row_count):
    seq_ends = jnp.cumsum(seq_lengths)
    starts = seq_ends - seq_lengths
    places = jnp.arange(row_count, dtype=jnp.int32)
    member = (places[:, None] >= starts[None, :]) & (places[:, None] < seq_ends[None, :])
    labels = jnp.arange(seq_lengths.shape[0], dtype=jnp.int32)
    segment = jnp.sum(jnp.where(member, labels[None, :], 0), axis=1)
    offset = jnp.sum(jnp.where(member, starts[None, :], 0), axis=1)
    return (segment, places - offset)


def turn_tables(position):
    half_dim = HD // 2
    inv_freq = jnp.exp(
        -(jnp.arange(half_dim, dtype=f32) * (2.0 / HD)) * math.log(rope_base)
    )
    angles = position.astype(f32)[:, None] * inv_freq[None, :]
    cosine, sine_val = jnp.cos(angles), jnp.sin(angles)
    return (
        jnp.concatenate([cosine] * 4, axis=1),
        jnp.concatenate([-sine_val, sine_val] * 2, axis=1),
    )


def swap(value, bit, device_count):
    return lax.ppermute(value, "fsdp", [(i, i ^ bit) for i in range(device_count)])


def group_gather(own, device_count):
    half = own.shape[0] // 2
    from2 = swap(own, 2, device_count)
    from4 = swap(own, 4, device_count)
    from1 = swap(own, 1, device_count)
    from6 = jnp.concatenate(
        [swap(from2[:half], 4, device_count), swap(from4[half:], 2, device_count)], axis=0
    )
    from3 = swap(from2, 1, device_count)
    from5 = swap(from4, 1, device_count)
    from7 = swap(from6, 1, device_count)
    return [own, from1, from2, from3, from4, from5, from6, from7]


def add_low(left, right):
    return (left.astype(f32) + right.astype(f32)).astype(bf16)


def group_sum(parts, device_count):
    half = parts[0].shape[0] // 2
    chip = {j: add_low(parts[j], swap(parts[j + 1], 1, device_count)) for j in (6, 2, 4, 0)}
    low = swap(chip[6][:half], 4, device_count)
    high = swap(chip[6][half:], 2, device_count)
    sum2 = jnp.concatenate([add_low(chip[2][:half], low), chip[2][half:]], axis=0)
    sum4 = jnp.concatenate([chip[4][:half], add_low(chip[4][half:], high)], axis=0)
    return (
        chip[0].astype(f32)
        + swap(sum2, 2, device_count).astype(f32)
        + swap(sum4, 4, device_count).astype(f32)
    )


def turn(values, cosine, sine_val, low_half):
    shifted = jnp.where(low_half, pltpu.roll(values, LANES - 32, 1), pltpu.roll(values, 32, 1))
    return values * cosine + shifted * sine_val


def half_views(pair, scale):
    lane = lax.broadcasted_iota(jnp.int32, pair.shape, 1)
    wide = pair.astype(f32) * scale
    other = pltpu.roll(wide, HD, 1)
    low = lane < HD
    return [
        [jnp.where(low, wide, 0.0).astype(bf16), jnp.where(low, other, 0.0).astype(bf16)],
        [jnp.where(low, 0.0, other).astype(bf16), jnp.where(low, 0.0, wide).astype(bf16)],
    ]


def visible_keys(seg_col, seg_row, row_start, rows, keys):
    query_at = row_start + lax.broadcasted_iota(jnp.int32, (rows, keys), 0)
    key_at = lax.broadcasted_iota(jnp.int32, (rows, keys), 1)
    return (seg_col[row_start : row_start + rows, :] == seg_row[:, :keys]) & (key_at <= query_at)


def attend_kernel(block, normed_ref, wq_ref, wk_ref, wv_ref, cos_ref, sin_ref, segc_ref, segr_ref,
                  q_ref, k_ref, v_ref, out_ref, lse_ref):
    rows_all = normed_ref.shape[0]
    normed = normed_ref[...]
    lane = lax.broadcasted_iota(jnp.int32, (rows_all, LANES), 1)
    first = (lane % HD) < (HD // 2)
    cosine, sine_val = cos_ref[...], sin_ref[...]
    q_pre = matmul(normed, wq_ref[...])
    for t in range(3):
        cols = slice(t * LANES, (t + 1) * LANES)
        q_ref[:, cols] = turn(q_pre[:, cols], cosine, sine_val, first).astype(bf16)
    k_low = turn(matmul(normed, wk_ref[...]), cosine, sine_val, first).astype(bf16)
    v_low = matmul(normed, wv_ref[...]).astype(bf16)
    k_ref[...] = k_low
    v_ref[...] = v_low
    k_views = half_views(k_low, score_scale)
    v_views = half_views(v_low, 1.0)
    seg_col, seg_row = segc_ref[...], segr_ref[...]
    for start in range(0, rows_all, block):
        keys = start + block
        visible = visible_keys(seg_col, seg_row, start, block, keys)
        lane_b = lax.broadcasted_iota(jnp.int32, (block, LANES), 1)
        norms = jnp.zeros((block, LANES), f32)
        for t in range(3):
            cols = slice(t * LANES, (t + 1) * LANES)
            q_tile = q_ref[start : start + block, cols]
            total = jnp.zeros((block, LANES), f32)
            for side in range(2):
                head = 2 * t + side
                kv = head // 3
                scores = contract_last(q_tile, k_views[side][kv][:keys])
                scores = jnp.where(visible, scores, masked_score)
                peak = jnp.max(scores, axis=-1, keepdims=True)
                expo = jnp.exp(scores - peak)
                mass = jnp.sum(expo, axis=-1, keepdims=True)
                probs = (expo * (1.0 / mass)).astype(bf16)
                total = total + matmul(probs, v_views[side][kv][:keys])
                norms = jnp.where(lane_b == head, peak + jnp.log(mass), norms)
            out_ref[start : start + block, cols] = total.astype(bf16)
        lse_ref[0, start : start + block, :] = norms


def attend_forward(normed, packed, cosine, sine_val, segment):
    rows = normed.shape[0]
    width = normed.shape[1]
    steps = HK // 2
    whole = lambda shape: pl.BlockSpec(shape, lambda i: (0, 0))
    return pl.pallas_call(
        functools.partial(attend_kernel, 128),
        grid=(steps,),
        in_specs=[
            whole((rows, width)),
            pl.BlockSpec((width, 3 * LANES), lambda i: (0, i)),
            pl.BlockSpec((width, LANES), lambda i: (0, 24 + i)),
            pl.BlockSpec((width, LANES), lambda i: (0, 28 + i)),
            whole((rows, LANES)),
            whole((rows, LANES)),
            whole((rows, 1)),
            whole((1, rows)),
        ],
        out_specs=[
            pl.BlockSpec((rows, 3 * LANES), lambda i: (0, i)),
            pl.BlockSpec((rows, LANES), lambda i: (0, i)),
            pl.BlockSpec((rows, LANES), lambda i: (0, i)),
            pl.BlockSpec((rows, 3 * LANES), lambda i: (0, i)),
            pl.BlockSpec((1, rows, LANES), lambda i: (i, 0, 0)),
        ],
        out_shape=[
            jax.ShapeDtypeStruct((rows, HQ * HD), bf16),
            jax.ShapeDtypeStruct((rows, HK * HD), bf16),
            jax.ShapeDtypeStruct((rows, HK * HD), bf16),
            jax.ShapeDtypeStruct((rows, HQ * HD), bf16),
            jax.ShapeDtypeStruct((steps, rows, LANES), f32),
        ],
        compiler_params=pltpu.CompilerParams(vmem_limit_bytes=56 * 1024 * 1024),
        cost_estimate=pl.CostEstimate(
            flops=9_000_000_000, bytes_accessed=20_000_000, transcendentals=4_000_000
        ),
    )(normed, packed, packed, packed, cosine, sine_val, segment[:, None], segment[None, :])


def attend_back_kernel(block, q_ref, k_ref, v_ref, grad_ref, lse_ref, cos_ref, sin_ref, segc_ref,
                       segr_ref, dq_ref, dk_ref, dv_ref, qt_ref, gt_ref, dkt_ref, dvt_ref):
    rows_all = q_ref.shape[0]
    lane = lax.broadcasted_iota(jnp.int32, (rows_all, LANES), 1)
    first = (lane % HD) < (HD // 2)
    k_views = half_views(k_ref[...], score_scale)
    v_views = half_views(v_ref[...], 1.0)
    qt_ref[...] = q_ref[...].astype(f32).T.astype(bf16)
    gt_ref[...] = grad_ref[...].astype(f32).T.astype(bf16)
    dkt_ref[...] = jnp.zeros_like(dkt_ref)
    dvt_ref[...] = jnp.zeros_like(dvt_ref)
    seg_col, seg_row = segc_ref[...], segr_ref[...]
    cosine, sine_val = cos_ref[...], -sin_ref[...]
    for start in range(0, rows_all, block):
        keys = start + block
        rows = slice(start, start + block)
        visible = visible_keys(seg_col, seg_row, start, block, keys)
        norms = lse_ref[0, rows, :]
        for t in range(3):
            cols = slice(t * LANES, (t + 1) * LANES)
            q_tile = q_ref[rows, cols]
            g_tile = grad_ref[rows, cols]
            q_turned = qt_ref[cols, rows]
            g_turned = gt_ref[cols, rows]
            dq = jnp.zeros((block, LANES), f32)
            for side in range(2):
                head = 2 * t + side
                kv = head // 3
                scores = contract_last(q_tile, k_views[side][kv][:keys])
                probs = jnp.where(visible, jnp.exp(scores - norms[:, head : head + 1]), 0.0)
                prob_grad = contract_last(g_tile, v_views[side][kv][:keys])
                centre = jnp.sum(probs * prob_grad, axis=-1, keepdims=True)
                score_grad = (probs * (prob_grad - centre)).astype(bf16)
                dq = dq + matmul(score_grad, k_views[side][kv][:keys])
                slot = 2 * side + kv
                dkt_ref[slot, :, :keys] += matmul(q_turned, score_grad)
                dvt_ref[slot, :, :keys] += matmul(g_turned, probs.astype(bf16))
            dq_ref[rows, cols] = turn(dq, cosine[rows], sine_val[rows], first[rows]).astype(bf16)

    def joined(ref):
        low_low, low_high, high_low, high_high = [ref[s].T for s in range(4)]
        is_low = lane < HD
        straight = jnp.where(is_low, low_low, high_high)
        crossed = pltpu.roll(jnp.where(is_low, low_high, high_low), HD, 1)
        return straight + crossed

    dk_ref[...] = turn(joined(dkt_ref) * score_scale, cosine, sine_val, first).astype(bf16)
    dv_ref[...] = joined(dvt_ref).astype(bf16)


def attend_backward(queries, keys, values, grads, norms, cosine, sine_val, segment):
    rows = queries.shape[0]
    steps = HK // 2
    whole = lambda shape: pl.BlockSpec(shape, lambda i: (0, 0))
    wide = pl.BlockSpec((rows, 3 * LANES), lambda i: (0, i))
    thin = pl.BlockSpec((rows, LANES), lambda i: (0, i))
    return pl.pallas_call(
        functools.partial(attend_back_kernel, 128),
        grid=(steps,),
        in_specs=[
            wide,
            thin,
            thin,
            wide,
            pl.BlockSpec((1, rows, LANES), lambda i: (i, 0, 0)),
            whole((rows, LANES)),
            whole((rows, LANES)),
            whole((rows, 1)),
            whole((1, rows)),
        ],
        out_specs=[wide, thin, thin],
        out_shape=[
            jax.ShapeDtypeStruct((rows, HQ * HD), bf16),
            jax.ShapeDtypeStruct((rows, HK * HD), bf16),
            jax.ShapeDtypeStruct((rows, HK * HD), bf16),
        ],
        scratch_shapes=[
            pltpu.VMEM((3 * LANES, rows), bf16),
            pltpu.VMEM((3 * LANES, rows), bf16),
            pltpu.VMEM((4, LANES, rows), f32),
            pltpu.VMEM((4, LANES, rows), f32),
        ],
        compiler_params=pltpu.CompilerParams(vmem_limit_bytes=56 * 1024 * 1024),
        cost_estimate=pl.CostEstimate(
            flops=15_000_000_000, bytes_accessed=10_000_000, transcendentals=4_000_000
        ),
    )(queries, keys, values, grads, norms, cosine, sine_val, segment[:, None], segment[None, :])


def experts_kernel(rows_ref, cot_ref, gate_ref, wgu_ref, wd_ref,
                   out_ref, grad_ref, mix_ref, gate_grad_ref, up_grad_ref, mid_ref):
    rows_in = rows_ref[...]
    cot = cot_ref[...]
    cot_wide = cot.astype(f32)
    width = rows_in.shape[1]
    hidden = wgu_ref.shape[3] // 2
    lane = lax.broadcasted_iota(jnp.int32, mix_ref.shape, 1)
    mixes = jnp.zeros(mix_ref.shape, f32)
    for e in range(PAIR_E):
        gate_row = gate_ref[:, e : e + 1]
        w_gate = wgu_ref[:, e, :, :hidden].reshape(width, hidden)
        w_up = wgu_ref[:, e, :, hidden:].reshape(width, hidden)
        w_down = wd_ref[:, e].reshape(hidden, width)
        gate_proj = matmul(rows_in, w_gate)
        up_proj = matmul(rows_in, w_up)
        sigmoid_g = 1.0 / (1.0 + jnp.exp(-gate_proj))
        active = gate_proj * sigmoid_g
        mid = (active * up_proj).astype(bf16)
        cols = slice(e * hidden, (e + 1) * hidden)
        mid_ref[:, cols] = mid
        out_grad = ((resid_scale * gate_row) * cot_wide).astype(bf16)
        mid_grad = contract_last(out_grad, w_down)
        gate_grad = (
            mid_grad * up_proj * sigmoid_g * (1.0 + gate_proj * (1.0 - sigmoid_g))
        ).astype(bf16)
        up_grad = (mid_grad * active).astype(bf16)
        gate_grad_ref[:, cols] = gate_grad
        up_grad_ref[:, cols] = up_grad
        out_rows = matmul(mid, w_down)
        mix = resid_scale * jnp.sum(cot_wide * out_rows, axis=-1, keepdims=True)
        mixes = jnp.where(lane == e, mix, mixes)
        back = contract_last(gate_grad, w_gate) + contract_last(up_grad, w_up)
        if e == 0:
            total, grads = gate_row * out_rows, back
        else:
            total, grads = total + gate_row * out_rows, grads + back
    out_ref[...] = total.astype(bf16)
    grad_ref[...] = grads.astype(bf16)
    mix_ref[...] = mixes


def run_experts(rows_in, cots, gates, w_gate_up, w_down, tile):
    count, width = rows_in.shape
    hidden = w_gate_up.shape[3] // 2
    once = pl.Buffered(1)
    tall = lambda cols: pl.BlockSpec((tile, cols), lambda i: (i, 0))
    return pl.pallas_call(
        experts_kernel,
        grid=(count // tile,),
        in_specs=[
            tall(width),
            tall(width),
            tall(PAIR_E),
            pl.BlockSpec(w_gate_up.shape, lambda i: (0, 0, 0, 0), pipeline_mode=once),
            pl.BlockSpec(w_down.shape, lambda i: (0, 0, 0, 0), pipeline_mode=once),
        ],
        out_specs=[
            tall(width),
            tall(width),
            tall(PAIR_E),
            tall(PAIR_E * hidden),
            tall(PAIR_E * hidden),
            tall(PAIR_E * hidden),
        ],
        out_shape=[
            jax.ShapeDtypeStruct((count, width), bf16),
            jax.ShapeDtypeStruct((count, width), bf16),
            jax.ShapeDtypeStruct((count, PAIR_E), f32),
            jax.ShapeDtypeStruct((count, PAIR_E * hidden), bf16),
            jax.ShapeDtypeStruct((count, PAIR_E * hidden), bf16),
            jax.ShapeDtypeStruct((count, PAIR_E * hidden), bf16),
        ],
        compiler_params=pltpu.CompilerParams(vmem_limit_bytes=60 * 1024 * 1024),
        cost_estimate=pl.CostEstimate(
            flops=12 * count * width * hidden * PAIR_E,
            bytes_accessed=60_000_000,
            transcendentals=count * hidden * PAIR_E,
        ),
    )(rows_in, cots, gates, w_gate_up, w_down)


def xor_order(stacked, place):
    for bit in (1, 2, 4):
        flipped = jnp.concatenate(
            [stacked[k ^ bit][None] for k in range(GROUP)], axis=0
        )
        stacked = jnp.where((place & bit) != 0, flipped, stacked)
    return stacked


def shards(device_count, hidden_in, lengths, routes, norm_attn, w_query, w_key, w_value, w_out,
           norm_moe, w_router, w_gate, w_up, w_down, cotangent):
    n = device_count
    layers = n // GROUP
    along = [[q + GROUP * j for j in range(layers)] for q in range(GROUP)]
    inside = [[GROUP * j + q for q in range(GROUP)] for j in range(layers)]
    place = lax.axis_index("fsdp") % GROUP
    rows, width = hidden_in.shape
    own_rows = w_query.shape[0]
    hidden = w_gate.shape[2]
    own_hidden = w_down.shape[1]

    extras = jnp.concatenate(
        [w_router, norm_attn[:, None], norm_moe[:, None], jnp.zeros((own_rows, LANES - E - 2), bf16)],
        axis=1,
    )
    packed = lax.all_gather(
        jnp.concatenate([w_query, w_out, w_key, w_value, extras], axis=1), "fsdp", axis=0, tiled=True
    )
    gathered_out = packed[:, width : 2 * width]
    extras_full = packed[:, 2 * width + 2 * HK * HD :]
    router = extras_full[:, :E]
    gains = extras_full[:, E : E + 2].astype(f32).T
    gain_one, gain_two = gains[0:1], gains[1:2]

    gate_up = jnp.concatenate([w_gate, w_up], axis=2)
    gate_up = lax.all_to_all(
        gate_up.reshape(GROUP, PAIR_E, own_rows, 2 * hidden), "fsdp", 0, 0, tiled=True,
        axis_index_groups=inside,
    )
    gate_up = gate_up.transpose(1, 0, 2, 3).reshape(PAIR_E, GROUP * own_rows, 2 * hidden)
    gate_up = lax.all_gather(gate_up, "fsdp", axis=0, axis_index_groups=along)
    down = lax.all_to_all(
        w_down.reshape(GROUP, PAIR_E, own_hidden, width), "fsdp", 0, 0, tiled=True,
        axis_index_groups=inside,
    )
    down = down.transpose(1, 0, 2, 3).reshape(PAIR_E, GROUP * own_hidden, width)
    down = lax.all_gather(down, "fsdp", axis=0, axis_index_groups=along)
    cots = jnp.concatenate(group_gather(cotangent, n), axis=0)

    hidden_f32 = hidden_in.astype(f32)
    cot_f32 = cotangent.astype(f32)
    segment, position = layout(lengths[0], rows)
    cosine, sine_val = turn_tables(position)
    rinv_one = lax.rsqrt(jnp.mean(hidden_f32 * hidden_f32, axis=-1, keepdims=True) + norm_eps)
    normed = (hidden_f32 * rinv_one * gain_one).astype(bf16)
    queries, keys, values, attn_out, norms = attend_forward(
        normed, packed, cosine, sine_val, segment
    )
    middle = hidden_f32 + resid_scale * matmul(attn_out, gathered_out)
    rinv_two = lax.rsqrt(jnp.mean(middle * middle, axis=-1, keepdims=True) + norm_eps)
    inner = (middle * rinv_two * gain_two).astype(bf16)
    all_inner = jnp.concatenate(group_gather(inner, n), axis=0)

    logits = matmul(inner, router)
    named = jnp.any(routes[:, :, None] == jnp.arange(E, dtype=jnp.int32)[None, None, :], axis=1)
    peak = jnp.max(jnp.where(named, logits, masked_score), axis=-1, keepdims=True)
    expo = jnp.where(named, jnp.exp(jnp.where(named, logits - peak, 0.0)), 0.0)
    mix = expo / jnp.sum(expo, axis=-1, keepdims=True)
    mix_turned = mix.T.reshape(GROUP, PAIR_E, rows)
    got = []
    for k in range(GROUP):
        piece = lax.dynamic_index_in_dim(mix_turned, place ^ k, 0, keepdims=False)
        got.append(swap(piece, k, n) if k else piece)
    gates = jnp.concatenate([piece.T for piece in got], axis=0)

    out_part, grad_part, mix_part, gate_grad, up_grad, mid = run_experts(
        all_inner, cots, gates, gate_up, down, rows
    )
    grad_parts = [grad_part[k * rows : (k + 1) * rows] for k in range(GROUP)]
    inner_grad = group_sum(grad_parts, n)
    back = []
    for k in range(GROUP):
        piece = mix_part[k * rows : (k + 1) * rows].T
        back.append(swap(piece, k, n) if k else piece)
    mix_grad = xor_order(jnp.stack(back), place).reshape(E, rows).T

    shared_gate_up, shared_down = [], []
    for e in range(PAIR_E):
        cols = slice(e * hidden, (e + 1) * hidden)
        out_grad = (resid_scale * gates[:, e : e + 1] * cots.astype(f32)).astype(bf16)
        both = jnp.concatenate(
            [contract_rows(all_inner, gate_grad[:, cols]), contract_rows(all_inner, up_grad[:, cols])],
            axis=1,
        ).astype(bf16)
        low = contract_rows(mid[:, cols], out_grad).astype(bf16)
        shared_gate_up.append(
            lax.psum_scatter(both, "fsdp", scatter_dimension=0, tiled=True, axis_index_groups=along)
        )
        shared_down.append(
            lax.psum_scatter(low, "fsdp", scatter_dimension=0, tiled=True, axis_index_groups=along)
        )
    both = jnp.stack([s.reshape(GROUP, own_rows, 2 * hidden) for s in shared_gate_up], axis=1)
    low = jnp.stack([s.reshape(GROUP, own_hidden, width) for s in shared_down], axis=1)
    both = lax.all_to_all(both, "fsdp", 0, 0, tiled=True, axis_index_groups=inside)
    low = lax.all_to_all(low, "fsdp", 0, 0, tiled=True, axis_index_groups=inside)
    both = both.reshape(E, own_rows, 2 * hidden).astype(f32)
    grad_gate, grad_up = both[:, :, :hidden], both[:, :, hidden:]
    grad_down = low.reshape(E, own_hidden, width).astype(f32)

    logit_grad = (
        mix * (mix_grad - jnp.sum(mix * mix_grad, axis=-1, keepdims=True))
    ).astype(bf16)
    grad_router = contract_rows(inner, logit_grad)
    inner_grad = inner_grad + contract_last(logit_grad, router)
    grad_norm_moe = jnp.sum(inner_grad * middle * rinv_two, axis=0)
    middle_grad = cot_f32 + norm_back(middle, rinv_two, gain_two, inner_grad)

    proj_grad = (resid_scale * middle_grad).astype(bf16)
    grad_out = contract_rows(attn_out, proj_grad)
    attn_grad = contract_last(proj_grad, gathered_out).astype(bf16)
    query_grad, key_grad, value_grad = attend_backward(
        queries, keys, values, attn_grad, norms, cosine, sine_val, segment
    )
    inner_grad_b, out_part = lax.optimization_barrier((inner_grad, out_part))
    out_sum = group_sum([out_part[k * rows : (k + 1) * rows] for k in range(GROUP)], n)
    mixed = (middle + resid_scale * out_sum).astype(bf16)

    grad_query = contract_rows(normed, query_grad)
    grad_key = contract_rows(normed, key_grad)
    grad_value = contract_rows(normed, value_grad)
    normed_grad = (
        contract_last(query_grad, packed[:, :width])
        + contract_last(key_grad, packed[:, 2 * width : 2 * width + HK * HD])
        + contract_last(value_grad, packed[:, 2 * width + HK * HD : 2 * width + 2 * HK * HD])
    )
    grad_norm_attn = jnp.sum(normed_grad * hidden_f32 * rinv_one, axis=0)
    input_grad = middle_grad + norm_back(hidden_f32, rinv_one, gain_one, normed_grad)

    extra_grads = jnp.concatenate(
        [
            grad_router,
            grad_norm_attn[:, None],
            grad_norm_moe[:, None],
            jnp.zeros((width, LANES - E - 2), f32),
        ],
        axis=1,
    )
    whole = jnp.concatenate([grad_query, grad_out, grad_key, grad_value, extra_grads], axis=1)
    columns = whole.shape[1]
    whole = whole.astype(bf16).reshape(layers, GROUP, own_rows, columns)
    parts = [
        lax.dynamic_index_in_dim(whole, place ^ k, 1, keepdims=False).reshape(-1, columns)
        for k in range(GROUP)
    ]
    mine = group_sum(parts, n).astype(bf16)
    mine = lax.psum_scatter(
        mine, "fsdp", scatter_dimension=0, tiled=True, axis_index_groups=along
    ).astype(f32)
    kv = HK * HD
    return (
        mixed,
        input_grad,
        mine[:, 2 * width + 2 * kv + E],
        mine[:, :width],
        mine[:, 2 * width : 2 * width + kv],
        mine[:, 2 * width + kv : 2 * width + 2 * kv],
        mine[:, width : 2 * width],
        mine[:, 2 * width + 2 * kv + E + 1],
        mine[:, 2 * width + 2 * kv : 2 * width + 2 * kv + E],
        grad_gate,
        grad_up,
        grad_down,
    )


def solution(mesh):

    in_specs = (
        P("fsdp", None),
        P("fsdp", None),
        P("fsdp", None),
        P("fsdp"),
        P("fsdp", None),
        P("fsdp", None),
        P("fsdp", None),
        P("fsdp", None),
        P("fsdp"),
        P("fsdp", None),
        P(None, "fsdp", None),
        P(None, "fsdp", None),
        P(None, "fsdp", None),
        P("fsdp", None),
    )
    out_specs = (
        P("fsdp", None),
        P("fsdp", None),
        P("fsdp"),
        P("fsdp", None),
        P("fsdp", None),
        P("fsdp", None),
        P("fsdp", None),
        P("fsdp"),
        P("fsdp", None),
        P(None, "fsdp", None),
        P(None, "fsdp", None),
        P(None, "fsdp", None),
    )
    return jax.shard_map(
        functools.partial(shards, mesh.shape["fsdp"]),
        mesh=mesh,
        in_specs=in_specs,
        out_specs=out_specs,
        check_vma=False,
    )
```

```python
import functools
import math

import jax
import jax.numpy as jnp
from jax import lax
from jax.experimental import pallas as pl
from jax.experimental.pallas import tpu as pltpu
from jax.sharding import PartitionSpec as P

HQ = 24
HK = 8
HD = 64
E = 16
GROUP = 8
PAIR_E = E // GROUP
LANES = 128
QW = HQ * HD
KW = HK * HD
QKV_WIDE = QW + 2 * KW + LANES
GAIN_ONE = E
GAIN_TWO = E + 1
VMEM_LIMIT = 58 * 1024 * 1024

norm_eps = 1e-06
resid_scale = 0.22
score_scale = 0.015625
rope_base = 10000.0
masked_score = -1e30

f32 = jnp.float32
bf16 = jnp.bfloat16


def matmul(left, right):
    return jnp.dot(left, right, preferred_element_type=f32)


def contract_rows(left, right):
    return lax.dot_general(left, right, (((0,), (0,)), ((), ())), preferred_element_type=f32)


def contract_last(left, right):
    return lax.dot_general(left, right, (((1,), (1,)), ((), ())), preferred_element_type=f32)


def layout(seq_lengths, row_count):
    seq_ends = jnp.cumsum(seq_lengths)
    starts = seq_ends - seq_lengths
    places = jnp.arange(row_count, dtype=jnp.int32)
    member = (places[:, None] >= starts[None, :]) & (places[:, None] < seq_ends[None, :])
    labels = jnp.arange(seq_lengths.shape[0], dtype=jnp.int32)
    segment = jnp.sum(jnp.where(member, labels[None, :], 0), axis=1)
    offset = jnp.sum(jnp.where(member, starts[None, :], 0), axis=1)
    return (segment, places - offset)


def turn_tables(position):
    half_dim = HD // 2
    inv_freq = jnp.exp(
        -(jnp.arange(half_dim, dtype=f32) * (2.0 / HD)) * math.log(rope_base)
    )
    angles = position.astype(f32)[:, None] * inv_freq[None, :]
    cosine, sine_val = jnp.cos(angles), jnp.sin(angles)
    return (
        jnp.concatenate([cosine] * 4, axis=1),
        jnp.concatenate([-sine_val, sine_val] * 2, axis=1),
    )


def swap(value, bit, device_count):
    return lax.ppermute(value, "fsdp", [(i, i ^ bit) for i in range(device_count)])


def shift(value, steps, device_count):
    moved = [(i, (i + GROUP * steps) % device_count) for i in range(device_count)]
    return lax.ppermute(value, "fsdp", moved)


def after(value, *needed):
    return lax.optimization_barrier((value, needed))[0]


def tie(*values):
    return lax.optimization_barrier(values)


def gather_start(own, device_count):
    return swap(own, 2, device_count), swap(own, 4, device_count)


def gather_far(from2, from4, device_count):
    half = from2.shape[0] // 2
    return swap(from2[:half], 4, device_count), swap(from4[half:], 2, device_count)


def gather_cores(own, near, far, device_count):
    other = lambda value: swap(value, 1, device_count)
    return [
        [own], [other(own)], [near[0]], [other(near[0])], [near[1]], [other(near[1])],
        list(far), [other(far[0]), other(far[1])],
    ]


def add_low(left, right):
    return (left.astype(f32) + right.astype(f32)).astype(bf16)


def sum_cores(parts, device_count):
    return add_low(parts[0], swap(parts[1], 1, device_count))


def sum_far(chip, device_count):
    half = chip.shape[0] // 2
    return swap(chip[:half], 4, device_count), swap(chip[half:], 2, device_count)


def sum_near(chip2, chip4, low, high, device_count):
    half = chip2.shape[0] // 2
    sum2 = jnp.concatenate([add_low(chip2[:half], low), chip2[half:]], axis=0)
    sum4 = jnp.concatenate([chip4[:half], add_low(chip4[half:], high)], axis=0)
    return swap(sum2, 2, device_count), swap(sum4, 4, device_count)


def add_up(parts):
    return parts[0].astype(f32) + parts[1].astype(f32) + parts[2].astype(f32)


def layer_start(stacked, layer, layers, device_count):
    pick = lambda at: lax.dynamic_index_in_dim(stacked, at % layers, 0, keepdims=False)
    return [pick(layer)] + [shift(pick(layer + k), k, device_count) for k in range(1, layers)]


def layer_add(blocks):
    total = blocks[0].astype(f32)
    for block in blocks[1:]:
        total = total + block.astype(f32)
    return total


def turn(values, cosine, sine_val, low_half):
    shifted = jnp.where(low_half, pltpu.roll(values, LANES - 32, 1), pltpu.roll(values, 32, 1))
    return values * cosine + shifted * sine_val


def half_views(pair, scale):
    lane = lax.broadcasted_iota(jnp.int32, pair.shape, 1)
    wide = pair.astype(f32) * scale
    other = pltpu.roll(wide, HD, 1)
    low = lane < HD
    return [
        [jnp.where(low, wide, 0.0).astype(bf16), jnp.where(low, other, 0.0).astype(bf16)],
        [jnp.where(low, 0.0, other).astype(bf16), jnp.where(low, 0.0, wide).astype(bf16)],
    ]


def visible_keys(seg_col, seg_row, row_start, rows, keys):
    query_at = row_start + lax.broadcasted_iota(jnp.int32, (rows, keys), 0)
    key_at = lax.broadcasted_iota(jnp.int32, (rows, keys), 1)
    return (seg_col[row_start : row_start + rows, :] == seg_row[:, :keys]) & (key_at <= query_at)


def any_spec():
    return pl.BlockSpec(memory_space=pl.ANY)


def smem_spec():
    return pl.BlockSpec(memory_space=pltpu.SMEM)


def small_cost():
    return pl.CostEstimate(flops=1_000_000, bytes_accessed=100_000, transcendentals=0)


def params():
    return pltpu.CompilerParams(vmem_limit_bytes=VMEM_LIMIT)


def whole_spec(shape):
    zeros = (0,) * len(shape)
    return pl.BlockSpec(shape, lambda *_: zeros, pipeline_mode=pl.Buffered(1))


def gather_copies(plan, refs, table_ref, dst, sems):
    copies = []
    for ref, runs in zip(refs, plan):
        rows = ref.shape[0] // len(runs)
        for number, (member, step) in enumerate(runs):
            start = pl.multiple_of(table_ref[member, step], 16)
            copies.append(
                pltpu.make_async_copy(
                    ref.at[pl.ds(number * rows, rows)],
                    dst.at[pl.ds(start, rows)],
                    sems.at[len(copies)],
                )
            )
    return copies


def spread_copies(src, table_ref, refs, sems):
    copies = []
    members, blocks = table_ref.shape
    rows = src.shape[0] // (members * blocks)
    for member in range(members):
        for block in range(blocks):
            start = pl.multiple_of(table_ref[member, block], 16)
            to = (member // 2 * blocks + block) * rows
            copies.append(
                pltpu.make_async_copy(
                    src.at[pl.ds(start, rows)], refs[member % 2].at[pl.ds(to, rows)], sems.at[len(copies)]
                )
            )
    return copies


def stack_shapes(table, width, full):
    members = table.shape[0]
    stacks = min(members, 2)
    return [jax.ShapeDtypeStruct((width // stacks, full), bf16)] * stacks


def attend_kernel(block, plan, table_ref, x_ref, cos_ref, sin_ref, segc_ref, segr_ref, *refs):
    pair = pl.program_id(0)
    rows_all, width = x_ref.shape
    at = lambda start, wide: pl.ds(pl.multiple_of(start, LANES), wide)
    if plan is None:
        wq_ref, wk_ref, wv_ref, q_ref, k_ref, v_ref, out_ref, lse_ref = refs
        normed_ref = x_ref
        w_q, w_k, w_v = wq_ref[...], wk_ref[...], wv_ref[...]
    else:
        sources = refs[: len(plan)]
        (w_out_ref, normed_ref, turned_ref, q_ref, k_ref, v_ref, out_ref, lse_ref,
         w_ref, sems, save_sem) = refs[len(plan) :]

        @pl.when(pair == 0)
        def _():
            copies = gather_copies(plan, sources, table_ref, w_ref, sems)
            for c in copies:
                c.start()
            x = x_ref[...].astype(f32)
            rinv = lax.rsqrt(jnp.mean(x * x, axis=-1, keepdims=True) + norm_eps)
            for c in copies:
                c.wait()
            pltpu.make_async_copy(w_ref, w_out_ref, save_sem).start()
            gains = w_ref[:, QW + 2 * KW :].astype(f32).T
            scaled = x * rinv * gains[GAIN_ONE : GAIN_ONE + 1, :]
            normed_ref[...] = scaled.astype(bf16)
            turned_ref[...] = scaled.T.astype(bf16)

        w_q = w_ref[:, at(pair * 3 * LANES, 3 * LANES)]
        w_k = w_ref[:, at(QW + pair * LANES, LANES)]
        w_v = w_ref[:, at(QW + KW + pair * LANES, LANES)]

    normed = normed_ref[...]
    lane = lax.broadcasted_iota(jnp.int32, (rows_all, LANES), 1)
    first = (lane % HD) < (HD // 2)
    cosine, sine_val = cos_ref[...], sin_ref[...]
    q_pre = matmul(normed, w_q)
    for t in range(3):
        cols = slice(t * LANES, (t + 1) * LANES)
        q_ref[:, cols] = turn(q_pre[:, cols], cosine, sine_val, first).astype(bf16)
    k_low = turn(matmul(normed, w_k), cosine, sine_val, first).astype(bf16)
    v_low = matmul(normed, w_v).astype(bf16)
    k_ref[...] = k_low
    v_ref[...] = v_low
    k_views = half_views(k_low, score_scale)
    v_views = half_views(v_low, 1.0)
    seg_col, seg_row = segc_ref[...], segr_ref[...]
    for start in range(0, rows_all, block):
        keys = start + block
        visible = visible_keys(seg_col, seg_row, start, block, keys)
        lane_b = lax.broadcasted_iota(jnp.int32, (block, LANES), 1)
        norms = jnp.zeros((block, LANES), f32)
        for t in range(3):
            cols = slice(t * LANES, (t + 1) * LANES)
            q_tile = q_ref[start : start + block, cols]
            total = jnp.zeros((block, LANES), f32)
            for side in range(2):
                head = 2 * t + side
                kv = head // 3
                scores = contract_last(q_tile, k_views[side][kv][:keys])
                scores = jnp.where(visible, scores, masked_score)
                peak = jnp.max(scores, axis=-1, keepdims=True)
                expo = jnp.exp(scores - peak)
                mass = jnp.sum(expo, axis=-1, keepdims=True)
                probs = (expo * (1.0 / mass)).astype(bf16)
                total = total + matmul(probs, v_views[side][kv][:keys])
                norms = jnp.where(lane_b == head, peak + jnp.log(mass), norms)
            out_ref[start : start + block, cols] = total.astype(bf16)
        lse_ref[0, start : start + block, :] = norms

    if plan is not None:
        @pl.when(pair == pl.num_programs(0) - 1)
        def _():
            pltpu.make_async_copy(w_ref, w_out_ref, save_sem).wait()


def attend_forward(base, steps, table, plan, weights, rows_in, cosine, sine_val, segment):
    rows, width = rows_in.shape
    wide = pl.BlockSpec((rows, 3 * LANES), lambda i: (0, i))
    thin = pl.BlockSpec((rows, LANES), lambda i: (0, i))
    in_specs = [
        smem_spec(),
        whole_spec((rows, width)),
        whole_spec((rows, LANES)),
        whole_spec((rows, LANES)),
        whole_spec((rows, 1)),
        whole_spec((1, rows)),
    ]
    out_specs = [wide, thin, thin, wide, pl.BlockSpec((1, rows, LANES), lambda i: (i, 0, 0))]
    out_shape = [
        jax.ShapeDtypeStruct((rows, 3 * LANES * steps), bf16),
        jax.ShapeDtypeStruct((rows, LANES * steps), bf16),
        jax.ShapeDtypeStruct((rows, LANES * steps), bf16),
        jax.ShapeDtypeStruct((rows, 3 * LANES * steps), bf16),
        jax.ShapeDtypeStruct((steps, rows, LANES), f32),
    ]
    if plan is None:
        in_specs += [
            pl.BlockSpec((width, 3 * LANES), lambda i: (0, base + i)),
            pl.BlockSpec((width, LANES), lambda i: (0, QW // LANES + base + i)),
            pl.BlockSpec((width, LANES), lambda i: (0, (QW + KW) // LANES + base + i)),
        ]
        weights = [weights] * 3
        scratch = []
    else:
        in_specs += [any_spec()] * len(weights)
        out_specs = [any_spec(), whole_spec((rows, width)), whole_spec((width, rows))] + out_specs
        out_shape = [
            jax.ShapeDtypeStruct((width, QKV_WIDE), bf16),
            jax.ShapeDtypeStruct((rows, width), bf16),
            jax.ShapeDtypeStruct((width, rows), bf16),
        ] + out_shape
        scratch = [
            pltpu.VMEM((width, QKV_WIDE), bf16),
            pltpu.SemaphoreType.DMA((sum(len(r) for r in plan),)),
            pltpu.SemaphoreType.DMA(()),
        ]
    return pl.pallas_call(
        functools.partial(attend_kernel, 128, plan),
        grid=(steps,),
        in_specs=in_specs,
        out_specs=out_specs,
        out_shape=out_shape,
        scratch_shapes=scratch,
        compiler_params=params(),
        cost_estimate=small_cost(),
    )(table, rows_in, cosine, sine_val, segment[:, None], segment[None, :], *weights)


def middle_kernel(plan, table_ref, x_ref, attn0_ref, attn1_ref, extras_ref, routes_ref, *refs):
    sources = refs[: len(plan)]
    w_out_ref, middle_ref, inner_ref, mix_ref, w_ref, sems, save_sem = refs[len(plan) :]
    copies = gather_copies(plan, sources, table_ref, w_ref, sems)
    for c in copies:
        c.start()
    extras = extras_ref[...]
    gains = extras.astype(f32).T
    rows, width = x_ref.shape
    for c in copies:
        c.wait()
    save = pltpu.make_async_copy(w_ref, w_out_ref, save_sem)
    save.start()
    half = attn0_ref.shape[1]
    product = matmul(attn0_ref[...], w_ref[:half]) + matmul(attn1_ref[...], w_ref[half:])
    middle = x_ref[...].astype(f32) + resid_scale * product
    middle_ref[...] = middle
    rinv = lax.rsqrt(jnp.mean(middle * middle, axis=-1, keepdims=True) + norm_eps)
    inner = (middle * rinv * gains[GAIN_TWO : GAIN_TWO + 1, :]).astype(bf16)
    inner_ref[:, :width] = inner
    logits = matmul(inner, extras)
    lane = lax.broadcasted_iota(jnp.int32, logits.shape, 1)
    routes = routes_ref[...]
    named = lane == routes[:, 0:1]
    for k in range(1, routes.shape[1]):
        named = named | (lane == routes[:, k : k + 1])
    chosen = jnp.where(named, logits, masked_score)
    peak = jnp.max(chosen, axis=-1, keepdims=True)
    expo = jnp.where(named, jnp.exp(chosen - peak), 0.0)
    mix = expo / jnp.sum(expo, axis=-1, keepdims=True)
    mix_ref[...] = mix
    high = mix.astype(bf16).astype(f32)
    rest = (mix - high).astype(bf16).astype(f32)
    low = mix - high - rest
    spread = high + pltpu.roll(rest, E, 1) + pltpu.roll(low, 2 * E, 1)
    inner_ref[:, width:] = spread.astype(bf16)
    save.wait()


def to_middle(table, plan, pieces, hidden_in, attn_out, extras, routes):
    rows, width = hidden_in.shape
    vmem = pl.BlockSpec(memory_space=pltpu.VMEM)
    return pl.pallas_call(
        functools.partial(middle_kernel, plan),
        in_specs=[smem_spec()] + [vmem] * 5 + [any_spec()] * len(pieces),
        out_specs=[any_spec(), vmem, vmem, vmem],
        out_shape=[
            jax.ShapeDtypeStruct((QW, width), bf16),
            jax.ShapeDtypeStruct((rows, width), f32),
            jax.ShapeDtypeStruct((rows, width + LANES), bf16),
            jax.ShapeDtypeStruct((rows, LANES), f32),
        ],
        scratch_shapes=[
            pltpu.VMEM((QW, width), bf16),
            pltpu.SemaphoreType.DMA((sum(len(r) for r in plan),)),
            pltpu.SemaphoreType.DMA(()),
        ],
        compiler_params=params(),
        cost_estimate=small_cost(),
    )(table, hidden_in, *attn_out, extras, routes, *pieces)


def middle_back_kernel(blocks, table_ref, sum0_ref, sum1_ref, sum2_ref, inner_ref, mix_ref, middle_ref,
                       cot_ref, extras_ref, attn0_ref, attn1_ref, w_ref, *refs):
    dests = refs[:blocks]
    grad_ref, attn_grad0_ref, attn_grad1_ref, wgrad_ref, sems = refs[blocks:]
    rows, width = middle_ref.shape
    total = sum0_ref[...].astype(f32) + sum1_ref[...].astype(f32) + sum2_ref[...].astype(f32)
    inner_grad, tail = total[:, :width], total[:, width:]
    lane = lax.broadcasted_iota(jnp.int32, tail.shape, 1)
    mix = mix_ref[...]
    mix_grad = tail + pltpu.roll(tail, LANES - E, 1) + pltpu.roll(tail, LANES - 2 * E, 1)
    mix_grad = jnp.where(lane < E, mix_grad, 0.0)
    logit_grad = mix * (mix_grad - jnp.sum(mix * mix_grad, axis=-1, keepdims=True))
    logit_grad = logit_grad.astype(bf16)
    extras = extras_ref[...]
    gain = extras.astype(f32).T[GAIN_TWO : GAIN_TWO + 1, :]
    inner_grad = inner_grad + contract_last(logit_grad, extras)
    middle = middle_ref[...]
    rinv = lax.rsqrt(jnp.mean(middle * middle, axis=-1, keepdims=True) + norm_eps)
    scaled = gain * inner_grad
    back = rinv * scaled - middle * (rinv * rinv * rinv * jnp.mean(scaled * middle, axis=-1, keepdims=True))
    middle_grad = cot_ref[...].astype(f32) + back
    grad_ref[...] = middle_grad
    proj_grad = (resid_scale * middle_grad).astype(bf16)
    half = attn0_ref.shape[1]
    attn_grad0_ref[...] = contract_last(proj_grad, w_ref[:half]).astype(bf16)
    attn_grad1_ref[...] = contract_last(proj_grad, w_ref[half:]).astype(bf16)
    wgrad_ref[:half, :width] = contract_rows(attn0_ref[...], proj_grad).astype(bf16)
    wgrad_ref[half:, :width] = contract_rows(attn1_ref[...], proj_grad).astype(bf16)
    wgrad_ref[:, width:] = contract_rows(inner_ref[:, :width], logit_grad).astype(bf16)
    copies = spread_copies(wgrad_ref, table_ref, dests, sems)
    for c in copies:
        c.start()
    for c in copies:
        c.wait()


def middle_back(table, sums, inner, mix, middle, cotangent, extras, attn_out, w_out):
    rows, width = middle.shape
    members, layers = table.shape
    vmem = pl.BlockSpec(memory_space=pltpu.VMEM)
    full = width + LANES
    return pl.pallas_call(
        functools.partial(middle_back_kernel, min(members, 2)),
        in_specs=[smem_spec()] + [vmem] * 11,
        out_specs=[any_spec()] * min(members, 2) + [vmem] * 3,
        out_shape=stack_shapes(table, width, full)
        + [jax.ShapeDtypeStruct((rows, width), f32)]
        + [jax.ShapeDtypeStruct((rows, QW // 2), bf16)] * 2,
        scratch_shapes=[
            pltpu.VMEM((width, full), bf16),
            pltpu.SemaphoreType.DMA((members * layers,)),
        ],
        compiler_params=params(),
        cost_estimate=small_cost(),
    )(table, *sums, inner, mix, middle, cotangent, extras, *attn_out, w_out)


def attend_back_kernel(block, blocks, table_ref, turned_ref, q_ref, k_ref, v_ref, grad_ref, lse_ref,
                       cos_ref, sin_ref, segc_ref, segr_ref, *refs):
    dests = refs[:blocks]
    dq_ref, dk_ref, dv_ref, qt_ref, gt_ref, dkt_ref, dvt_ref, wgrad_ref, sems = refs[blocks:]
    step = pl.program_id(0)
    width, rows_all = turned_ref.shape
    lane = lax.broadcasted_iota(jnp.int32, (rows_all, LANES), 1)
    first = (lane % HD) < (HD // 2)
    k_views = half_views(k_ref[...], score_scale)
    v_views = half_views(v_ref[...], 1.0)

    qt_ref[...] = q_ref[...].astype(f32).T.astype(bf16)
    gt_ref[...] = grad_ref[...].astype(f32).T.astype(bf16)
    dkt_ref[...] = jnp.zeros_like(dkt_ref)
    dvt_ref[...] = jnp.zeros_like(dvt_ref)
    seg_col, seg_row = segc_ref[...], segr_ref[...]
    cosine, sine_val = cos_ref[...], -sin_ref[...]
    for start in range(0, rows_all, block):
        keys = start + block
        rows = slice(start, start + block)
        visible = visible_keys(seg_col, seg_row, start, block, keys)
        norms = lse_ref[0, rows, :]
        for t in range(3):
            cols = slice(t * LANES, (t + 1) * LANES)
            q_tile = q_ref[rows, cols]
            g_tile = grad_ref[rows, cols]
            q_turned = qt_ref[cols, rows]
            g_turned = gt_ref[cols, rows]
            dq = jnp.zeros((block, LANES), f32)
            for side in range(2):
                head = 2 * t + side
                kv = head // 3
                scores = contract_last(q_tile, k_views[side][kv][:keys])
                probs = jnp.where(visible, jnp.exp(scores - norms[:, head : head + 1]), 0.0)
                prob_grad = contract_last(g_tile, v_views[side][kv][:keys])
                centre = jnp.sum(probs * prob_grad, axis=-1, keepdims=True)
                score_grad = (probs * (prob_grad - centre)).astype(bf16)
                dq = dq + matmul(score_grad, k_views[side][kv][:keys])
                slot = 2 * side + kv
                dkt_ref[slot, :, :keys] += matmul(q_turned, score_grad)
                dvt_ref[slot, :, :keys] += matmul(g_turned, probs.astype(bf16))
            dq_ref[rows, cols] = turn(dq, cosine[rows], sine_val[rows], first[rows]).astype(bf16)

    def joined(ref):
        low_low, low_high, high_low, high_high = [ref[s].T for s in range(4)]
        is_low = lane < HD
        straight = jnp.where(is_low, low_low, high_high)
        crossed = pltpu.roll(jnp.where(is_low, low_high, high_low), HD, 1)
        return straight + crossed

    dk_ref[...] = turn(joined(dkt_ref) * score_scale, cosine, sine_val, first).astype(bf16)
    dv_ref[...] = joined(dvt_ref).astype(bf16)
    at = lambda start, wide: pl.ds(pl.multiple_of(start, LANES), wide)
    normed_turned = turned_ref[...]
    count = wgrad_ref.shape[1] // (5 * LANES)
    wgrad_ref[:, at(step * 3 * LANES, 3 * LANES)] = matmul(normed_turned, dq_ref[...]).astype(bf16)
    wgrad_ref[:, at((3 * count + step) * LANES, LANES)] = matmul(normed_turned, dk_ref[...]).astype(bf16)
    wgrad_ref[:, at((4 * count + step) * LANES, LANES)] = matmul(normed_turned, dv_ref[...]).astype(bf16)

    @pl.when(step == pl.num_programs(0) - 1)
    def _():
        copies = spread_copies(wgrad_ref, table_ref, dests, sems)
        for c in copies:
            c.start()
        for c in copies:
            c.wait()


def attend_backward(base, steps, table, turned, queries, keys, values, grads, norms, cosine, sine_val,
                    segment):
    width, rows = turned.shape
    members, layers = table.shape
    full = 5 * steps * LANES
    wide = pl.BlockSpec((rows, 3 * LANES), lambda i: (0, base + i))
    thin = pl.BlockSpec((rows, LANES), lambda i: (0, base + i))
    out_wide = pl.BlockSpec((rows, 3 * LANES), lambda i: (0, i))
    out_thin = pl.BlockSpec((rows, LANES), lambda i: (0, i))
    return pl.pallas_call(
        functools.partial(attend_back_kernel, 128, min(members, 2)),
        grid=(steps,),
        in_specs=[
            smem_spec(),
            whole_spec((width, rows)),
            wide,
            thin,
            thin,
            wide,
            pl.BlockSpec((1, rows, LANES), lambda i: (base + i, 0, 0)),
            whole_spec((rows, LANES)),
            whole_spec((rows, LANES)),
            whole_spec((rows, 1)),
            whole_spec((1, rows)),
        ],
        out_specs=[any_spec()] * min(members, 2) + [out_wide, out_thin, out_thin],
        out_shape=stack_shapes(table, width, full)
        + [jax.ShapeDtypeStruct((rows, k * LANES * steps), bf16) for k in (3, 1, 1)],
        scratch_shapes=[
            pltpu.VMEM((3 * LANES, rows), bf16),
            pltpu.VMEM((3 * LANES, rows), bf16),
            pltpu.VMEM((4, LANES, rows), f32),
            pltpu.VMEM((4, LANES, rows), f32),
            pltpu.VMEM((width, full), bf16),
            pltpu.SemaphoreType.DMA((members * layers,)),
        ],
        compiler_params=params(),
        cost_estimate=small_cost(),
    )(table, turned, queries, keys, values, grads, norms, cosine, sine_val, segment[:, None],
      segment[None, :])


def input_kernel(x_ref, mgrad_ref, w_ref, *refs):
    *grads, out_ref = refs
    x = x_ref[...].astype(f32)
    rinv = lax.rsqrt(jnp.mean(x * x, axis=-1, keepdims=True) + norm_eps)
    gain = w_ref[:, QW + 2 * KW :].astype(f32).T[GAIN_ONE : GAIN_ONE + 1, :]
    start = [0, QW, QW + KW]
    total = None
    for number, ref in enumerate(grads):
        wide = ref.shape[1]
        kind = number % 3
        product = contract_last(ref[...], w_ref[:, start[kind] : start[kind] + wide])
        start[kind] += wide
        total = product if total is None else total + product
    scaled = gain * total
    back = rinv * scaled - x * (rinv * rinv * rinv * jnp.mean(scaled * x, axis=-1, keepdims=True))
    out_ref[...] = mgrad_ref[...] + back


def to_input(hidden_in, middle_grad, w_qkv, grads):
    vmem = pl.BlockSpec(memory_space=pltpu.VMEM)
    return pl.pallas_call(
        input_kernel,
        in_specs=[vmem] * (3 + len(grads)),
        out_specs=vmem,
        out_shape=jax.ShapeDtypeStruct(hidden_in.shape, f32),
        compiler_params=params(),
        cost_estimate=small_cost(),
    )(hidden_in, middle_grad, w_qkv, *grads)


def experts_kernel(tiles, expert, packed, has_prev, has_sums, last, *refs):
    refs = list(refs)
    take = lambda count: [refs.pop(0) for _ in range(count)]
    (place_ref,) = take(1)
    x_src = [take(len(t)) for t in tiles]
    c_src = [take(len(t)) for t in tiles]
    weights = take(1 if packed else 3)
    prev_src = [take(2) for _ in tiles] if has_prev else None
    sums_src = take(3) if has_sums else None
    dest = [take(2) for _ in tiles]
    sums_dst = take(1 if packed and last else 3)
    xs, cs, og_out, og_grad = take(4)
    prevs = take(2) if has_prev else None
    acc = take(3)
    held = take(3) if packed else weights
    sem_in, sem_out, sem_sum, sem_w = take(4)
    i = pl.program_id(0)
    count = len(tiles)
    width = cs.shape[2]
    hidden = acc[0].shape[1]

    def weight_loads():
        own, low = held[0].shape[2], held[2].shape[2]
        src = weights[0]
        pairs = [(src.at[:, :, pl.ds(0, own)], held[0]), (src.at[:, :, pl.ds(own, own)], held[1])]
        for third in range(width // hidden):
            pairs.append(
                (
                    src.at[:, :, pl.ds(2 * own + third * low, low)],
                    held[2].at[:, :, :, pl.ds(third * hidden, hidden)],
                )
            )
        return [pltpu.make_async_copy(a, b, sem_w.at[q]) for q, (a, b) in enumerate(pairs)]

    def loads(t):
        out = []
        slot = t % 2
        number = 0
        for srcs, dst in ((x_src[t], xs), (c_src[t], cs)):
            row = 0
            for r in srcs:
                rows = r.shape[0]
                out.append(pltpu.make_async_copy(r, dst.at[slot, pl.ds(row, rows)], sem_in.at[slot, number]))
                row += rows
                number += 1
        if has_prev:
            for r, dst in zip(prev_src[t], prevs):
                out.append(pltpu.make_async_copy(r, dst.at[slot], sem_in.at[slot, number]))
                number += 1
        return out

    def stores(t):
        slot = t % 2
        return [
            pltpu.make_async_copy(og_out.at[slot], dest[t][0], sem_out.at[slot, 0]),
            pltpu.make_async_copy(og_grad.at[slot], dest[t][1], sem_out.at[slot, 1]),
        ]

    def sum_loads():
        return [pltpu.make_async_copy(s, a, sem_sum.at[q]) for q, (s, a) in enumerate(zip(sums_src, acc))]

    @pl.when(i == 0)
    def _():
        for c in loads(0):
            c.start()
        if packed:
            for c in weight_loads():
                c.start()
        if has_sums:
            for c in sum_loads():
                c.start()
        else:
            for a in acc:
                a[...] = jnp.zeros_like(a)
        if packed:
            for c in weight_loads():
                c.wait()

    for t in range(count):
        @pl.when(i == t)
        def _(t=t):
            for c in loads(t):
                c.wait()
            if t + 1 < count:
                for c in loads(t + 1):
                    c.start()
            if t >= 2:
                for c in stores(t - 2):
                    c.wait()

    slot = lax.rem(i, 2)
    rows_in = xs[slot, :, :width]
    extra = xs[slot, :, width:].astype(f32)
    lane = lax.broadcasted_iota(jnp.int32, extra.shape, 1)
    mine = place_ref[0] * PAIR_E + expert
    gate_row = jnp.sum(jnp.where((lane < 3 * E) & (lax.rem(lane, E) == mine), extra, 0.0), axis=-1, keepdims=True)
    cot_wide = cs[slot].astype(f32)
    w_gate = held[0][...].reshape(width, hidden)
    w_up = held[1][...].reshape(width, hidden)
    w_down = held[2][...].reshape(hidden, width)
    gate_proj = matmul(rows_in, w_gate)
    up_proj = matmul(rows_in, w_up)
    sigmoid_g = 1.0 / (1.0 + jnp.exp(-gate_proj))
    active = gate_proj * sigmoid_g
    mid = (active * up_proj).astype(bf16)
    out_grad = ((resid_scale * gate_row) * cot_wide).astype(bf16)
    mid_grad = contract_last(out_grad, w_down)
    gate_grad = (mid_grad * up_proj * sigmoid_g * (1.0 + gate_proj * (1.0 - sigmoid_g))).astype(bf16)
    up_grad = (mid_grad * active).astype(bf16)
    out_rows = matmul(mid, w_down)
    mix = resid_scale * jnp.sum(cot_wide * out_rows, axis=-1, keepdims=True)
    mixed = gate_row * out_rows
    if has_prev:
        mixed = mixed + prevs[0][slot].astype(f32)
    og_out[slot] = mixed.astype(bf16)
    back = contract_last(gate_grad, w_gate) + contract_last(up_grad, w_up)
    if has_prev:
        back = back + prevs[1][slot, :, :width].astype(f32)
    og_grad[slot, :, :width] = back.astype(bf16)
    high = mix.astype(bf16).astype(f32)
    middle = (mix - high).astype(bf16).astype(f32)
    low = mix - high - middle
    spread = jnp.where(lane == mine, high, jnp.where(lane == mine + E, middle, jnp.where(lane == mine + 2 * E, low, 0.0)))
    if has_prev:
        spread = spread + prevs[1][slot, :, width:].astype(f32)
    og_grad[slot, :, width:] = spread.astype(bf16)
    for t in range(count):
        @pl.when(i == t)
        def _(t=t):
            for c in stores(t):
                c.start()
    if has_sums:
        @pl.when(i == 0)
        def _():
            for c in sum_loads():
                c.wait()
    acc[0][...] += contract_rows(rows_in, gate_grad)
    acc[1][...] += contract_rows(rows_in, up_grad)
    acc[2][...] += contract_rows(mid, out_grad)

    @pl.when(i == count - 1)
    def _():
        if last and packed:
            out = sums_dst[0]
            layers, members, own, _ = held[0].shape
            low = held[2].shape[2]
            out[:, :, :own] = acc[0][...].astype(bf16).reshape(layers, members, own, hidden)
            out[:, :, own : 2 * own] = acc[1][...].astype(bf16).reshape(layers, members, own, hidden)
            for third in range(width // hidden):
                piece = acc[2][:, third * hidden : (third + 1) * hidden].astype(bf16)
                start = 2 * own + third * low
                out[:, :, start : start + low] = piece.reshape(layers, members, low, hidden)
        elif last:
            for a, d in zip(acc, sums_dst):
                d[...] = a[...].astype(bf16)
        else:
            copies = [pltpu.make_async_copy(a, d, sem_sum.at[q]) for q, (a, d) in enumerate(zip(acc, sums_dst))]
            for c in copies:
                c.start()
            for c in copies:
                c.wait()
        for t in range(max(0, count - 2), count):
            for c in stores(t):
                c.wait()


def experts_call(place, expert, xs, cs, weights, own, prev, sums, last):
    tiles = [x if isinstance(x, (list, tuple)) else [x] for x in xs]
    cots = [c if isinstance(c, (list, tuple)) else [c] for c in cs]
    rows = sum(a.shape[0] for a in tiles[0])
    full = tiles[0][0].shape[1]
    packed = len(weights) == 1
    width, hidden = cots[0][0].shape[1], weights[0].shape[-1] if packed else weights[0].shape[1]
    anyspace = pl.BlockSpec(memory_space=pl.ANY)
    resident = lambda a: pl.BlockSpec(a.shape, lambda i: (0, 0), pipeline_mode=pl.Buffered(1))
    args, specs = [jnp.asarray(place, jnp.int32).reshape(1)], [pl.BlockSpec(memory_space=pltpu.SMEM)]
    for group in tiles + cots:
        args += group
        specs += [anyspace] * len(group)
    args += list(weights)
    specs += [anyspace] if packed else [resident(w) for w in weights]
    if prev is not None:
        for pair in prev:
            args += list(pair)
            specs += [anyspace] * 2
    if sums is not None:
        args += list(sums)
        specs += [anyspace] * 3
    shapes, out_specs = [], []
    for _ in tiles:
        shapes += [jax.ShapeDtypeStruct((rows, width), bf16), jax.ShapeDtypeStruct((rows, full), bf16)]
        out_specs += [anyspace] * 2
    sum_shapes = ((width, hidden), (width, hidden), (hidden, width))
    if packed and last:
        shapes.append(jax.ShapeDtypeStruct(weights[0].shape, bf16))
        out_specs.append(whole_spec(weights[0].shape))
        sum_shapes = ()
    for shape in sum_shapes:
        shapes.append(jax.ShapeDtypeStruct(shape, bf16 if last else f32))
        out_specs.append(pl.BlockSpec(shape, lambda i: (0, 0), pipeline_mode=pl.Buffered(1)) if last else anyspace)
    scratch = [
        pltpu.VMEM((2, rows, full), bf16), pltpu.VMEM((2, rows, width), bf16),
        pltpu.VMEM((2, rows, width), bf16), pltpu.VMEM((2, rows, full), bf16),
    ]
    if prev is not None:
        scratch += [pltpu.VMEM((2, rows, width), bf16), pltpu.VMEM((2, rows, full), bf16)]
    scratch += [pltpu.VMEM((width, hidden), f32), pltpu.VMEM((width, hidden), f32), pltpu.VMEM((hidden, width), f32)]
    if packed:
        layers = weights[0].shape[0]
        low = hidden // (layers * GROUP)
        scratch += [
            pltpu.VMEM((layers, GROUP, own, hidden), bf16),
            pltpu.VMEM((layers, GROUP, own, hidden), bf16),
            pltpu.VMEM((layers, GROUP, low, width), bf16),
        ]
    scratch += [pltpu.SemaphoreType.DMA(shape) for shape in ((2, 6), (2, 2), (3,), (2 + width // hidden,))]
    out = pl.pallas_call(
        functools.partial(experts_kernel, [[0] * len(t) for t in tiles], expert, packed,
                          prev is not None, sums is not None, last),
        grid=(len(tiles),),
        in_specs=specs,
        out_specs=out_specs,
        out_shape=shapes,
        scratch_shapes=scratch,
        compiler_params=pltpu.CompilerParams(vmem_limit_bytes=60 * 1024 * 1024),
        cost_estimate=small_cost(),
    )(*args)
    parts = [(out[2 * t], out[2 * t + 1]) for t in range(len(tiles))]
    return parts, tuple(out[2 * len(tiles) :])


def shards(device_count, hidden_in, lengths, routes, norm_attn, w_query, w_key, w_value, w_out,
           norm_moe, w_router, w_gate, w_up, w_down, cotangent):
    n = device_count
    layers = n // GROUP
    along = [[q + GROUP * j for j in range(layers)] for q in range(GROUP)]
    inside = [[GROUP * j + q for q in range(GROUP)] for j in range(layers)]
    me = lax.axis_index("fsdp")
    place, layer = me % GROUP, me // GROUP
    rows, width = hidden_in.shape
    own_rows = w_query.shape[0]
    hidden = w_gate.shape[2]
    own_hidden = w_down.shape[1]
    split = own_rows % 16 == 0
    thirds = width // hidden
    members = jnp.arange(GROUP, dtype=jnp.int32) ^ place
    steps = jnp.arange(layers, dtype=jnp.int32)

    extras = jnp.concatenate(
        [w_router, norm_attn[:, None], norm_moe[:, None], jnp.zeros((own_rows, LANES - E - 2), bf16)],
        axis=1,
    )
    own_attn = jnp.concatenate([w_query, w_key, w_value, extras, w_out], axis=1)
    if split:
        column = lax.all_gather(own_attn, "fsdp", axis=0, tiled=True, axis_index_groups=along)
    else:
        column = lax.all_gather(own_attn, "fsdp", axis=0, tiled=True)

    down_rows = jnp.concatenate(
        [w_down[:, :, t * hidden : (t + 1) * hidden] for t in range(thirds)], axis=1
    )
    expert_rows = jnp.concatenate([w_gate, w_up, down_rows], axis=1)
    per_expert = expert_rows.shape[1]
    expert_rows = expert_rows.reshape(GROUP, PAIR_E, per_expert, hidden).transpose(1, 0, 2, 3)
    expert_rows = lax.all_to_all(expert_rows, "fsdp", 1, 1, tiled=True, axis_index_groups=inside)
    column, expert_rows = tie(column, expert_rows)
    column, out_column = column[:, :QKV_WIDE], column[:, QKV_WIDE:]
    gathered_first = lax.all_gather(expert_rows[0], "fsdp", axis=0, axis_index_groups=along)
    gathered_second = lax.all_gather(expert_rows[1], "fsdp", axis=0, axis_index_groups=along)

    aligned = own_rows % 16 == 0 and own_hidden % 16 == 0

    def expert_parts(gathered):
        if aligned:
            return (gathered,)
        gate = gathered[:, :, :own_rows].reshape(width, hidden)
        up = gathered[:, :, own_rows : 2 * own_rows].reshape(width, hidden)
        low = gathered[:, :, 2 * own_rows :].reshape(layers, GROUP, thirds, own_hidden, hidden)
        return gate, up, low.transpose(0, 1, 3, 2, 4).reshape(hidden, width)

    def flat(pieces):
        for k, group in enumerate(pieces):
            if layers % len(group):
                pieces[k] = [jnp.concatenate(group, axis=0)]
        runs = []
        for k, group in enumerate(pieces):
            per = layers // len(group)
            runs += [[(k, c * per + j) for j in range(per)] for c in range(len(group))]
        return runs, [a for group in pieces for a in group]

    if split:
        near = gather_start(column, n)
        plan, pieces = flat(gather_cores(column, near, gather_far(*near, n), n))
        table = own_rows * (GROUP * steps[None, :] + members[:, None])
    else:
        plan, pieces = [[(0, 0)]], [column]
        table = jnp.zeros((1, 1), jnp.int32)
    table = table.astype(jnp.int32)

    core = lambda value: swap(value, 1, n)
    pieces, out_column, cotangent = tie(pieces, out_column, cotangent)
    if split:
        near = gather_start(out_column, n)
    cots_near = gather_start(cotangent, n)
    segment, position = layout(lengths[0], rows)
    cosine, sine_val = turn_tables(position)
    half = HK // 4
    w_qkv, normed, turned, *first_half = attend_forward(
        0, half, table, plan, pieces, hidden_in, cosine, sine_val, segment
    )
    extras_full = w_qkv[:, QW + 2 * KW :]
    if split:
        near, normed = tie(near, normed)
        out_far = gather_far(*near, n)
        out_other = [core(v) for v in (out_column, *near)]
    second_half = attend_forward(half, half, table, None, w_qkv, normed, cosine, sine_val, segment)
    attn_out = (first_half[3], second_half[3])
    if split:
        attn_out, out_far, out_other, cots_near = tie(attn_out, out_far, out_other, cots_near)
        _, out_pieces = flat(
            [[out_column], [out_other[0]], [near[0]], [out_other[1]], [near[1]], [out_other[2]],
             list(out_far), [core(v) for v in out_far]]
        )
    else:
        out_pieces = [out_column]

    cots_core = [core(cotangent), core(cots_near[0]), core(cots_near[1])]
    w_out_full, middle, inner, mix = to_middle(
        table, plan, out_pieces, hidden_in, attn_out, extras_full, routes
    )
    cots_core = after(cots_core, inner)

    def expert_sums(sums):
        if len(sums) == 1:
            return lax.psum_scatter(
                sums[0], "fsdp", scatter_dimension=0, tiled=True, axis_index_groups=along
            )[0]
        gate, up, low = sums
        low = low.reshape(layers, GROUP, own_hidden, thirds, hidden).transpose(0, 1, 3, 2, 4)
        joined = jnp.concatenate(
            [
                gate.reshape(layers, GROUP, own_rows, hidden),
                up.reshape(layers, GROUP, own_rows, hidden),
                low.reshape(layers, GROUP, thirds * own_hidden, hidden),
            ],
            axis=2,
        )
        return lax.psum_scatter(
            joined, "fsdp", scatter_dimension=0, tiled=True, axis_index_groups=along
        )[0]

    first = expert_parts(gathered_first)
    second = expert_parts(gathered_second)
    part = {}

    def run(expert, tiles, xs, cs, weights, sums, last):
        done, sums = experts_call(
            place, expert, xs, cs, weights, own_rows, [part[k] for k in tiles] if expert else None, sums, last
        )
        part.update(zip(tiles, done))
        return sums

    inner_near = gather_start(inner, n)
    x_own, c_own = [[inner], [core(inner)]], [[cotangent], [cots_core[0]]]
    sums = run(0, [0, 1], x_own, c_own, first, None, False)
    inner_near = after(inner_near, sums)
    inner_far = gather_far(*inner_near, n)
    cots_far = gather_far(*tie(*cots_near, *inner_near)[:2], n)
    x_near = [[inner_near[0]], [core(inner_near[0])], [inner_near[1]], [core(inner_near[1])]]
    c_near = [[cots_near[0]], [cots_core[1]], [cots_near[1]], [cots_core[2]]]
    sums = run(0, [2, 3, 4, 5], x_near, c_near, first, sums, False)
    inner_far, cots_far = after((inner_far, cots_far), sums)
    x_far = [list(inner_far), [core(v) for v in inner_far]]
    c_far = [list(cots_far), [core(v) for v in cots_far]]
    sums0 = run(0, [6, 7], x_far, c_far, first, sums, True)
    shared0 = expert_sums(sums0)

    sums = run(1, [6, 7], x_far, c_far, second, None, False)
    chip6, out6 = [sum_cores([part[6][i], part[7][i]], n) for i in (1, 0)]
    x_near[0], chip6, out6 = tie(x_near[0], chip6, out6)
    far_sums, out_far = sum_far(chip6, n), sum_far(out6, n)
    sums = run(1, [2, 3, 4, 5], x_near, c_near, second, sums, False)
    done = [part[k] for k in (2, 3, 4, 5)]
    far_sums, out_far, sums, done = tie(far_sums, out_far, sums, done)
    part.update(zip((2, 3, 4, 5), done))
    chip2, chip4 = [sum_cores([part[k][1], part[k + 1][1]], n) for k in (2, 4)]
    x_own[0], chip2, chip4, shared0 = tie(x_own[0], chip2, chip4, shared0)
    inner_two, inner_four = sum_near(chip2, chip4, *far_sums, n)
    out_core = [core(part[3][0]), core(part[5][0])]
    sums = run(1, [0, 1], x_own, c_own, second, sums, True)
    inner_two, inner_four, out_core, sums, part[0], part[1] = tie(
        inner_two, inner_four, out_core, sums, part[0], part[1]
    )
    shared1 = expert_sums(sums)
    inner_chip = sum_cores([part[0][1], part[1][1]], n)
    out_chips = [add_low(part[k][0], other) for k, other in zip((2, 4), out_core)]
    out_chips, inner_chip = tie(out_chips, inner_chip)
    out_near = sum_near(*out_chips, *out_far, n)
    out_other = core(part[1][0])
    *out_grads, middle_grad, attn_grad0, attn_grad1 = middle_back(
        table, (inner_chip, inner_two, inner_four), inner, mix, middle, cotangent, extras_full, attn_out,
        w_out_full,
    )

    def chips_of(stacks):
        return add_low(stacks[0], core(stacks[1])) if split else stacks[0]

    def far_of(chips):
        rows_each = chips.shape[0] // 4
        return sum_far(chips[3 * rows_each :], n) if split else ()

    def near_of(chips, far):
        rows_each = chips.shape[0] // 4
        if not split:
            return ()
        return sum_near(chips[rows_each : 2 * rows_each], chips[2 * rows_each : 3 * rows_each], *far, n)

    def owned(chips, near):
        return add_up([chips[: chips.shape[0] // 4], *near]).astype(bf16)

    def over_layers(pairs):
        if not split:
            sums = [
                lax.psum_scatter(chips, "fsdp", scatter_dimension=0, tiled=True) for chips, _ in pairs
            ]
            return [jnp.concatenate(sums, axis=1)]
        total = jnp.concatenate([owned(*pair) for pair in pairs], axis=1)
        return layer_start(total.reshape(layers, own_rows, -1), layer, layers, n)

    def back(base, steps, half_set, grads):
        return attend_backward(
            base, steps, table, turned, *half_set[:3], grads, half_set[4], cosine, sine_val, segment
        )

    wo_chips = chips_of(out_grads)
    attn_grad0, wo_chips = tie(attn_grad0, wo_chips)
    wo_far = far_of(wo_chips)
    to_owner = lambda block: lax.all_to_all(
        block, "fsdp", 0, 0, tiled=True, axis_index_groups=inside
    )
    owned0 = to_owner(shared0)
    *stacks0, dq0, dk0, dv0 = back(0, half, first_half, attn_grad0)
    owned0, out_other, wo_far, stacks0, dq0 = tie(owned0, out_other, wo_far, stacks0, dq0)

    chips0 = chips_of(stacks0)
    attn_grad1, chips0, shared1 = tie(attn_grad1, chips0, shared1)
    wo_near, far0 = near_of(wo_chips, wo_far), far_of(chips0)
    *stacks1, dq1, dk1, dv1 = back(0, half // 2, second_half, attn_grad1)
    wo_near, far0, stacks1, dq1, out_near = tie(wo_near, far0, stacks1, dq1, out_near)

    chips1 = chips_of(stacks1)
    attn_grad1, chips1 = tie(attn_grad1, chips1)
    near0, far1 = near_of(chips0, far0), far_of(chips1)
    *stacks2, dq2, dk2, dv2 = back(half // 2, half - half // 2, second_half, attn_grad1)
    near0, far1, stacks2, dq2, wo_near = tie(near0, far1, stacks2, dq2, wo_near)

    chips2 = chips_of(stacks2)
    dq2, chips2 = tie(dq2, chips2)
    near1, far2 = near_of(chips1, far1), far_of(chips2)
    early = over_layers([(wo_chips, wo_near), (chips0, near0)])
    input_grad = to_input(
        hidden_in, middle_grad, w_qkv, (dq0, dk0, dv0, dq1, dk1, dv1, dq2, dk2, dv2)
    )
    near1, far2, early, input_grad = tie(near1, far2, early, input_grad)
    near2 = near_of(chips2, far2)
    owned1 = to_owner(after(shared1, near2))
    out_own = add_low(part[0][0], out_other)
    mixed = (middle + resid_scale * add_up([out_own, *out_near])).astype(bf16)
    early = layer_add(early)
    mine_out = early[:, : width + LANES]
    late = layer_add(over_layers([(chips1, near1), (chips2, near2)]))
    unit1, unit2 = chips1.shape[1], chips2.shape[1]
    mine = [early[:, width + LANES :], late[:, :unit1], late[:, unit1 : unit1 + unit2]]

    shared = jnp.stack([owned0, owned1], axis=1).reshape(E, per_expert, hidden).astype(f32)
    grad_gate, grad_up = shared[:, :own_rows], shared[:, own_rows : 2 * own_rows]
    grad_down = jnp.concatenate(
        [
            shared[:, 2 * own_rows + t * own_hidden : 2 * own_rows + (t + 1) * own_hidden]
            for t in range(thirds)
        ],
        axis=2,
    )
    def joined(kind):
        pieces = []
        for part_grads in mine:
            unit = part_grads.shape[1] // 5
            start, wide = ((0, 3 * unit), (3 * unit, unit), (4 * unit, unit))[kind]
            pieces.append(part_grads[:, start : start + wide])
        return jnp.concatenate(pieces, axis=1)

    grad_query, grad_key, grad_value = joined(0), joined(1), joined(2)
    grad_router = mine_out[:, width : width + E]

    def row_sums(weight, grad):
        return jnp.sum(weight.astype(f32) * grad, axis=-1)

    grad_norm_attn = (
        row_sums(w_query, grad_query) + row_sums(w_key, grad_key) + row_sums(w_value, grad_value)
    ) / norm_attn.astype(f32)
    grad_norm_moe = (
        jnp.sum(row_sums(w_gate, grad_gate) + row_sums(w_up, grad_up), axis=0)
        + row_sums(w_router, grad_router)
    ) / norm_moe.astype(f32)
    return (
        mixed,
        input_grad,
        grad_norm_attn,
        grad_query,
        grad_key,
        grad_value,
        mine_out[:, :width],
        grad_norm_moe,
        grad_router,
        grad_gate,
        grad_up,
        grad_down,
    )


def solution(mesh):

    in_specs = (
        P("fsdp", None),
        P("fsdp", None),
        P("fsdp", None),
        P("fsdp"),
        P("fsdp", None),
        P("fsdp", None),
        P("fsdp", None),
        P("fsdp", None),
        P("fsdp"),
        P("fsdp", None),
        P(None, "fsdp", None),
        P(None, "fsdp", None),
        P(None, "fsdp", None),
        P("fsdp", None),
    )
    out_specs = (
        P("fsdp", None),
        P("fsdp", None),
        P("fsdp"),
        P("fsdp", None),
        P("fsdp", None),
        P("fsdp", None),
        P("fsdp", None),
        P("fsdp"),
        P("fsdp", None),
        P(None, "fsdp", None),
        P(None, "fsdp", None),
        P(None, "fsdp", None),
    )
    return jax.shard_map(
        functools.partial(shards, mesh.shape["fsdp"]),
        mesh=mesh,
        in_specs=in_specs,
        out_specs=out_specs,
        check_vma=False,
    )
```

```python
import functools
import math

import jax
import jax.numpy as jnp
from jax import lax
from jax.experimental import pallas as pl
from jax.experimental.pallas import tpu as pltpu
from jax.sharding import PartitionSpec as P

HQ = 24
HK = 8
HD = 64
E = 16
GROUP = 8
PAIR_E = E // GROUP
HEADS_STEP = 2 * HQ // HK
LANES = 128
QW = HQ * HD
KW = HK * HD
QKV_WIDE = QW + 2 * KW + LANES
GAIN_ONE = E
GAIN_TWO = E + 1
VMEM_LIMIT = 58 * 1024 * 1024

norm_eps = 1e-06
resid_scale = 0.22
score_scale = 0.015625
rope_base = 10000.0
masked_score = -1e30

f32 = jnp.float32
bf16 = jnp.bfloat16


def matmul(left, right):
    return jnp.dot(left, right, preferred_element_type=f32)


def contract_rows(left, right):
    return lax.dot_general(left, right, (((0,), (0,)), ((), ())), preferred_element_type=f32)


def contract_last(left, right):
    return lax.dot_general(left, right, (((1,), (1,)), ((), ())), preferred_element_type=f32)


def layout(seq_lengths, row_count):
    seq_ends = jnp.cumsum(seq_lengths)
    starts = seq_ends - seq_lengths
    places = jnp.arange(row_count, dtype=jnp.int32)
    member = (places[:, None] >= starts[None, :]) & (places[:, None] < seq_ends[None, :])
    labels = jnp.arange(seq_lengths.shape[0], dtype=jnp.int32)
    segment = jnp.sum(jnp.where(member, labels[None, :], 0), axis=1)
    offset = jnp.sum(jnp.where(member, starts[None, :], 0), axis=1)
    return (segment, places - offset)


def turn_tables(position):
    half_dim = HD // 2
    inv_freq = jnp.exp(
        -(jnp.arange(half_dim, dtype=f32) * (2.0 / HD)) * math.log(rope_base)
    )
    angles = position.astype(f32)[:, None] * inv_freq[None, :]
    cosine, sine_val = jnp.cos(angles), jnp.sin(angles)
    return (
        jnp.concatenate([cosine] * 4, axis=1),
        jnp.concatenate([-sine_val, sine_val] * 2, axis=1),
    )


def swap(value, bit, device_count):
    return lax.ppermute(value, "fsdp", [(i, i ^ bit) for i in range(device_count)])


def shift(value, steps, device_count):
    moved = [(i, (i + GROUP * steps) % device_count) for i in range(device_count)]
    return lax.ppermute(value, "fsdp", moved)


def after(value, *needed):
    return lax.optimization_barrier((value, needed))[0]


def tie(*values):
    return lax.optimization_barrier(values)


def ring_start(own, layers, device_count):
    blocks = {0: own}
    ahead, behind = own, own
    for step in range(1, (layers - 1) // 2 + 1):
        ahead, behind = shift(ahead, 1, device_count), shift(behind, -1, device_count)
        blocks[step], blocks[layers - step] = ahead, behind
    return blocks


def ring_end(blocks, layers, device_count):
    if layers % 2 == 0:
        ahead, behind = blocks[layers // 2 - 1], blocks[(layers // 2 + 1) % layers]
        half = ahead.shape[1] // 2 // LANES * LANES
        blocks[layers // 2] = jnp.concatenate(
            [shift(ahead[:, :half], 1, device_count), shift(behind[:, half:], -1, device_count)], axis=1
        )
    return blocks


def joined_rows(blocks, places):
    return jnp.concatenate([blocks[j] for j in places], axis=0)


def gather_start(own, device_count):
    return swap(own, 2, device_count), swap(own, 4, device_count)


def gather_far(from2, from4, device_count):
    half = from2.shape[0] // 2
    return swap(from2[:half], 4, device_count), swap(from4[half:], 2, device_count)


def gather_cores(own, near, far, device_count):
    other = lambda value: swap(value, 1, device_count)
    return [
        [own], [other(own)], [near[0]], [other(near[0])], [near[1]], [other(near[1])],
        list(far), [other(far[0]), other(far[1])],
    ]


def layer_start(stacked, layer, layers, device_count):
    pick = lambda at: lax.dynamic_index_in_dim(stacked, at % layers, 0, keepdims=False)
    return [pick(layer)] + [shift(pick(layer + k), k, device_count) for k in range(1, layers)]


def layer_add(blocks):
    total = blocks[0].astype(f32)
    for block in blocks[1:]:
        total = total + block.astype(f32)
    return total


def turn(values, cosine, sine_val, low_half):
    shifted = jnp.where(low_half, pltpu.roll(values, LANES - 32, 1), pltpu.roll(values, 32, 1))
    return values * cosine + shifted * sine_val


def half_views(pair, scale):
    lane = lax.broadcasted_iota(jnp.int32, pair.shape, 1)
    scaled = pair.astype(f32) * scale
    low = lane < HD
    return jnp.where(low, scaled, 0.0).astype(bf16), jnp.where(low, 0.0, scaled).astype(bf16)


def head_tiles(tiles):
    return [
        tiles[head // 2] if head % 2 == head // 3 else pltpu.roll(tiles[head // 2], HD, 1)
        for head in range(HEADS_STEP)
    ]


def visible_keys(seg_col, seg_row, row_start, rows, keys):
    query_at = row_start + lax.broadcasted_iota(jnp.int32, (rows, keys), 0)
    key_at = lax.broadcasted_iota(jnp.int32, (rows, keys), 1)
    return (seg_col[row_start : row_start + rows, :] == seg_row[:, :keys]) & (key_at <= query_at)


def any_spec():
    return pl.BlockSpec(memory_space=pl.ANY)


def smem_spec():
    return pl.BlockSpec(memory_space=pltpu.SMEM)


def small_cost():
    return pl.CostEstimate(flops=1_000_000, bytes_accessed=100_000, transcendentals=0)


def params():
    return pltpu.CompilerParams(vmem_limit_bytes=VMEM_LIMIT)


def whole_spec(shape):
    zeros = (0,) * len(shape)
    return pl.BlockSpec(shape, lambda *_: zeros, pipeline_mode=pl.Buffered(1))


def gather_copies(plan, refs, table_ref, dst, sems):
    copies = []
    for ref, runs in zip(refs, plan):
        rows = ref.shape[0] // len(runs)
        for number, (member, step) in enumerate(runs):
            start = pl.multiple_of(table_ref[member, step], 16)
            copies.append(
                pltpu.make_async_copy(
                    ref.at[pl.ds(number * rows, rows)],
                    dst.at[pl.ds(start, rows)],
                    sems.at[len(copies)],
                )
            )
    return copies


def spread_copies(src, table_ref, refs, sems):
    copies = []
    members, blocks = table_ref.shape
    rows = src.shape[0] // (members * blocks)
    for member in range(members):
        for block in range(blocks):
            start = pl.multiple_of(table_ref[member, block], 16)
            to = (member // 2 * blocks + block) * rows
            copies.append(
                pltpu.make_async_copy(
                    src.at[pl.ds(start, rows)], refs[member % 2].at[pl.ds(to, rows)], sems.at[len(copies)]
                )
            )
    return copies


def stack_shapes(table, width, full):
    members = table.shape[0]
    stacks = min(members, 2)
    return [jax.ShapeDtypeStruct((width // stacks, full), bf16)] * stacks


def far_kernel(*refs):
    count = len(refs) // 4
    for q in range(count):
        left, right = refs[2 * q : 2 * q + 2]
        low, high = refs[2 * count + 2 * q : 2 * count + 2 * q + 2]
        total = (left[...].astype(f32) + right[...].astype(f32)).astype(bf16)
        low[...] = total[0]
        high[...] = total[1]


def sums_for_far(pairs):
    rows = pairs[0][0].shape[0]
    tile = rows // 8
    args, in_specs, out_specs, shapes = [], [], [], []
    for pair in pairs:
        width = pair[0].shape[1]
        args += [value.reshape(2, rows // 2, width) for value in pair]
        in_specs += [pl.BlockSpec((2, tile, width), lambda i: (0, i, 0))] * 2
        out_specs += [pl.BlockSpec((tile, width), lambda i: (i, 0))] * 2
        shapes += [jax.ShapeDtypeStruct((rows // 2, width), bf16)] * 2
    out = pl.pallas_call(
        far_kernel, grid=(4,), in_specs=in_specs, out_specs=out_specs, out_shape=shapes,
        compiler_params=params(), cost_estimate=small_cost(),
    )(*args)
    return [out[2 * q : 2 * q + 2] for q in range(len(pairs))]


def near_kernel(a2_ref, b2_ref, a4_ref, b4_ref, low_ref, high_ref, sum2_ref, sum4_ref):
    two = a2_ref[...].astype(f32) + b2_ref[...].astype(f32)
    four = a4_ref[...].astype(f32) + b4_ref[...].astype(f32)
    sum2_ref[0] = (two[0] + low_ref[...].astype(f32)).astype(bf16)
    sum2_ref[1] = two[1].astype(bf16)
    sum4_ref[0] = four[0].astype(bf16)
    sum4_ref[1] = (four[1] + high_ref[...].astype(f32)).astype(bf16)


def sums_for_near(a2, b2, a4, b4, low, high):
    rows, width = a2.shape
    tile = rows // 8
    pair = pl.BlockSpec((2, tile, width), lambda i: (0, i, 0))
    single = pl.BlockSpec((tile, width), lambda i: (i, 0))
    out = pl.pallas_call(
        near_kernel, grid=(4,), in_specs=[pair] * 4 + [single] * 2, out_specs=[pair] * 2,
        out_shape=[jax.ShapeDtypeStruct((2, rows // 2, width), bf16)] * 2,
        compiler_params=params(), cost_estimate=small_cost(),
    )(*[value.reshape(2, rows // 2, width) for value in (a2, b2, a4, b4)], low, high)
    return [value.reshape(rows, width) for value in out]


def half_kernel(more_for, a2_ref, b2_ref, a4_ref, b4_ref, more_ref, sum2_ref, sum4_ref):
    two = a2_ref[...].astype(f32) + b2_ref[...].astype(f32)
    four = a4_ref[...].astype(f32) + b4_ref[...].astype(f32)
    more = more_ref[...].astype(f32)
    sum2_ref[...] = (two + more if more_for == 2 else two).astype(bf16)
    sum4_ref[...] = (four + more if more_for == 4 else four).astype(bf16)


def half_for_near(which, a2, b2, a4, b4, more):
    rows, width = a2.shape
    tile = rows // 8
    picked = pl.BlockSpec((tile, width), lambda i: (4 * which + i, 0))
    single = pl.BlockSpec((tile, width), lambda i: (i, 0))
    return pl.pallas_call(
        functools.partial(half_kernel, (2, 4)[which]), grid=(4,), in_specs=[picked] * 4 + [single],
        out_specs=[single] * 2, out_shape=[jax.ShapeDtypeStruct((rows // 2, width), bf16)] * 2,
        compiler_params=params(), cost_estimate=small_cost(),
    )(a2, b2, a4, b4, more)


def stack_kernel(even_ref, odd_ref, own_ref, two_ref, four_ref, low_ref, high_ref):
    rows = own_ref.shape[0]
    half = rows // 2
    spots = ((own_ref, 0, rows), (two_ref, rows, rows), (four_ref, 2 * rows, rows), (low_ref, 3 * rows, half),
             (high_ref, 3 * rows + half, half))
    for ref, start, count in spots:
        at = slice(start, start + count)
        ref[...] = (even_ref[at].astype(f32) + odd_ref[at].astype(f32)).astype(bf16)


def sums_of_stack(even, odd):
    rows, width = even.shape[0] // 4, even.shape[1]
    vmem = pl.BlockSpec(memory_space=pltpu.VMEM)
    return pl.pallas_call(
        stack_kernel, in_specs=[vmem] * 2, out_specs=[vmem] * 5,
        out_shape=[jax.ShapeDtypeStruct((r, width), bf16) for r in (rows, rows, rows, rows // 2, rows // 2)],
        compiler_params=params(), cost_estimate=small_cost(),
    )(even, odd)


def stack_near_kernel(*refs):
    *sources, sum2_ref, sum4_ref = refs
    start = 0
    for q in range(0, len(sources), 4):
        two_ref, four_ref, low_ref, high_ref = sources[q : q + 4]
        half = low_ref.shape[0]
        at = slice(start, start + two_ref.shape[1])
        sum2_ref[:half, at] = (two_ref[:half].astype(f32) + low_ref[...].astype(f32)).astype(bf16)
        sum2_ref[half:, at] = two_ref[half:]
        sum4_ref[:half, at] = four_ref[:half]
        sum4_ref[half:, at] = (four_ref[half:].astype(f32) + high_ref[...].astype(f32)).astype(bf16)
        start += two_ref.shape[1]


def stack_near(sets):
    vmem = pl.BlockSpec(memory_space=pltpu.VMEM)
    shape = (sets[0][0].shape[0], sum(one[0].shape[1] for one in sets))
    return pl.pallas_call(
        stack_near_kernel, in_specs=[vmem] * (4 * len(sets)), out_specs=[vmem] * 2,
        out_shape=[jax.ShapeDtypeStruct(shape, bf16)] * 2,
        compiler_params=params(), cost_estimate=small_cost(),
    )(*[value for one in sets for value in one])


def attend_kernel(block, plan, table_ref, x_ref, cos_ref, sin_ref, segc_ref, segr_ref, *refs):
    pair = pl.program_id(0)
    rows_all, width = x_ref.shape
    at = lambda start, wide: pl.ds(pl.multiple_of(start, LANES), wide)
    if plan is None:
        wq_ref, wk_ref, wv_ref, q_ref, k_ref, v_ref, out_ref, lse_ref = refs
        normed_ref = x_ref
        w_q, w_k, w_v = wq_ref[...], wk_ref[...], wv_ref[...]
    else:
        sources = refs[: len(plan)]
        (w_out_ref, normed_ref, turned_ref, q_ref, k_ref, v_ref, out_ref, lse_ref,
         w_ref, sems, save_sem) = refs[len(plan) :]

        @pl.when(pair == 0)
        def _():
            copies = gather_copies(plan, sources, table_ref, w_ref, sems)
            for c in copies:
                c.start()
            x = x_ref[...].astype(f32)
            rinv = lax.rsqrt(jnp.mean(x * x, axis=-1, keepdims=True) + norm_eps)
            for c in copies:
                c.wait()
            pltpu.make_async_copy(w_ref, w_out_ref, save_sem).start()
            gains = w_ref[:, QW + 2 * KW :].astype(f32).T
            scaled = x * rinv * gains[GAIN_ONE : GAIN_ONE + 1, :]
            normed_ref[...] = scaled.astype(bf16)
            turned_ref[...] = scaled.T.astype(bf16)

        w_q = w_ref[:, at(pair * 3 * LANES, 3 * LANES)]
        w_k = w_ref[:, at(QW + pair * LANES, LANES)]
        w_v = w_ref[:, at(QW + KW + pair * LANES, LANES)]

    normed = normed_ref[...]
    lane = lax.broadcasted_iota(jnp.int32, (rows_all, LANES), 1)
    first = (lane % HD) < (HD // 2)
    cosine, sine_val = cos_ref[...], sin_ref[...]
    q_pre = matmul(normed, w_q)
    tiles = []
    for t in range(3):
        cols = slice(t * LANES, (t + 1) * LANES)
        tiles.append(turn(q_pre[:, cols], cosine, sine_val, first))
        q_ref[:, cols] = tiles[t].astype(bf16)
    heads = [tile.astype(bf16) for tile in head_tiles(tiles)]
    k_low = turn(matmul(normed, w_k), cosine, sine_val, first).astype(bf16)
    v_low = matmul(normed, w_v).astype(bf16)
    k_ref[...] = k_low
    v_ref[...] = v_low
    k_views = half_views(k_low, score_scale)
    v_views = half_views(v_low, 1.0)
    seg_col, seg_row = segc_ref[...], segr_ref[...]
    lane_b = lax.broadcasted_iota(jnp.int32, (block, LANES), 1)
    for start in range(0, rows_all, block):
        keys = start + block
        rows = slice(start, keys)
        visible = visible_keys(seg_col, seg_row, start, block, keys)
        norms = jnp.zeros((block, LANES), f32)
        outs = []
        for kv in range(2):
            q_rows = jnp.concatenate([heads[3 * kv + j][rows] for j in range(3)], axis=0)
            scores = contract_last(q_rows, k_views[kv][:keys]).reshape(3, block, keys)
            scores = jnp.where(visible[None], scores, masked_score)
            peak = jnp.max(scores, axis=-1, keepdims=True)
            expo = jnp.exp(scores - peak)
            mass = jnp.sum(expo, axis=-1, keepdims=True)
            probs = (expo * (1.0 / mass)).astype(bf16)
            total = matmul(probs.reshape(3 * block, keys), v_views[kv][:keys])
            norm = peak + jnp.log(mass)
            for j in range(3):
                outs.append(total[j * block : (j + 1) * block])
                norms = jnp.where(lane_b == 3 * kv + j, norm[j], norms)
        for t in range(3):
            low, high = outs[2 * t], outs[2 * t + 1]
            low = pltpu.roll(low, HD, 1) if t == 2 else low
            high = pltpu.roll(high, HD, 1) if t == 0 else high
            out_ref[rows, t * LANES : (t + 1) * LANES] = (low + high).astype(bf16)
        lse_ref[0, rows, :] = norms

    if plan is not None:
        @pl.when(pair == pl.num_programs(0) - 1)
        def _():
            pltpu.make_async_copy(w_ref, w_out_ref, save_sem).wait()


def attend_forward(base, steps, table, plan, weights, rows_in, cosine, sine_val, segment):
    rows, width = rows_in.shape
    wide = pl.BlockSpec((rows, 3 * LANES), lambda i: (0, i))
    thin = pl.BlockSpec((rows, LANES), lambda i: (0, i))
    in_specs = [
        smem_spec(),
        whole_spec((rows, width)),
        whole_spec((rows, LANES)),
        whole_spec((rows, LANES)),
        whole_spec((rows, 1)),
        whole_spec((1, rows)),
    ]
    out_specs = [wide, thin, thin, wide, pl.BlockSpec((1, rows, LANES), lambda i: (i, 0, 0))]
    out_shape = [
        jax.ShapeDtypeStruct((rows, 3 * LANES * steps), bf16),
        jax.ShapeDtypeStruct((rows, LANES * steps), bf16),
        jax.ShapeDtypeStruct((rows, LANES * steps), bf16),
        jax.ShapeDtypeStruct((rows, 3 * LANES * steps), bf16),
        jax.ShapeDtypeStruct((steps, rows, LANES), f32),
    ]
    if plan is None:
        in_specs += [
            pl.BlockSpec((width, 3 * LANES), lambda i: (0, base + i)),
            pl.BlockSpec((width, LANES), lambda i: (0, QW // LANES + base + i)),
            pl.BlockSpec((width, LANES), lambda i: (0, (QW + KW) // LANES + base + i)),
        ]
        weights = [weights] * 3
        scratch = []
    else:
        in_specs += [any_spec()] * len(weights)
        out_specs = [any_spec(), whole_spec((rows, width)), whole_spec((width, rows))] + out_specs
        out_shape = [
            jax.ShapeDtypeStruct((width, QKV_WIDE), bf16),
            jax.ShapeDtypeStruct((rows, width), bf16),
            jax.ShapeDtypeStruct((width, rows), bf16),
        ] + out_shape
        scratch = [
            pltpu.VMEM((width, QKV_WIDE), bf16),
            pltpu.SemaphoreType.DMA((sum(len(r) for r in plan),)),
            pltpu.SemaphoreType.DMA(()),
        ]
    return pl.pallas_call(
        functools.partial(attend_kernel, 128, plan),
        grid=(steps,),
        in_specs=in_specs,
        out_specs=out_specs,
        out_shape=out_shape,
        scratch_shapes=scratch,
        compiler_params=params(),
        cost_estimate=small_cost(),
    )(table, rows_in, cosine, sine_val, segment[:, None], segment[None, :], *weights)


def middle_kernel(plan, table_ref, x_ref, attn0_ref, attn1_ref, extras_ref, routes_ref, *refs):
    sources = refs[: len(plan)]
    w_out_ref, middle_ref, inner_ref, mix_ref, w_ref, sems, save_sem = refs[len(plan) :]
    copies = gather_copies(plan, sources, table_ref, w_ref, sems)
    for c in copies:
        c.start()
    extras = extras_ref[...]
    gains = extras.astype(f32).T
    rows, width = x_ref.shape
    for c in copies:
        c.wait()
    save = pltpu.make_async_copy(w_ref, w_out_ref, save_sem)
    save.start()
    half = attn0_ref.shape[1]
    product = matmul(attn0_ref[...], w_ref[:half]) + matmul(attn1_ref[...], w_ref[half:])
    middle = x_ref[...].astype(f32) + resid_scale * product
    middle_ref[...] = middle
    rinv = lax.rsqrt(jnp.mean(middle * middle, axis=-1, keepdims=True) + norm_eps)
    inner = (middle * rinv * gains[GAIN_TWO : GAIN_TWO + 1, :]).astype(bf16)
    inner_ref[:, :width] = inner
    logits = matmul(inner, extras)
    lane = lax.broadcasted_iota(jnp.int32, logits.shape, 1)
    routes = routes_ref[...]
    named = lane == routes[:, 0:1]
    for k in range(1, routes.shape[1]):
        named = named | (lane == routes[:, k : k + 1])
    chosen = jnp.where(named, logits, masked_score)
    peak = jnp.max(chosen, axis=-1, keepdims=True)
    expo = jnp.where(named, jnp.exp(chosen - peak), 0.0)
    mix = expo / jnp.sum(expo, axis=-1, keepdims=True)
    mix_ref[...] = mix
    high = mix.astype(bf16).astype(f32)
    rest = (mix - high).astype(bf16).astype(f32)
    low = mix - high - rest
    spread = high + pltpu.roll(rest, E, 1) + pltpu.roll(low, 2 * E, 1)
    inner_ref[:, width:] = spread.astype(bf16)
    save.wait()


def to_middle(table, plan, pieces, hidden_in, attn_out, extras, routes):
    rows, width = hidden_in.shape
    vmem = pl.BlockSpec(memory_space=pltpu.VMEM)
    return pl.pallas_call(
        functools.partial(middle_kernel, plan),
        in_specs=[smem_spec()] + [vmem] * 5 + [any_spec()] * len(pieces),
        out_specs=[any_spec(), vmem, vmem, vmem],
        out_shape=[
            jax.ShapeDtypeStruct((QW, width), bf16),
            jax.ShapeDtypeStruct((rows, width), f32),
            jax.ShapeDtypeStruct((rows, width + LANES), bf16),
            jax.ShapeDtypeStruct((rows, LANES), f32),
        ],
        scratch_shapes=[
            pltpu.VMEM((QW, width), bf16),
            pltpu.SemaphoreType.DMA((sum(len(r) for r in plan),)),
            pltpu.SemaphoreType.DMA(()),
        ],
        compiler_params=params(),
        cost_estimate=small_cost(),
    )(table, hidden_in, *attn_out, extras, routes, *pieces)


def middle_back_kernel(blocks, table_ref, own0_ref, own1_ref, near2_ref, near4_ref, inner_ref, mix_ref, middle_ref,
                       cot_ref, extras_ref, attn0_ref, attn1_ref, w_ref, *refs):
    dests = refs[:blocks]
    grad_ref, attn_grad0_ref, attn_grad1_ref, wgrad_ref, sems = refs[blocks:]
    rows, width = middle_ref.shape
    total = own0_ref[...].astype(f32) + own1_ref[...].astype(f32)
    total = total + near2_ref[...].astype(f32) + near4_ref[...].astype(f32)
    inner_grad, tail = total[:, :width], total[:, width:]
    lane = lax.broadcasted_iota(jnp.int32, tail.shape, 1)
    mix = mix_ref[...]
    mix_grad = tail + pltpu.roll(tail, LANES - E, 1) + pltpu.roll(tail, LANES - 2 * E, 1)
    mix_grad = jnp.where(lane < E, mix_grad, 0.0)
    logit_grad = mix_grad - mix * jnp.sum(mix_grad, axis=-1, keepdims=True)
    logit_grad = logit_grad.astype(bf16)
    extras = extras_ref[...]
    gain = extras.astype(f32).T[GAIN_TWO : GAIN_TWO + 1, :]
    inner_grad = inner_grad + contract_last(logit_grad, extras)
    middle = middle_ref[...]
    rinv = lax.rsqrt(jnp.mean(middle * middle, axis=-1, keepdims=True) + norm_eps)
    scaled = gain * inner_grad
    back = rinv * scaled - middle * (rinv * rinv * rinv * jnp.mean(scaled * middle, axis=-1, keepdims=True))
    middle_grad = cot_ref[...].astype(f32) + back
    grad_ref[...] = middle_grad
    proj_grad = (resid_scale * middle_grad).astype(bf16)
    half = attn0_ref.shape[1]
    attn_grad0_ref[...] = contract_last(proj_grad, w_ref[:half]).astype(bf16)
    attn_grad1_ref[...] = contract_last(proj_grad, w_ref[half:]).astype(bf16)
    wgrad_ref[:half, :width] = contract_rows(attn0_ref[...], proj_grad).astype(bf16)
    wgrad_ref[half:, :width] = contract_rows(attn1_ref[...], proj_grad).astype(bf16)
    wgrad_ref[:, width:] = contract_rows(inner_ref[:, :width], logit_grad).astype(bf16)
    copies = spread_copies(wgrad_ref, table_ref, dests, sems)
    for c in copies:
        c.start()
    for c in copies:
        c.wait()


def middle_back(table, sums, inner, mix, middle, cotangent, extras, attn_out, w_out):
    rows, width = middle.shape
    members, layers = table.shape
    vmem = pl.BlockSpec(memory_space=pltpu.VMEM)
    full = width + LANES
    return pl.pallas_call(
        functools.partial(middle_back_kernel, min(members, 2)),
        in_specs=[smem_spec()] + [vmem] * 12,
        out_specs=[any_spec()] * min(members, 2) + [vmem] * 3,
        out_shape=stack_shapes(table, width, full)
        + [jax.ShapeDtypeStruct((rows, width), f32)]
        + [jax.ShapeDtypeStruct((rows, QW // 2), bf16)] * 2,
        scratch_shapes=[
            pltpu.VMEM((width, full), bf16),
            pltpu.SemaphoreType.DMA((members * layers,)),
        ],
        compiler_params=params(),
        cost_estimate=small_cost(),
    )(table, *sums, inner, mix, middle, cotangent, extras, *attn_out, w_out)


def attend_back_kernel(block, blocks, table_ref, turned_ref, q_ref, k_ref, v_ref, grad_ref, lse_ref,
                       cos_ref, sin_ref, segc_ref, segr_ref, *refs):
    dests = refs[:blocks]
    dq_ref, dk_ref, dv_ref, dkt_ref, dvt_ref, wgrad_ref, sems = refs[blocks:]
    step = pl.program_id(0)
    width, rows_all = turned_ref.shape
    lane = lax.broadcasted_iota(jnp.int32, (rows_all, LANES), 1)
    first = (lane % HD) < (HD // 2)
    k_views = half_views(k_ref[...], score_scale)
    v_views = half_views(v_ref[...], 1.0)
    tile_cols = [slice(t * LANES, (t + 1) * LANES) for t in range(3)]
    q_tiles = [q_ref[:, cols].astype(f32) for cols in tile_cols]
    g_tiles = [grad_ref[:, cols].astype(f32) for cols in tile_cols]
    q_heads = [tile.astype(bf16) for tile in head_tiles(q_tiles)]
    g_heads = [tile.astype(bf16) for tile in head_tiles(g_tiles)]

    def turned_heads(tiles):
        out = []
        for head in range(HEADS_STEP):
            tile = tiles[head // 2].T
            if head % 2 != head // 3:
                tile = jnp.concatenate([tile[HD:], tile[:HD]], axis=0)
            out.append(tile.astype(bf16))
        return out

    q_turned, g_turned = turned_heads(q_tiles), turned_heads(g_tiles)
    dkt_ref[...] = jnp.zeros_like(dkt_ref)
    dvt_ref[...] = jnp.zeros_like(dvt_ref)
    seg_col, seg_row = segc_ref[...], segr_ref[...]
    cosine, sine_val = cos_ref[...], -sin_ref[...]
    for start in range(0, rows_all, block):
        keys = start + block
        rows = slice(start, keys)
        visible = visible_keys(seg_col, seg_row, start, block, keys)
        norms = lse_ref[0, rows, :]
        parts = []
        for kv in range(2):
            three = [3 * kv + j for j in range(3)]
            q_rows = jnp.concatenate([q_heads[h][rows] for h in three], axis=0)
            g_rows = jnp.concatenate([g_heads[h][rows] for h in three], axis=0)
            norm = jnp.concatenate([norms[:, h : h + 1] for h in three], axis=0).reshape(3, block, 1)
            scores = contract_last(q_rows, k_views[kv][:keys]).reshape(3, block, keys)
            probs = jnp.where(visible[None], jnp.exp(scores - norm), 0.0)
            prob_grad = contract_last(g_rows, v_views[kv][:keys]).reshape(3, block, keys)
            centre = jnp.sum(probs * prob_grad, axis=-1, keepdims=True)
            score_grad = (probs * (prob_grad - centre)).astype(bf16).reshape(3 * block, keys)
            probs = probs.astype(bf16).reshape(3 * block, keys)
            dq = matmul(score_grad, k_views[kv][:keys])
            parts += [dq[j * block : (j + 1) * block] for j in range(3)]
            q_across = jnp.concatenate([q_turned[h][:, rows] for h in three], axis=1)
            g_across = jnp.concatenate([g_turned[h][:, rows] for h in three], axis=1)
            dkt_ref[kv, :, :keys] += matmul(q_across, score_grad)
            dvt_ref[kv, :, :keys] += matmul(g_across, probs)
        for t in range(3):
            low, high = parts[2 * t], parts[2 * t + 1]
            low = pltpu.roll(low, HD, 1) if t == 2 else low
            high = pltpu.roll(high, HD, 1) if t == 0 else high
            turned_back = turn(low + high, cosine[rows], sine_val[rows], first[rows])
            dq_ref[rows, tile_cols[t]] = turned_back.astype(bf16)

    def joined(ref):
        return jnp.where(lane < HD, ref[0].T, ref[1].T)

    dk_ref[...] = turn(joined(dkt_ref) * score_scale, cosine, sine_val, first).astype(bf16)
    dv_ref[...] = joined(dvt_ref).astype(bf16)
    at = lambda start, wide: pl.ds(pl.multiple_of(start, LANES), wide)
    normed_turned = turned_ref[...]
    count = wgrad_ref.shape[1] // (5 * LANES)
    wgrad_ref[:, at(step * 3 * LANES, 3 * LANES)] = matmul(normed_turned, dq_ref[...]).astype(bf16)
    wgrad_ref[:, at((3 * count + step) * LANES, LANES)] = matmul(normed_turned, dk_ref[...]).astype(bf16)
    wgrad_ref[:, at((4 * count + step) * LANES, LANES)] = matmul(normed_turned, dv_ref[...]).astype(bf16)

    @pl.when(step == pl.num_programs(0) - 1)
    def _():
        copies = spread_copies(wgrad_ref, table_ref, dests, sems)
        for c in copies:
            c.start()
        for c in copies:
            c.wait()


def attend_backward(base, steps, table, turned, queries, keys, values, grads, norms, cosine, sine_val,
                    segment):
    width, rows = turned.shape
    members, layers = table.shape
    full = 5 * steps * LANES
    wide = pl.BlockSpec((rows, 3 * LANES), lambda i: (0, base + i))
    thin = pl.BlockSpec((rows, LANES), lambda i: (0, base + i))
    out_wide = pl.BlockSpec((rows, 3 * LANES), lambda i: (0, i))
    out_thin = pl.BlockSpec((rows, LANES), lambda i: (0, i))
    return pl.pallas_call(
        functools.partial(attend_back_kernel, 128, min(members, 2)),
        grid=(steps,),
        in_specs=[
            smem_spec(),
            whole_spec((width, rows)),
            wide,
            thin,
            thin,
            wide,
            pl.BlockSpec((1, rows, LANES), lambda i: (base + i, 0, 0)),
            whole_spec((rows, LANES)),
            whole_spec((rows, LANES)),
            whole_spec((rows, 1)),
            whole_spec((1, rows)),
        ],
        out_specs=[any_spec()] * min(members, 2) + [out_wide, out_thin, out_thin],
        out_shape=stack_shapes(table, width, full)
        + [jax.ShapeDtypeStruct((rows, k * LANES * steps), bf16) for k in (3, 1, 1)],
        scratch_shapes=[
            pltpu.VMEM((2, LANES, rows), f32),
            pltpu.VMEM((2, LANES, rows), f32),
            pltpu.VMEM((width, full), bf16),
            pltpu.SemaphoreType.DMA((members * layers,)),
        ],
        compiler_params=params(),
        cost_estimate=small_cost(),
    )(table, turned, queries, keys, values, grads, norms, cosine, sine_val, segment[:, None],
      segment[None, :])


def input_kernel(x_ref, mgrad_ref, w_ref, *refs):
    *grads, out_ref = refs
    x = x_ref[...].astype(f32)
    rinv = lax.rsqrt(jnp.mean(x * x, axis=-1, keepdims=True) + norm_eps)
    gain = w_ref[:, QW + 2 * KW :].astype(f32).T[GAIN_ONE : GAIN_ONE + 1, :]
    start = [0, QW, QW + KW]
    total = None
    for number, ref in enumerate(grads):
        wide = ref.shape[1]
        kind = number % 3
        product = contract_last(ref[...], w_ref[:, start[kind] : start[kind] + wide])
        start[kind] += wide
        total = product if total is None else total + product
    scaled = gain * total
    back = rinv * scaled - x * (rinv * rinv * rinv * jnp.mean(scaled * x, axis=-1, keepdims=True))
    out_ref[...] = mgrad_ref[...] + back


def to_input(hidden_in, middle_grad, w_qkv, grads):
    vmem = pl.BlockSpec(memory_space=pltpu.VMEM)
    return pl.pallas_call(
        input_kernel,
        in_specs=[vmem] * (3 + len(grads)),
        out_specs=vmem,
        out_shape=jax.ShapeDtypeStruct(hidden_in.shape, f32),
        compiler_params=params(),
        cost_estimate=small_cost(),
    )(hidden_in, middle_grad, w_qkv, *grads)


def experts_kernel(x_counts, c_counts, expert, packed, has_prev, has_sums, last, *refs):
    refs = list(refs)
    take = lambda count: [refs.pop(0) for _ in range(count)]
    (place_ref,) = take(1)
    x_src = [take(c) for c in x_counts]
    c_src = [take(c) for c in c_counts]
    weights = take(1 if packed else 3)
    prev_src = [take(2) for _ in x_counts] if has_prev else None
    sums_src = take(3) if has_sums else None
    dest = [take(2) for _ in x_counts]
    sums_dst = take(1 if packed and last else 3)
    xs, cs, og_out, og_grad = take(4)
    prevs = take(2) if has_prev else None
    acc = take(3)
    held = take(3) if packed else weights
    sem_in, sem_out, sem_sum, sem_w = take(4)
    i = pl.program_id(0)
    count = len(x_counts)
    width = cs.shape[2]
    hidden = acc[0].shape[1]

    def weight_loads():
        own, low = held[0].shape[2], held[2].shape[2]
        src = weights[0]
        pairs = [(src.at[:, :, pl.ds(0, own)], held[0]), (src.at[:, :, pl.ds(own, own)], held[1])]
        for third in range(width // hidden):
            pairs.append(
                (
                    src.at[:, :, pl.ds(2 * own + third * low, low)],
                    held[2].at[:, :, :, pl.ds(third * hidden, hidden)],
                )
            )
        return [pltpu.make_async_copy(a, b, sem_w.at[q]) for q, (a, b) in enumerate(pairs)]

    def loads(t):
        out = []
        slot = t % 2
        number = 0
        for srcs, dst in ((x_src[t], xs), (c_src[t], cs)):
            row = 0
            for r in srcs:
                rows = r.shape[0]
                out.append(pltpu.make_async_copy(r, dst.at[slot, pl.ds(row, rows)], sem_in.at[slot, number]))
                row += rows
                number += 1
        if has_prev:
            for r, dst in zip(prev_src[t], prevs):
                out.append(pltpu.make_async_copy(r, dst.at[slot], sem_in.at[slot, number]))
                number += 1
        return out

    def stores(t):
        slot = t % 2
        return [
            pltpu.make_async_copy(og_out.at[slot], dest[t][0], sem_out.at[slot, 0]),
            pltpu.make_async_copy(og_grad.at[slot], dest[t][1], sem_out.at[slot, 1]),
        ]

    def sum_loads():
        return [pltpu.make_async_copy(s, a, sem_sum.at[q]) for q, (s, a) in enumerate(zip(sums_src, acc))]

    @pl.when(i == 0)
    def _():
        for c in loads(0):
            c.start()
        if packed:
            for c in weight_loads():
                c.start()
        if has_sums:
            for c in sum_loads():
                c.start()
        else:
            for a in acc:
                a[...] = jnp.zeros_like(a)
        if packed:
            for c in weight_loads():
                c.wait()

    for t in range(count):
        @pl.when(i == t)
        def _(t=t):
            for c in loads(t):
                c.wait()
            if t + 1 < count:
                for c in loads(t + 1):
                    c.start()
            if t >= 2:
                for c in stores(t - 2):
                    c.wait()

    slot = lax.rem(i, 2)
    rows_in = xs[slot, :, :width]
    extra = xs[slot, :, width:].astype(f32)
    lane = lax.broadcasted_iota(jnp.int32, extra.shape, 1)
    mine = place_ref[0] * PAIR_E + expert
    gate_row = jnp.sum(jnp.where((lane < 3 * E) & (lax.rem(lane, E) == mine), extra, 0.0), axis=-1, keepdims=True)
    cot_wide = cs[slot].astype(f32)
    w_gate = held[0][...].reshape(width, hidden)
    w_up = held[1][...].reshape(width, hidden)
    w_down = held[2][...].reshape(hidden, width)
    gate_proj = matmul(rows_in, w_gate)
    up_proj = matmul(rows_in, w_up)
    sigmoid_g = 1.0 / (1.0 + jnp.exp(-gate_proj))
    active = gate_proj * sigmoid_g
    mid = (active * up_proj).astype(bf16)
    out_grad = ((resid_scale * gate_row) * cot_wide).astype(bf16)
    mid_grad = contract_last(out_grad, w_down)
    gate_grad = (mid_grad * up_proj * sigmoid_g * (1.0 + gate_proj * (1.0 - sigmoid_g))).astype(bf16)
    up_grad = (mid_grad * active).astype(bf16)
    out_rows = matmul(mid, w_down)
    mix = jnp.sum(mid.astype(f32) * mid_grad, axis=-1, keepdims=True)
    mixed = gate_row * out_rows
    if has_prev:
        mixed = mixed + prevs[0][slot].astype(f32)
    og_out[slot] = mixed.astype(bf16)
    back = contract_last(gate_grad, w_gate) + contract_last(up_grad, w_up)
    if has_prev:
        back = back + prevs[1][slot, :, :width].astype(f32)
    og_grad[slot, :, :width] = back.astype(bf16)
    high = mix.astype(bf16).astype(f32)
    middle = (mix - high).astype(bf16).astype(f32)
    low = mix - high - middle
    spread = jnp.where(lane == mine, high, jnp.where(lane == mine + E, middle, jnp.where(lane == mine + 2 * E, low, 0.0)))
    if has_prev:
        spread = spread + prevs[1][slot, :, width:].astype(f32)
    og_grad[slot, :, width:] = spread.astype(bf16)
    for t in range(count):
        @pl.when(i == t)
        def _(t=t):
            for c in stores(t):
                c.start()
    if has_sums:
        @pl.when(i == 0)
        def _():
            for c in sum_loads():
                c.wait()
    acc[0][...] += contract_rows(rows_in, gate_grad)
    acc[1][...] += contract_rows(rows_in, up_grad)
    acc[2][...] += contract_rows(mid, out_grad)

    @pl.when(i == count - 1)
    def _():
        if last and packed:
            out = sums_dst[0]
            layers, members, own, _ = held[0].shape
            low = held[2].shape[2]
            out[:, :, :own] = acc[0][...].astype(bf16).reshape(layers, members, own, hidden)
            out[:, :, own : 2 * own] = acc[1][...].astype(bf16).reshape(layers, members, own, hidden)
            for third in range(width // hidden):
                piece = acc[2][:, third * hidden : (third + 1) * hidden].astype(bf16)
                start = 2 * own + third * low
                out[:, :, start : start + low] = piece.reshape(layers, members, low, hidden)
        elif last:
            for a, d in zip(acc, sums_dst):
                d[...] = a[...].astype(bf16)
        else:
            copies = [pltpu.make_async_copy(a, d, sem_sum.at[q]) for q, (a, d) in enumerate(zip(acc, sums_dst))]
            for c in copies:
                c.start()
            for c in copies:
                c.wait()
        for t in range(max(0, count - 2), count):
            for c in stores(t):
                c.wait()


def experts_call(place, expert, xs, cs, weights, own, prev, sums, last):
    tiles = [x if isinstance(x, (list, tuple)) else [x] for x in xs]
    cots = [c if isinstance(c, (list, tuple)) else [c] for c in cs]
    rows = sum(a.shape[0] for a in tiles[0])
    full = tiles[0][0].shape[1]
    packed = len(weights) == 1
    width, hidden = cots[0][0].shape[1], weights[0].shape[-1] if packed else weights[0].shape[1]
    anyspace = pl.BlockSpec(memory_space=pl.ANY)
    resident = lambda a: pl.BlockSpec(a.shape, lambda i: (0, 0), pipeline_mode=pl.Buffered(1))
    args, specs = [jnp.asarray(place, jnp.int32).reshape(1)], [pl.BlockSpec(memory_space=pltpu.SMEM)]
    for group in tiles + cots:
        args += group
        specs += [anyspace] * len(group)
    args += list(weights)
    specs += [anyspace] if packed else [resident(w) for w in weights]
    if prev is not None:
        for pair in prev:
            args += list(pair)
            specs += [anyspace] * 2
    if sums is not None:
        args += list(sums)
        specs += [anyspace] * 3
    shapes, out_specs = [], []
    for _ in tiles:
        shapes += [jax.ShapeDtypeStruct((rows, width), bf16), jax.ShapeDtypeStruct((rows, full), bf16)]
        out_specs += [anyspace] * 2
    sum_shapes = ((width, hidden), (width, hidden), (hidden, width))
    if packed and last:
        shapes.append(jax.ShapeDtypeStruct(weights[0].shape, bf16))
        out_specs.append(whole_spec(weights[0].shape))
        sum_shapes = ()
    for shape in sum_shapes:
        shapes.append(jax.ShapeDtypeStruct(shape, bf16 if last else f32))
        out_specs.append(pl.BlockSpec(shape, lambda i: (0, 0), pipeline_mode=pl.Buffered(1)) if last else anyspace)
    scratch = [
        pltpu.VMEM((2, rows, full), bf16), pltpu.VMEM((2, rows, width), bf16),
        pltpu.VMEM((2, rows, width), bf16), pltpu.VMEM((2, rows, full), bf16),
    ]
    if prev is not None:
        scratch += [pltpu.VMEM((2, rows, width), bf16), pltpu.VMEM((2, rows, full), bf16)]
    scratch += [pltpu.VMEM((width, hidden), f32), pltpu.VMEM((width, hidden), f32), pltpu.VMEM((hidden, width), f32)]
    if packed:
        layers = weights[0].shape[0]
        low = hidden // (layers * GROUP)
        scratch += [
            pltpu.VMEM((layers, GROUP, own, hidden), bf16),
            pltpu.VMEM((layers, GROUP, own, hidden), bf16),
            pltpu.VMEM((layers, GROUP, low, width), bf16),
        ]
    scratch += [pltpu.SemaphoreType.DMA(shape) for shape in ((2, 6), (2, 2), (3,), (2 + width // hidden,))]
    out = pl.pallas_call(
        functools.partial(experts_kernel, [len(t) for t in tiles], [len(c) for c in cots], expert, packed,
                          prev is not None, sums is not None, last),
        grid=(len(tiles),),
        in_specs=specs,
        out_specs=out_specs,
        out_shape=shapes,
        scratch_shapes=scratch,
        compiler_params=pltpu.CompilerParams(vmem_limit_bytes=60 * 1024 * 1024),
        cost_estimate=small_cost(),
    )(*args)
    parts = [(out[2 * t], out[2 * t + 1]) for t in range(len(tiles))]
    return parts, tuple(out[2 * len(tiles) :])


def shards(device_count, hidden_in, lengths, routes, norm_attn, w_query, w_key, w_value, w_out,
           norm_moe, w_router, w_gate, w_up, w_down, cotangent):
    n = device_count
    layers = n // GROUP
    along = [[q + GROUP * j for j in range(layers)] for q in range(GROUP)]
    inside = [[GROUP * j + q for q in range(GROUP)] for j in range(layers)]
    me = lax.axis_index("fsdp")
    place, layer = me % GROUP, me // GROUP
    core = lambda value: swap(value, 1, n)
    rows, width = hidden_in.shape
    own_rows = w_query.shape[0]
    hidden = w_gate.shape[2]
    own_hidden = w_down.shape[1]
    split = own_rows % 16 == 0
    thirds = width // hidden
    members = jnp.arange(GROUP, dtype=jnp.int32) ^ place
    steps = jnp.arange(layers, dtype=jnp.int32)

    extras = jnp.concatenate(
        [w_router, norm_attn[:, None], norm_moe[:, None], jnp.zeros((own_rows, LANES - E - 2), bf16)],
        axis=1,
    )
    own_qkv = jnp.concatenate([w_query, w_key, w_value, extras], axis=1)

    down_rows = jnp.concatenate(
        [w_down[:, :, t * hidden : (t + 1) * hidden] for t in range(thirds)], axis=1
    )
    expert_rows = jnp.concatenate([w_gate, w_up, down_rows], axis=1)
    per_expert = expert_rows.shape[1]
    expert_rows = expert_rows.reshape(GROUP, PAIR_E, per_expert, hidden).transpose(1, 0, 2, 3)

    expert_rows = lax.all_to_all(expert_rows, "fsdp", 1, 1, tiled=True, axis_index_groups=inside)

    def over_all(block):
        return lax.all_gather(block, "fsdp", axis=0, axis_index_groups=along)

    aligned = own_rows % 16 == 0 and own_hidden % 16 == 0

    def expert_parts(gathered):
        if aligned:
            return (gathered,)
        gate = gathered[:, :, :own_rows].reshape(width, hidden)
        up = gathered[:, :, own_rows : 2 * own_rows].reshape(width, hidden)
        low = gathered[:, :, 2 * own_rows :].reshape(layers, GROUP, thirds, own_hidden, hidden)
        return gate, up, low.transpose(0, 1, 3, 2, 4).reshape(hidden, width)

    segment, position = layout(lengths[0], rows)
    cosine, sine_val = turn_tables(position)
    half = HK // 4
    c_low, c_high = cotangent[: rows // 2], cotangent[rows // 2 :]
    near = lambda block: (swap(block, 2, n), swap(block, 4, n))
    cores = lambda *values: [core(value) for value in values]
    if split:
        ring = list(range(layers))
        plan = [[(k, j) for j in ring] for k in range(6)]
        upper = (layers + 1) // 2
        plan += [[(k, j) for j in part] for k in (6, 7) for part in (ring[:upper], ring[upper:]) if part]
        cut = upper * own_rows
        blocks = ring_start(own_qkv, layers, n)
        column = joined_rows(ring_end(blocks, layers, n), ring)
        column, expert_rows, w_out = tie(column, expert_rows, w_out)

        def far_ways(pair):
            ways = [swap(pair[0][:cut], 4, n)]
            return ways + ([swap(pair[1][cut:], 2, n)] if layers > 1 else [])

        def in_order(own, other, near_two, far):
            return [own, other[0], near_two[0], other[1], near_two[1], other[2], *far, *cores(*far)]

        near_qkv = near(column)
        wo_blocks = ring_start(w_out, layers, n)
        near_qkv, wo_blocks, cosine, sine_val = tie(near_qkv, wo_blocks, cosine, sine_val)
        far = far_ways(near_qkv)
        other = cores(column, *near_qkv)
        other, wo_blocks = tie(other, wo_blocks)
        wo_column = joined_rows(ring_end(wo_blocks, layers, n), ring)
        far, other, wo_column = tie(far, other, wo_column)
        pieces = in_order(column, other, near_qkv, far)
        pieces, wo_column = tie(pieces, wo_column)
        wo_near, wo_other = near(wo_column), core(wo_column)
        table = own_rows * (GROUP * steps[None, :] + members[:, None])
        ring_table = own_rows * (GROUP * ((layer - steps[None, :]) % layers) + members[:, None])
    else:
        pieces = [lax.all_gather(own_qkv, "fsdp", axis=0, tiled=True)]
        plan = [[(0, 0)]]
        table = ring_table = jnp.zeros((1, 1), jnp.int32)
    table, ring_table = table.astype(jnp.int32), ring_table.astype(jnp.int32)

    gathered_first, gathered_second = over_all(expert_rows[0]), over_all(expert_rows[1])
    w_qkv, normed, turned, *first_half = attend_forward(
        0, half, ring_table, plan, pieces, hidden_in, cosine, sine_val, segment
    )
    extras_full = w_qkv[:, QW + 2 * KW :]
    normed, c_low = tie(normed, c_low)
    if split:
        wo_near, wo_other, normed = tie(wo_near, wo_other, normed)
        wo_far = far_ways(wo_near)
    c_near_low = near(c_low)
    second_half = attend_forward(half, half, table, None, w_qkv, normed, cosine, sine_val, segment)
    attn_out = (first_half[3], second_half[3])
    if split:
        attn_out, c_near_low, c_high, wo_far, wo_near = tie(attn_out, c_near_low, c_high, wo_far, wo_near)
    else:
        attn_out, c_near_low, c_high = tie(attn_out, c_near_low, c_high)
    if split:
        out_pieces = in_order(wo_column, [wo_other, *cores(*wo_near)], wo_near, wo_far)
        out_pieces, c_high = tie(out_pieces, c_high)
    else:
        out_pieces = [lax.all_gather(w_out, "fsdp", axis=0, tiled=True)]

    c_near_high = near(c_high)
    c_other = [cores(c_low, *c_near_low)]
    w_out_full, middle, inner, mix = to_middle(
        ring_table, plan, out_pieces, hidden_in, attn_out, extras_full, routes
    )
    c_near_high, c_other, inner = tie(c_near_high, c_other, inner)
    c_other.append(cores(c_high, *c_near_high))

    def expert_sums(sums):
        if len(sums) == 1:
            return lax.psum_scatter(
                sums[0], "fsdp", scatter_dimension=0, tiled=True, axis_index_groups=along
            )[0]
        gate, up, low = sums
        low = low.reshape(layers, GROUP, own_hidden, thirds, hidden).transpose(0, 1, 3, 2, 4)
        joined = jnp.concatenate(
            [
                gate.reshape(layers, GROUP, own_rows, hidden),
                up.reshape(layers, GROUP, own_rows, hidden),
                low.reshape(layers, GROUP, thirds * own_hidden, hidden),
            ],
            axis=2,
        )
        return lax.psum_scatter(
            joined, "fsdp", scatter_dimension=0, tiled=True, axis_index_groups=along
        )[0]

    first = expert_parts(gathered_first)
    second = expert_parts(gathered_second)
    part = {}

    def run(expert, tiles, xs, cs, weights, sums, last):
        done, sums = experts_call(
            place, expert, xs, cs, weights, own_rows, [part[k] for k in tiles] if expert else None, sums, last
        )
        part.update(zip(tiles, done))
        return sums

    inner_near = gather_start(inner, n)
    x_own, c_own = [[inner], [core(inner)]], [[cotangent], [c_other[0][0], c_other[1][0]]]
    sums = run(0, [0, 1], x_own, c_own, first, None, False)
    inner_near = after(inner_near, sums)
    inner_far = gather_far(*inner_near, n)
    c_near_low, c_near_high, sums = tie(c_near_low, c_near_high, sums)
    cots_far = swap(c_near_low[0], 4, n), swap(c_near_high[1], 2, n)
    x_near = [[inner_near[0]], [core(inner_near[0])], [inner_near[1]], [core(inner_near[1])]]
    c_near = []
    for q in (0, 1):
        c_near += [[c_near_low[q], c_near_high[q]], [c_other[0][1 + q], c_other[1][1 + q]]]
    sums = run(0, [2, 3, 4, 5], x_near, c_near, first, sums, False)
    inner_far, cots_far = after((inner_far, cots_far), sums)
    x_far = [list(inner_far), [core(v) for v in inner_far]]
    c_far = [list(cots_far), [core(v) for v in cots_far]]
    sums0 = run(0, [6, 7], x_far, c_far, first, sums, True)
    shared0 = expert_sums(sums0)

    sums = run(1, [6, 7], x_far, c_far, second, None, False)
    both_ways = lambda low, high: (swap(low, 4, n), swap(high, 2, n))
    halves, out_halves = sums_for_far([(part[6][i], core(part[7][i])) for i in (1, 0)])
    x_near[0], halves, out_halves = tie(x_near[0], halves, out_halves)
    far_sums, out_far = both_ways(*halves), both_ways(*out_halves)
    sums = run(1, [2, 3, 4, 5], x_near, c_near, second, sums, False)
    done = [part[k] for k in (2, 3, 4, 5)]
    far_sums, out_far, sums, done = tie(far_sums, out_far, sums, done)
    part.update(zip((2, 3, 4, 5), done))
    near_sums = sums_for_near(part[2][1], core(part[3][1]), part[4][1], core(part[5][1]), *far_sums)
    x_own[0], near_sums, shared0 = tie(x_own[0], near_sums, shared0)
    inner_near = [swap(value, bit, n) for value, bit in zip(near_sums, (2, 4))]
    out_core = [core(part[3][0]), core(part[5][0])]
    sums = run(1, [0, 1], x_own, c_own, second, sums, True)
    inner_near, out_core, sums, part[0], part[1] = tie(inner_near, out_core, sums, part[0], part[1])
    shared1 = expert_sums(sums)
    inner_other = core(part[1][1])
    out_blocks = (part[2][0], out_core[0], part[4][0], out_core[1])
    out_sums = half_for_near(0, *out_blocks, out_far[0])
    out_sums, inner_other = tie(out_sums, inner_other)
    out_low = [swap(out_sums[0], 2, n), swap(out_sums[1], 4, n)]
    out_other = core(part[1][0])
    *out_grads, middle_grad, attn_grad0, attn_grad1 = middle_back(
        table, (part[0][1], inner_other, *inner_near), inner, mix, middle, cotangent, extras_full, attn_out,
        w_out_full,
    )
    out_low, out_other, out_grads, middle_grad, attn_grad0, attn_grad1 = tie(
        out_low, out_other, out_grads, middle_grad, attn_grad0, attn_grad1
    )

    wide = lambda value: value.astype(f32)

    def chips_of(stacks):
        return sums_of_stack(stacks[0], core(stacks[1])) if split else [stacks[0]]

    def far_of(chips):
        return both_ways(*chips[3:]) if split else ()

    def near_of(*sets):
        if not split:
            return ()
        sum2, sum4 = stack_near([(*chips[1:3], *far) for chips, far in sets])
        return swap(sum2, 2, n), swap(sum4, 4, n)

    def over_layers(sets):
        if not split:
            sums = [
                lax.psum_scatter(chips[0], "fsdp", scatter_dimension=0, tiled=True)
                for group, _ in sets
                for chips in group
            ]
            return [jnp.concatenate(sums, axis=1)]
        total = []
        for group, near_sums in sets:
            own = jnp.concatenate([chips[0] for chips in group], axis=1)
            total.append((wide(own) + wide(near_sums[0]) + wide(near_sums[1])).astype(bf16))
        total = jnp.concatenate(total, axis=1)
        return layer_start(total.reshape(layers, own_rows, -1), layer, layers, n)

    def back(base, steps, half_set, grads):
        return attend_backward(
            base, steps, table, turned, *half_set[:3], grads, half_set[4], cosine, sine_val, segment
        )

    wo_chips = chips_of(out_grads)
    out_sums = half_for_near(1, *tie(*out_blocks, middle_grad)[:4], out_far[1])
    attn_grad0, wo_chips, out_sums = tie(attn_grad0, wo_chips, out_sums)
    out_high = [swap(value, bit, n) for value, bit in zip(out_sums, (2, 4))]
    wo_far = far_of(wo_chips)
    *stacks0, dq0, dk0, dv0 = back(0, half, first_half, attn_grad0)
    out_high, wo_far, stacks0, dq0, dk0, dv0 = tie(out_high, wo_far, stacks0, dq0, dk0, dv0)

    chips0 = chips_of(stacks0)
    attn_grad1, chips0 = tie(attn_grad1, chips0)
    wo_near, far0 = near_of((wo_chips, wo_far)), far_of(chips0)
    *stacks1, dq1, dk1, dv1 = back(0, half // 2, second_half, attn_grad1)
    wo_near, far0, stacks1, dq1, dk1, dv1 = tie(wo_near, far0, stacks1, dq1, dk1, dv1)

    chips1 = chips_of(stacks1)
    attn_grad1, chips1, dq1, shared1 = tie(attn_grad1, chips1, dq1, shared1)
    near0, far1 = near_of((chips0, far0)), far_of(chips1)
    *stacks2, dq2, dk2, dv2 = back(half // 2, half - half // 2, second_half, attn_grad1)
    near0, far1, stacks2, dq2, dk2, dv2, wo_near = tie(near0, far1, stacks2, dq2, dk2, dv2, wo_near)

    to_owner = lambda block: lax.all_to_all(
        block, "fsdp", 0, 0, tiled=True, axis_index_groups=inside
    )
    chips2 = chips_of(stacks2)
    dq2, chips2 = tie(dq2, chips2)
    far2 = far_of(chips2)
    owned0 = to_owner(shared0)
    early = over_layers([([wo_chips], wo_near), ([chips0], near0)])
    input_grad = to_input(
        hidden_in, middle_grad, w_qkv, (dq0, dk0, dv0, dq1, dk1, dv1, dq2, dk2, dv2)
    )
    far2, early, input_grad, owned0 = tie(far2, early, input_grad, owned0)
    near12 = near_of((chips1, far1), (chips2, far2))
    owned1 = to_owner(after(shared1, near12))
    out_low, near12 = tie(out_low, near12)
    out_total = wide(part[0][0]) + wide(out_other) + jnp.concatenate(
        [wide(out_low[0]) + wide(out_low[1]), wide(out_high[0]) + wide(out_high[1])], axis=0
    )
    mixed = (middle + resid_scale * out_total).astype(bf16)
    early = layer_add(early)
    mine_out = early[:, : width + LANES]
    late = layer_add(over_layers([([chips1, chips2], near12)]))
    unit1, unit2 = chips1[0].shape[1], chips2[0].shape[1]
    mine = [early[:, width + LANES :], late[:, :unit1], late[:, unit1 : unit1 + unit2]]

    shared = jnp.stack([owned0, owned1], axis=1).reshape(E, per_expert, hidden).astype(f32)
    grad_gate, grad_up = shared[:, :own_rows], shared[:, own_rows : 2 * own_rows]
    grad_down = jnp.concatenate(
        [
            shared[:, 2 * own_rows + t * own_hidden : 2 * own_rows + (t + 1) * own_hidden]
            for t in range(thirds)
        ],
        axis=2,
    )
    def joined(kind):
        pieces = []
        for part_grads in mine:
            unit = part_grads.shape[1] // 5
            start, wide = ((0, 3 * unit), (3 * unit, unit), (4 * unit, unit))[kind]
            pieces.append(part_grads[:, start : start + wide])
        return jnp.concatenate(pieces, axis=1)

    grad_query, grad_key, grad_value = joined(0), joined(1), joined(2)
    grad_router = mine_out[:, width : width + E]

    def row_sums(weight, grad):
        return jnp.sum(weight.astype(f32) * grad, axis=-1)

    grad_norm_attn = (
        row_sums(w_query, grad_query) + row_sums(w_key, grad_key) + row_sums(w_value, grad_value)
    ) / norm_attn.astype(f32)
    grad_norm_moe = (
        jnp.sum(row_sums(w_gate, grad_gate) + row_sums(w_up, grad_up), axis=0)
        + row_sums(w_router, grad_router)
    ) / norm_moe.astype(f32)
    return (
        mixed,
        input_grad,
        grad_norm_attn,
        grad_query,
        grad_key,
        grad_value,
        mine_out[:, :width],
        grad_norm_moe,
        grad_router,
        grad_gate,
        grad_up,
        grad_down,
    )


def solution(mesh):

    in_specs = (
        P("fsdp", None),
        P("fsdp", None),
        P("fsdp", None),
        P("fsdp"),
        P("fsdp", None),
        P("fsdp", None),
        P("fsdp", None),
        P("fsdp", None),
        P("fsdp"),
        P("fsdp", None),
        P(None, "fsdp", None),
        P(None, "fsdp", None),
        P(None, "fsdp", None),
        P("fsdp", None),
    )
    out_specs = (
        P("fsdp", None),
        P("fsdp", None),
        P("fsdp"),
        P("fsdp", None),
        P("fsdp", None),
        P("fsdp", None),
        P("fsdp", None),
        P("fsdp"),
        P("fsdp", None),
        P(None, "fsdp", None),
        P(None, "fsdp", None),
        P(None, "fsdp", None),
    )
    return jax.shard_map(
        functools.partial(shards, mesh.shape["fsdp"]),
        mesh=mesh,
        in_specs=in_specs,
        out_specs=out_specs,
        check_vma=False,
    )
```

```python
import functools
import math

import jax
import jax.numpy as jnp
from jax import lax
from jax.experimental import pallas as pl
from jax.experimental.pallas import tpu as pltpu
from jax.sharding import PartitionSpec as P

HQ = 24
HK = 8
HD = 64
E = 16
GROUP = 8
PAIR_E = E // GROUP
HEADS_STEP = 2 * HQ // HK
LANES = 128
QW = HQ * HD
KW = HK * HD
QKV_WIDE = QW + 2 * KW + LANES
GAIN_ONE = E
GAIN_TWO = E + 1
VMEM_LIMIT = 58 * 1024 * 1024

norm_eps = 1e-06
resid_scale = 0.22
score_scale = 0.015625
rope_base = 10000.0
masked_score = -1e30

f32 = jnp.float32
bf16 = jnp.bfloat16


def matmul(left, right):
    return jnp.dot(left, right, preferred_element_type=f32)


def contract_rows(left, right):
    return lax.dot_general(left, right, (((0,), (0,)), ((), ())), preferred_element_type=f32)


def contract_last(left, right):
    return lax.dot_general(left, right, (((1,), (1,)), ((), ())), preferred_element_type=f32)


def layout(seq_lengths, row_count):
    seq_ends = jnp.cumsum(seq_lengths)
    starts = seq_ends - seq_lengths
    places = jnp.arange(row_count, dtype=jnp.int32)
    member = (places[:, None] >= starts[None, :]) & (places[:, None] < seq_ends[None, :])
    labels = jnp.arange(seq_lengths.shape[0], dtype=jnp.int32)
    segment = jnp.sum(jnp.where(member, labels[None, :], 0), axis=1)
    offset = jnp.sum(jnp.where(member, starts[None, :], 0), axis=1)
    return (segment, places - offset)


def turn_tables(position):
    half_dim = HD // 2
    inv_freq = jnp.exp(
        -(jnp.arange(half_dim, dtype=f32) * (2.0 / HD)) * math.log(rope_base)
    )
    angles = position.astype(f32)[:, None] * inv_freq[None, :]
    cosine, sine_val = jnp.cos(angles), jnp.sin(angles)
    return (
        jnp.concatenate([cosine] * 4, axis=1),
        jnp.concatenate([-sine_val, sine_val] * 2, axis=1),
    )


def swap(value, bit, device_count):
    return lax.ppermute(value, "fsdp", [(i, i ^ bit) for i in range(device_count)])


def shift(value, steps, device_count):
    moved = [(i, (i + GROUP * steps) % device_count) for i in range(device_count)]
    return lax.ppermute(value, "fsdp", moved)


def after(value, *needed):
    return lax.optimization_barrier((value, needed))[0]


def tie(*values):
    return lax.optimization_barrier(values)


def ring_start(own, layers, device_count):
    blocks = {0: own}
    ahead, behind = own, own
    for step in range(1, (layers - 1) // 2 + 1):
        ahead, behind = shift(ahead, 1, device_count), shift(behind, -1, device_count)
        blocks[step], blocks[layers - step] = ahead, behind
    return blocks


def ring_end(blocks, layers, device_count):
    if layers % 2 == 0:
        ahead, behind = blocks[layers // 2 - 1], blocks[(layers // 2 + 1) % layers]
        half = ahead.shape[1] // 2 // LANES * LANES
        blocks[layers // 2] = jnp.concatenate(
            [shift(ahead[:, :half], 1, device_count), shift(behind[:, half:], -1, device_count)], axis=1
        )
    return blocks


def joined_rows(blocks, places):
    return jnp.concatenate([blocks[j] for j in places], axis=0)


def gather_start(own, device_count):
    return swap(own, 2, device_count), swap(own, 4, device_count)


def gather_far(from2, from4, device_count):
    half = from2.shape[0] // 2
    return swap(from2[:half], 4, device_count), swap(from4[half:], 2, device_count)


def gather_cores(own, near, far, device_count):
    other = lambda value: swap(value, 1, device_count)
    return [
        [own], [other(own)], [near[0]], [other(near[0])], [near[1]], [other(near[1])],
        list(far), [other(far[0]), other(far[1])],
    ]


def layer_start(stacked, layer, layers, device_count):
    pick = lambda at: lax.dynamic_index_in_dim(stacked, at % layers, 0, keepdims=False)
    return [pick(layer)] + [shift(pick(layer + k), k, device_count) for k in range(1, layers)]


def layer_add(blocks):
    total = blocks[0].astype(f32)
    for block in blocks[1:]:
        total = total + block.astype(f32)
    return total


def turn(values, cosine, sine_val, low_half):
    shifted = jnp.where(low_half, pltpu.roll(values, LANES - 32, 1), pltpu.roll(values, 32, 1))
    return values * cosine + shifted * sine_val


def half_views(pair, scale):
    lane = lax.broadcasted_iota(jnp.int32, pair.shape, 1)
    scaled = pair.astype(f32) * scale
    low = lane < HD
    return jnp.where(low, scaled, 0.0).astype(bf16), jnp.where(low, 0.0, scaled).astype(bf16)


def head_tiles(tiles):
    return [
        tiles[head // 2] if head % 2 == head // 3 else pltpu.roll(tiles[head // 2], HD, 1)
        for head in range(HEADS_STEP)
    ]


def visible_keys(seg_col, seg_row, row_start, rows, keys):
    query_at = row_start + lax.broadcasted_iota(jnp.int32, (rows, keys), 0)
    key_at = lax.broadcasted_iota(jnp.int32, (rows, keys), 1)
    return (seg_col[row_start : row_start + rows, :] == seg_row[:, :keys]) & (key_at <= query_at)


def any_spec():
    return pl.BlockSpec(memory_space=pl.ANY)


def smem_spec():
    return pl.BlockSpec(memory_space=pltpu.SMEM)


def small_cost():
    return pl.CostEstimate(flops=1_000_000, bytes_accessed=100_000, transcendentals=0)


def extras_spec(width):
    return pl.BlockSpec((width, LANES), lambda *_: (0, (QW + 2 * KW) // LANES))


def params():
    return pltpu.CompilerParams(vmem_limit_bytes=VMEM_LIMIT)


def whole_spec(shape):
    zeros = (0,) * len(shape)
    return pl.BlockSpec(shape, lambda *_: zeros, pipeline_mode=pl.Buffered(1))


def gather_copies(plan, refs, table_ref, dst, sems):
    copies = []
    for ref, runs in zip(refs, plan):
        rows = ref.shape[0] // len(runs)
        for number, (member, step) in enumerate(runs):
            start = pl.multiple_of(table_ref[member, step], 16)
            copies.append(
                pltpu.make_async_copy(
                    ref.at[pl.ds(number * rows, rows)],
                    dst.at[pl.ds(start, rows)],
                    sems.at[len(copies)],
                )
            )
    return copies


def spread_copies(src, table_ref, refs, sems):
    copies = []
    members, blocks = table_ref.shape
    rows = src.shape[0] // (members * blocks)
    for member in range(members):
        for block in range(blocks):
            start = pl.multiple_of(table_ref[member, block], 16)
            to = (member // 2 * blocks + block) * rows
            copies.append(
                pltpu.make_async_copy(
                    src.at[pl.ds(start, rows)], refs[member % 2].at[pl.ds(to, rows)], sems.at[len(copies)]
                )
            )
    return copies


def stack_shapes(table, width, full):
    members = table.shape[0]
    stacks = min(members, 2)
    return [jax.ShapeDtypeStruct((width // stacks, full), bf16)] * stacks


def far_kernel(*refs):
    count = len(refs) // 4
    for q in range(count):
        left, right = refs[2 * q : 2 * q + 2]
        low, high = refs[2 * count + 2 * q : 2 * count + 2 * q + 2]
        total = (left[...].astype(f32) + right[...].astype(f32)).astype(bf16)
        low[...] = total[0]
        high[...] = total[1]


def sums_for_far(pairs):
    rows = pairs[0][0].shape[0]
    tile = rows // 8
    args, in_specs, out_specs, shapes = [], [], [], []
    for pair in pairs:
        width = pair[0].shape[1]
        args += [value.reshape(2, rows // 2, width) for value in pair]
        in_specs += [pl.BlockSpec((2, tile, width), lambda i: (0, i, 0))] * 2
        out_specs += [pl.BlockSpec((tile, width), lambda i: (i, 0))] * 2
        shapes += [jax.ShapeDtypeStruct((rows // 2, width), bf16)] * 2
    out = pl.pallas_call(
        far_kernel, grid=(4,), in_specs=in_specs, out_specs=out_specs, out_shape=shapes,
        compiler_params=params(), cost_estimate=small_cost(),
    )(*args)
    return [out[2 * q : 2 * q + 2] for q in range(len(pairs))]


def near_kernel(a2_ref, b2_ref, a4_ref, b4_ref, low_ref, high_ref, sum2_ref, sum4_ref):
    two = a2_ref[...].astype(f32) + b2_ref[...].astype(f32)
    four = a4_ref[...].astype(f32) + b4_ref[...].astype(f32)
    sum2_ref[0] = (two[0] + low_ref[...].astype(f32)).astype(bf16)
    sum2_ref[1] = two[1].astype(bf16)
    sum4_ref[0] = four[0].astype(bf16)
    sum4_ref[1] = (four[1] + high_ref[...].astype(f32)).astype(bf16)


def sums_for_near(a2, b2, a4, b4, low, high):
    rows, width = a2.shape
    tile = rows // 8
    pair = pl.BlockSpec((2, tile, width), lambda i: (0, i, 0))
    single = pl.BlockSpec((tile, width), lambda i: (i, 0))
    out = pl.pallas_call(
        near_kernel, grid=(4,), in_specs=[pair] * 4 + [single] * 2, out_specs=[pair] * 2,
        out_shape=[jax.ShapeDtypeStruct((2, rows // 2, width), bf16)] * 2,
        compiler_params=params(), cost_estimate=small_cost(),
    )(*[value.reshape(2, rows // 2, width) for value in (a2, b2, a4, b4)], low, high)
    return [value.reshape(rows, width) for value in out]


def half_kernel(more_for, a2_ref, b2_ref, a4_ref, b4_ref, more_ref, sum2_ref, sum4_ref):
    two = a2_ref[...].astype(f32) + b2_ref[...].astype(f32)
    four = a4_ref[...].astype(f32) + b4_ref[...].astype(f32)
    more = more_ref[...].astype(f32)
    sum2_ref[...] = (two + more if more_for == 2 else two).astype(bf16)
    sum4_ref[...] = (four + more if more_for == 4 else four).astype(bf16)


def half_for_near(which, a2, b2, a4, b4, more):
    rows, width = a2.shape
    tile = rows // 8
    picked = pl.BlockSpec((tile, width), lambda i: (4 * which + i, 0))
    single = pl.BlockSpec((tile, width), lambda i: (i, 0))
    return pl.pallas_call(
        functools.partial(half_kernel, (2, 4)[which]), grid=(4,), in_specs=[picked] * 4 + [single],
        out_specs=[single] * 2, out_shape=[jax.ShapeDtypeStruct((rows // 2, width), bf16)] * 2,
        compiler_params=params(), cost_estimate=small_cost(),
    )(a2, b2, a4, b4, more)


def stack_kernel(even_ref, odd_ref, own_ref, two_ref, four_ref, low_ref, high_ref):
    rows = own_ref.shape[0]
    half = rows // 2
    spots = ((own_ref, 0, rows), (two_ref, rows, rows), (four_ref, 2 * rows, rows), (low_ref, 3 * rows, half),
             (high_ref, 3 * rows + half, half))
    for ref, start, count in spots:
        at = slice(start, start + count)
        ref[...] = (even_ref[at].astype(f32) + odd_ref[at].astype(f32)).astype(bf16)


def sums_of_stack(even, odd):
    rows, width = even.shape[0] // 4, even.shape[1]
    vmem = pl.BlockSpec(memory_space=pltpu.VMEM)
    return pl.pallas_call(
        stack_kernel, in_specs=[vmem] * 2, out_specs=[vmem] * 5,
        out_shape=[jax.ShapeDtypeStruct((r, width), bf16) for r in (rows, rows, rows, rows // 2, rows // 2)],
        compiler_params=params(), cost_estimate=small_cost(),
    )(even, odd)


def stack_near_kernel(*refs):
    *sources, sum2_ref, sum4_ref = refs
    start = 0
    for q in range(0, len(sources), 4):
        two_ref, four_ref, low_ref, high_ref = sources[q : q + 4]
        half = low_ref.shape[0]
        at = slice(start, start + two_ref.shape[1])
        sum2_ref[:half, at] = (two_ref[:half].astype(f32) + low_ref[...].astype(f32)).astype(bf16)
        sum2_ref[half:, at] = two_ref[half:]
        sum4_ref[:half, at] = four_ref[:half]
        sum4_ref[half:, at] = (four_ref[half:].astype(f32) + high_ref[...].astype(f32)).astype(bf16)
        start += two_ref.shape[1]


def stack_near(sets):
    vmem = pl.BlockSpec(memory_space=pltpu.VMEM)
    shape = (sets[0][0].shape[0], sum(one[0].shape[1] for one in sets))
    return pl.pallas_call(
        stack_near_kernel, in_specs=[vmem] * (4 * len(sets)), out_specs=[vmem] * 2,
        out_shape=[jax.ShapeDtypeStruct(shape, bf16)] * 2,
        compiler_params=params(), cost_estimate=small_cost(),
    )(*[value for one in sets for value in one])


def attend_kernel(block, plan, table_ref, x_ref, cos_ref, sin_ref, segc_ref, segr_ref, *refs):
    pair = pl.program_id(0)
    rows_all, width = x_ref.shape
    at = lambda start, wide: pl.ds(pl.multiple_of(start, LANES), wide)
    if plan is None:
        wq_ref, wk_ref, wv_ref, q_ref, k_ref, v_ref, out_ref, lse_ref = refs
        normed_ref = x_ref
        w_q, w_k, w_v = wq_ref[...], wk_ref[...], wv_ref[...]
    else:
        sources = refs[: len(plan)]
        (w_out_ref, normed_ref, turned_ref, q_ref, k_ref, v_ref, out_ref, lse_ref,
         w_ref, sems, save_sem) = refs[len(plan) :]

        @pl.when(pair == 0)
        def _():
            copies = gather_copies(plan, sources, table_ref, w_ref, sems)
            for c in copies:
                c.start()
            x = x_ref[...].astype(f32)
            rinv = lax.rsqrt(jnp.mean(x * x, axis=-1, keepdims=True) + norm_eps)
            for c in copies:
                c.wait()
            pltpu.make_async_copy(w_ref, w_out_ref, save_sem).start()
            gains = w_ref[:, QW + 2 * KW :].astype(f32).T
            scaled = x * rinv * gains[GAIN_ONE : GAIN_ONE + 1, :]
            normed_ref[...] = scaled.astype(bf16)
            turned_ref[...] = scaled.T.astype(bf16)

        w_q = w_ref[:, at(pair * 3 * LANES, 3 * LANES)]
        w_k = w_ref[:, at(QW + pair * LANES, LANES)]
        w_v = w_ref[:, at(QW + KW + pair * LANES, LANES)]

    normed = normed_ref[...]
    lane = lax.broadcasted_iota(jnp.int32, (rows_all, LANES), 1)
    first = (lane % HD) < (HD // 2)
    cosine, sine_val = cos_ref[...], sin_ref[...]
    q_pre = matmul(normed, w_q)
    tiles = []
    for t in range(3):
        cols = slice(t * LANES, (t + 1) * LANES)
        tiles.append(turn(q_pre[:, cols], cosine, sine_val, first))
        q_ref[:, cols] = tiles[t].astype(bf16)
    heads = [tile.astype(bf16) for tile in head_tiles(tiles)]
    k_low = turn(matmul(normed, w_k), cosine, sine_val, first).astype(bf16)
    v_low = matmul(normed, w_v).astype(bf16)
    k_ref[...] = k_low
    v_ref[...] = v_low
    k_views = half_views(k_low, score_scale)
    v_views = half_views(v_low, 1.0)
    seg_col, seg_row = segc_ref[...], segr_ref[...]
    lane_b = lax.broadcasted_iota(jnp.int32, (block, LANES), 1)
    for start in range(0, rows_all, block):
        keys = start + block
        rows = slice(start, keys)
        visible = visible_keys(seg_col, seg_row, start, block, keys)
        norms = jnp.zeros((block, LANES), f32)
        outs = []
        for kv in range(2):
            q_rows = jnp.concatenate([heads[3 * kv + j][rows] for j in range(3)], axis=0)
            scores = contract_last(q_rows, k_views[kv][:keys]).reshape(3, block, keys)
            scores = jnp.where(visible[None], scores, masked_score)
            peak = jnp.max(scores, axis=-1, keepdims=True)
            expo = jnp.exp(scores - peak)
            mass = jnp.sum(expo, axis=-1, keepdims=True)
            probs = (expo * (1.0 / mass)).astype(bf16)
            total = matmul(probs.reshape(3 * block, keys), v_views[kv][:keys])
            norm = peak + jnp.log(mass)
            for j in range(3):
                outs.append(total[j * block : (j + 1) * block])
                norms = jnp.where(lane_b == 3 * kv + j, norm[j], norms)
        for t in range(3):
            low, high = outs[2 * t], outs[2 * t + 1]
            low = pltpu.roll(low, HD, 1) if t == 2 else low
            high = pltpu.roll(high, HD, 1) if t == 0 else high
            out_ref[rows, t * LANES : (t + 1) * LANES] = (low + high).astype(bf16)
        lse_ref[0, rows, :] = norms

    if plan is not None:
        @pl.when(pair == pl.num_programs(0) - 1)
        def _():
            pltpu.make_async_copy(w_ref, w_out_ref, save_sem).wait()


def attend_forward(base, steps, table, plan, weights, rows_in, cosine, sine_val, segment):
    rows, width = rows_in.shape
    wide = pl.BlockSpec((rows, 3 * LANES), lambda i: (0, i))
    thin = pl.BlockSpec((rows, LANES), lambda i: (0, i))
    in_specs = [
        smem_spec(),
        whole_spec((rows, width)),
        whole_spec((rows, LANES)),
        whole_spec((rows, LANES)),
        whole_spec((rows, 1)),
        whole_spec((1, rows)),
    ]
    out_specs = [wide, thin, thin, wide, pl.BlockSpec((1, rows, LANES), lambda i: (i, 0, 0))]
    out_shape = [
        jax.ShapeDtypeStruct((rows, 3 * LANES * steps), bf16),
        jax.ShapeDtypeStruct((rows, LANES * steps), bf16),
        jax.ShapeDtypeStruct((rows, LANES * steps), bf16),
        jax.ShapeDtypeStruct((rows, 3 * LANES * steps), bf16),
        jax.ShapeDtypeStruct((steps, rows, LANES), f32),
    ]
    if plan is None:
        in_specs += [
            pl.BlockSpec((width, 3 * LANES), lambda i: (0, base + i)),
            pl.BlockSpec((width, LANES), lambda i: (0, QW // LANES + base + i)),
            pl.BlockSpec((width, LANES), lambda i: (0, (QW + KW) // LANES + base + i)),
        ]
        weights = [weights] * 3
        scratch = []
    else:
        in_specs += [any_spec()] * len(weights)
        out_specs = [any_spec(), whole_spec((rows, width)), whole_spec((width, rows))] + out_specs
        out_shape = [
            jax.ShapeDtypeStruct((width, QKV_WIDE), bf16),
            jax.ShapeDtypeStruct((rows, width), bf16),
            jax.ShapeDtypeStruct((width, rows), bf16),
        ] + out_shape
        scratch = [
            pltpu.VMEM((width, QKV_WIDE), bf16),
            pltpu.SemaphoreType.DMA((sum(len(r) for r in plan),)),
            pltpu.SemaphoreType.DMA(()),
        ]
    return pl.pallas_call(
        functools.partial(attend_kernel, 128, plan),
        grid=(steps,),
        in_specs=in_specs,
        out_specs=out_specs,
        out_shape=out_shape,
        scratch_shapes=scratch,
        compiler_params=params(),
        cost_estimate=small_cost(),
    )(table, rows_in, cosine, sine_val, segment[:, None], segment[None, :], *weights)


def middle_kernel(plan, table_ref, x_ref, attn0_ref, attn1_ref, extras_ref, routes_ref, *refs):
    sources = refs[: len(plan)]
    w_out_ref, middle_ref, inner_ref, mix_ref, w_ref, sems, save_sem = refs[len(plan) :]
    copies = gather_copies(plan, sources, table_ref, w_ref, sems)
    for c in copies:
        c.start()
    extras = extras_ref[...]
    gains = extras.astype(f32).T
    rows, width = x_ref.shape
    for c in copies:
        c.wait()
    save = pltpu.make_async_copy(w_ref, w_out_ref, save_sem)
    save.start()
    half = attn0_ref.shape[1]
    product = matmul(attn0_ref[...], w_ref[:half]) + matmul(attn1_ref[...], w_ref[half:])
    middle = x_ref[...].astype(f32) + resid_scale * product
    middle_ref[...] = middle
    rinv = lax.rsqrt(jnp.mean(middle * middle, axis=-1, keepdims=True) + norm_eps)
    inner = (middle * rinv * gains[GAIN_TWO : GAIN_TWO + 1, :]).astype(bf16)
    inner_ref[:, :width] = inner
    logits = matmul(inner, extras)
    lane = lax.broadcasted_iota(jnp.int32, logits.shape, 1)
    routes = routes_ref[...]
    named = lane == routes[:, 0:1]
    for k in range(1, routes.shape[1]):
        named = named | (lane == routes[:, k : k + 1])
    chosen = jnp.where(named, logits, masked_score)
    peak = jnp.max(chosen, axis=-1, keepdims=True)
    expo = jnp.where(named, jnp.exp(chosen - peak), 0.0)
    mix = expo / jnp.sum(expo, axis=-1, keepdims=True)
    mix_ref[...] = mix
    high = mix.astype(bf16).astype(f32)
    rest = (mix - high).astype(bf16).astype(f32)
    low = mix - high - rest
    spread = high + pltpu.roll(rest, E, 1) + pltpu.roll(low, 2 * E, 1)
    inner_ref[:, width:] = spread.astype(bf16)
    save.wait()


def to_middle(table, plan, pieces, hidden_in, attn_out, extras, routes):
    rows, width = hidden_in.shape
    vmem = pl.BlockSpec(memory_space=pltpu.VMEM)
    return pl.pallas_call(
        functools.partial(middle_kernel, plan),
        grid=(1,),
        in_specs=[smem_spec()] + [vmem] * 3 + [extras_spec(width), vmem] + [any_spec()] * len(pieces),
        out_specs=[any_spec(), vmem, vmem, vmem],
        out_shape=[
            jax.ShapeDtypeStruct((QW, width), bf16),
            jax.ShapeDtypeStruct((rows, width), f32),
            jax.ShapeDtypeStruct((rows, width + LANES), bf16),
            jax.ShapeDtypeStruct((rows, LANES), f32),
        ],
        scratch_shapes=[
            pltpu.VMEM((QW, width), bf16),
            pltpu.SemaphoreType.DMA((sum(len(r) for r in plan),)),
            pltpu.SemaphoreType.DMA(()),
        ],
        compiler_params=params(),
        cost_estimate=small_cost(),
    )(table, hidden_in, *attn_out, extras, routes, *pieces)


def middle_back_kernel(blocks, table_ref, own0_ref, own1_ref, near2_ref, near4_ref, inner_ref, mix_ref, middle_ref,
                       cot_ref, extras_ref, attn0_src, attn1_src, w_src, *refs):
    dests = refs[:blocks]
    (grad_ref, attn_grad0_ref, attn_grad1_ref, wgrad_ref, attn0_ref, attn1_ref, w_ref, sems,
     load_sems) = refs[blocks:]
    rows, width = middle_ref.shape
    loads = [
        pltpu.make_async_copy(a, b, load_sems.at[q])
        for q, (a, b) in enumerate(((w_src, w_ref), (attn0_src, attn0_ref), (attn1_src, attn1_ref)))
    ]
    for c in loads:
        c.start()
    total = own0_ref[...].astype(f32) + own1_ref[...].astype(f32)
    total = total + near2_ref[...].astype(f32) + near4_ref[...].astype(f32)
    inner_grad, tail = total[:, :width], total[:, width:]
    lane = lax.broadcasted_iota(jnp.int32, tail.shape, 1)
    mix = mix_ref[...]
    mix_grad = tail + pltpu.roll(tail, LANES - E, 1) + pltpu.roll(tail, LANES - 2 * E, 1)
    mix_grad = jnp.where(lane < E, mix_grad, 0.0)
    logit_grad = mix_grad - mix * jnp.sum(mix_grad, axis=-1, keepdims=True)
    logit_grad = logit_grad.astype(bf16)
    extras = extras_ref[...]
    gain = extras.astype(f32).T[GAIN_TWO : GAIN_TWO + 1, :]
    inner_grad = inner_grad + contract_last(logit_grad, extras)
    middle = middle_ref[...]
    rinv = lax.rsqrt(jnp.mean(middle * middle, axis=-1, keepdims=True) + norm_eps)
    scaled = gain * inner_grad
    back = rinv * scaled - middle * (rinv * rinv * rinv * jnp.mean(scaled * middle, axis=-1, keepdims=True))
    middle_grad = cot_ref[...].astype(f32) + back
    grad_ref[...] = middle_grad
    proj_grad = (resid_scale * middle_grad).astype(bf16)
    half = attn0_ref.shape[1]
    for c in loads:
        c.wait()
    attn_grad0_ref[...] = contract_last(proj_grad, w_ref[:half]).astype(bf16)
    attn_grad1_ref[...] = contract_last(proj_grad, w_ref[half:]).astype(bf16)
    wgrad_ref[:half, :width] = contract_rows(attn0_ref[...], proj_grad).astype(bf16)
    wgrad_ref[half:, :width] = contract_rows(attn1_ref[...], proj_grad).astype(bf16)
    wgrad_ref[:, width:] = contract_rows(inner_ref[:, :width], logit_grad).astype(bf16)
    copies = spread_copies(wgrad_ref, table_ref, dests, sems)
    for c in copies:
        c.start()
    for c in copies:
        c.wait()


def middle_back(table, sums, inner, mix, middle, cotangent, extras, attn_out, w_out):
    rows, width = middle.shape
    members, layers = table.shape
    vmem = pl.BlockSpec(memory_space=pltpu.VMEM)
    full = width + LANES
    return pl.pallas_call(
        functools.partial(middle_back_kernel, min(members, 2)),
        grid=(1,),
        in_specs=[smem_spec()] + [vmem] * 8 + [extras_spec(width)] + [any_spec()] * 3,
        out_specs=[any_spec()] * min(members, 2) + [vmem] * 3,
        out_shape=stack_shapes(table, width, full)
        + [jax.ShapeDtypeStruct((rows, width), f32)]
        + [jax.ShapeDtypeStruct((rows, QW // 2), bf16)] * 2,
        scratch_shapes=[
            pltpu.VMEM((width, full), bf16),
            pltpu.VMEM((rows, QW // 2), bf16),
            pltpu.VMEM((rows, QW // 2), bf16),
            pltpu.VMEM(w_out.shape, bf16),
            pltpu.SemaphoreType.DMA((members * layers,)),
            pltpu.SemaphoreType.DMA((3,)),
        ],
        compiler_params=params(),
        cost_estimate=small_cost(),
    )(table, *sums, inner, mix, middle, cotangent, extras, *attn_out, w_out)


def attend_back_kernel(block, blocks, table_ref, turned_ref, q_ref, k_ref, v_ref, grad_ref, lse_ref,
                       cos_ref, sin_ref, segc_ref, segr_ref, *refs):
    dests = refs[:blocks]
    dq_ref, dk_ref, dv_ref, dkt_ref, dvt_ref, wgrad_ref, sems = refs[blocks:]
    step = pl.program_id(0)
    width, rows_all = turned_ref.shape
    lane = lax.broadcasted_iota(jnp.int32, (rows_all, LANES), 1)
    first = (lane % HD) < (HD // 2)
    k_views = half_views(k_ref[...], score_scale)
    v_views = half_views(v_ref[...], 1.0)
    tile_cols = [slice(t * LANES, (t + 1) * LANES) for t in range(3)]
    q_tiles = [q_ref[:, cols].astype(f32) for cols in tile_cols]
    g_tiles = [grad_ref[:, cols].astype(f32) for cols in tile_cols]
    q_heads = [tile.astype(bf16) for tile in head_tiles(q_tiles)]
    g_heads = [tile.astype(bf16) for tile in head_tiles(g_tiles)]

    def turned_heads(tiles):
        out = []
        for head in range(HEADS_STEP):
            tile = tiles[head // 2].T
            if head % 2 != head // 3:
                tile = jnp.concatenate([tile[HD:], tile[:HD]], axis=0)
            out.append(tile.astype(bf16))
        return out

    q_turned, g_turned = turned_heads(q_tiles), turned_heads(g_tiles)
    dkt_ref[...] = jnp.zeros_like(dkt_ref)
    dvt_ref[...] = jnp.zeros_like(dvt_ref)
    seg_col, seg_row = segc_ref[...], segr_ref[...]
    cosine, sine_val = cos_ref[...], -sin_ref[...]
    for start in range(0, rows_all, block):
        keys = start + block
        rows = slice(start, keys)
        visible = visible_keys(seg_col, seg_row, start, block, keys)
        norms = lse_ref[0, rows, :]
        parts = []
        for kv in range(2):
            three = [3 * kv + j for j in range(3)]
            q_rows = jnp.concatenate([q_heads[h][rows] for h in three], axis=0)
            g_rows = jnp.concatenate([g_heads[h][rows] for h in three], axis=0)
            norm = jnp.concatenate([norms[:, h : h + 1] for h in three], axis=0).reshape(3, block, 1)
            scores = contract_last(q_rows, k_views[kv][:keys]).reshape(3, block, keys)
            probs = jnp.where(visible[None], jnp.exp(scores - norm), 0.0)
            prob_grad = contract_last(g_rows, v_views[kv][:keys]).reshape(3, block, keys)
            centre = jnp.sum(probs * prob_grad, axis=-1, keepdims=True)
            score_grad = (probs * (prob_grad - centre)).astype(bf16).reshape(3 * block, keys)
            probs = probs.astype(bf16).reshape(3 * block, keys)
            dq = matmul(score_grad, k_views[kv][:keys])
            parts += [dq[j * block : (j + 1) * block] for j in range(3)]
            q_across = jnp.concatenate([q_turned[h][:, rows] for h in three], axis=1)
            g_across = jnp.concatenate([g_turned[h][:, rows] for h in three], axis=1)
            dkt_ref[kv, :, :keys] += matmul(q_across, score_grad)
            dvt_ref[kv, :, :keys] += matmul(g_across, probs)
        for t in range(3):
            low, high = parts[2 * t], parts[2 * t + 1]
            low = pltpu.roll(low, HD, 1) if t == 2 else low
            high = pltpu.roll(high, HD, 1) if t == 0 else high
            turned_back = turn(low + high, cosine[rows], sine_val[rows], first[rows])
            dq_ref[rows, tile_cols[t]] = turned_back.astype(bf16)

    def joined(ref):
        return jnp.where(lane < HD, ref[0].T, ref[1].T)

    dk_ref[...] = turn(joined(dkt_ref) * score_scale, cosine, sine_val, first).astype(bf16)
    dv_ref[...] = joined(dvt_ref).astype(bf16)
    at = lambda start, wide: pl.ds(pl.multiple_of(start, LANES), wide)
    normed_turned = turned_ref[...]
    count = wgrad_ref.shape[1] // (5 * LANES)
    wgrad_ref[:, at(step * 3 * LANES, 3 * LANES)] = matmul(normed_turned, dq_ref[...]).astype(bf16)
    wgrad_ref[:, at((3 * count + step) * LANES, LANES)] = matmul(normed_turned, dk_ref[...]).astype(bf16)
    wgrad_ref[:, at((4 * count + step) * LANES, LANES)] = matmul(normed_turned, dv_ref[...]).astype(bf16)

    @pl.when(step == pl.num_programs(0) - 1)
    def _():
        copies = spread_copies(wgrad_ref, table_ref, dests, sems)
        for c in copies:
            c.start()
        for c in copies:
            c.wait()


def attend_backward(base, steps, table, turned, queries, keys, values, grads, norms, cosine, sine_val,
                    segment):
    width, rows = turned.shape
    members, layers = table.shape
    full = 5 * steps * LANES
    wide = pl.BlockSpec((rows, 3 * LANES), lambda i: (0, base + i))
    thin = pl.BlockSpec((rows, LANES), lambda i: (0, base + i))
    out_wide = pl.BlockSpec((rows, 3 * LANES), lambda i: (0, i))
    out_thin = pl.BlockSpec((rows, LANES), lambda i: (0, i))
    return pl.pallas_call(
        functools.partial(attend_back_kernel, 128, min(members, 2)),
        grid=(steps,),
        in_specs=[
            smem_spec(),
            whole_spec((width, rows)),
            wide,
            thin,
            thin,
            wide,
            pl.BlockSpec((1, rows, LANES), lambda i: (base + i, 0, 0)),
            whole_spec((rows, LANES)),
            whole_spec((rows, LANES)),
            whole_spec((rows, 1)),
            whole_spec((1, rows)),
        ],
        out_specs=[any_spec()] * min(members, 2) + [out_wide, out_thin, out_thin],
        out_shape=stack_shapes(table, width, full)
        + [jax.ShapeDtypeStruct((rows, k * LANES * steps), bf16) for k in (3, 1, 1)],
        scratch_shapes=[
            pltpu.VMEM((2, LANES, rows), f32),
            pltpu.VMEM((2, LANES, rows), f32),
            pltpu.VMEM((width, full), bf16),
            pltpu.SemaphoreType.DMA((members * layers,)),
        ],
        compiler_params=params(),
        cost_estimate=small_cost(),
    )(table, turned, queries, keys, values, grads, norms, cosine, sine_val, segment[:, None],
      segment[None, :])


def input_kernel(x_ref, mgrad_ref, w_ref, *refs):
    *grads, out_ref = refs
    x = x_ref[...].astype(f32)
    rinv = lax.rsqrt(jnp.mean(x * x, axis=-1, keepdims=True) + norm_eps)
    gain = w_ref[:, QW + 2 * KW :].astype(f32).T[GAIN_ONE : GAIN_ONE + 1, :]
    start = [0, QW, QW + KW]
    total = None
    for number, ref in enumerate(grads):
        wide = ref.shape[1]
        kind = number % 3
        product = contract_last(ref[...], w_ref[:, start[kind] : start[kind] + wide])
        start[kind] += wide
        total = product if total is None else total + product
    scaled = gain * total
    back = rinv * scaled - x * (rinv * rinv * rinv * jnp.mean(scaled * x, axis=-1, keepdims=True))
    out_ref[...] = mgrad_ref[...] + back


def to_input(hidden_in, middle_grad, w_qkv, grads):
    vmem = pl.BlockSpec(memory_space=pltpu.VMEM)
    return pl.pallas_call(
        input_kernel,
        in_specs=[vmem] * (3 + len(grads)),
        out_specs=vmem,
        out_shape=jax.ShapeDtypeStruct(hidden_in.shape, f32),
        compiler_params=params(),
        cost_estimate=small_cost(),
    )(hidden_in, middle_grad, w_qkv, *grads)


def experts_kernel(x_counts, c_counts, expert, packed, has_prev, has_sums, last, *refs):
    refs = list(refs)
    take = lambda count: [refs.pop(0) for _ in range(count)]
    (place_ref,) = take(1)
    x_src = [take(c) for c in x_counts]
    c_src = [take(c) for c in c_counts]
    weights = take(1 if packed else 3)
    prev_src = [take(2) for _ in x_counts] if has_prev else None
    sums_src = take(3) if has_sums else None
    dest = [take(2) for _ in x_counts]
    sums_dst = take(1 if packed and last else 3)
    xs, cs, og_out, og_grad = take(4)
    prevs = take(2) if has_prev else None
    acc = take(3)
    held = take(3) if packed else weights
    (staged,) = take(1) if packed and last else (None,)
    sem_in, sem_out, sem_sum, sem_w = take(4)
    i = pl.program_id(0)
    count = len(x_counts)
    width = cs.shape[2]
    hidden = acc[0].shape[1]

    def weight_loads():
        own, low = held[0].shape[2], held[2].shape[2]
        src = weights[0]
        pairs = [(src.at[:, :, pl.ds(0, own)], held[0]), (src.at[:, :, pl.ds(own, own)], held[1])]
        for third in range(width // hidden):
            pairs.append(
                (
                    src.at[:, :, pl.ds(2 * own + third * low, low)],
                    held[2].at[:, :, :, pl.ds(third * hidden, hidden)],
                )
            )
        return [pltpu.make_async_copy(a, b, sem_w.at[q]) for q, (a, b) in enumerate(pairs)]

    def loads(t):
        out = []
        slot = t % 2
        number = 0
        for srcs, dst in ((x_src[t], xs), (c_src[t], cs)):
            row = 0
            for r in srcs:
                rows = r.shape[0]
                out.append(pltpu.make_async_copy(r, dst.at[slot, pl.ds(row, rows)], sem_in.at[slot, number]))
                row += rows
                number += 1
        return out

    def prev_loads(t):
        if not has_prev:
            return []
        slot = t % 2
        return [
            pltpu.make_async_copy(r, dst.at[slot], sem_in.at[slot, 4 + q])
            for q, (r, dst) in enumerate(zip(prev_src[t], prevs))
        ]

    def sum_stores():
        if last and packed:
            return [pltpu.make_async_copy(staged, sums_dst[0], sem_sum.at[0])]
        if last:
            return []
        return [pltpu.make_async_copy(a, d, sem_sum.at[q]) for q, (a, d) in enumerate(zip(acc, sums_dst))]

    def stores(t):
        slot = t % 2
        return [
            pltpu.make_async_copy(og_out.at[slot], dest[t][0], sem_out.at[slot, 0]),
            pltpu.make_async_copy(og_grad.at[slot], dest[t][1], sem_out.at[slot, 1]),
        ]

    def sum_loads():
        return [pltpu.make_async_copy(s, a, sem_sum.at[q]) for q, (s, a) in enumerate(zip(sums_src, acc))]

    @pl.when(i == 0)
    def _():
        for c in loads(0):
            c.start()
        if packed:
            for c in weight_loads():
                c.start()
        for c in prev_loads(0):
            c.start()
        if has_sums:
            for c in sum_loads():
                c.start()
        else:
            for a in acc:
                a[...] = jnp.zeros_like(a)
        if packed:
            for c in weight_loads():
                c.wait()

    for t in range(count):
        @pl.when(i == t)
        def _(t=t):
            for c in loads(t):
                c.wait()
            if t + 1 < count:
                for c in loads(t + 1) + prev_loads(t + 1):
                    c.start()
            if t >= 2:
                for c in stores(t - 2):
                    c.wait()

    slot = lax.rem(i, 2)
    rows_in = xs[slot, :, :width]
    extra = xs[slot, :, width:].astype(f32)
    lane = lax.broadcasted_iota(jnp.int32, extra.shape, 1)
    mine = place_ref[0] * PAIR_E + expert
    gate_row = jnp.sum(jnp.where((lane < 3 * E) & (lax.rem(lane, E) == mine), extra, 0.0), axis=-1, keepdims=True)
    cot_wide = cs[slot].astype(f32)
    w_gate = held[0][...].reshape(width, hidden)
    w_up = held[1][...].reshape(width, hidden)
    w_down = held[2][...].reshape(hidden, width)
    gate_proj = matmul(rows_in, w_gate)
    up_proj = matmul(rows_in, w_up)
    sigmoid_g = 1.0 / (1.0 + jnp.exp(-gate_proj))
    active = gate_proj * sigmoid_g
    mid = (active * up_proj).astype(bf16)
    out_grad = ((resid_scale * gate_row) * cot_wide).astype(bf16)
    mid_grad = contract_last(out_grad, w_down)
    gate_grad = (mid_grad * up_proj * sigmoid_g * (1.0 + gate_proj * (1.0 - sigmoid_g))).astype(bf16)
    up_grad = (mid_grad * active).astype(bf16)
    mix = jnp.sum(mid.astype(f32) * mid_grad, axis=-1, keepdims=True)
    if has_sums:
        @pl.when(i == 0)
        def _():
            for c in sum_loads():
                c.wait()
    acc[0][...] += contract_rows(rows_in, gate_grad)
    acc[1][...] += contract_rows(rows_in, up_grad)
    acc[2][...] += contract_rows(mid, out_grad)

    @pl.when(i == count - 1)
    def _():
        if last and packed:
            layers, members, own, _ = held[0].shape
            low = held[2].shape[2]
            staged[:, :, :own] = acc[0][...].astype(bf16).reshape(layers, members, own, hidden)
            staged[:, :, own : 2 * own] = acc[1][...].astype(bf16).reshape(layers, members, own, hidden)
            for third in range(width // hidden):
                piece = acc[2][:, third * hidden : (third + 1) * hidden].astype(bf16)
                start = 2 * own + third * low
                staged[:, :, start : start + low] = piece.reshape(layers, members, low, hidden)
        elif last:
            for a, d in zip(acc, sums_dst):
                d[...] = a[...].astype(bf16)
        for c in sum_stores():
            c.start()

    if has_prev:
        for t in range(count):
            @pl.when(i == t)
            def _(t=t):
                for c in prev_loads(t):
                    c.wait()
    mixed = gate_row * matmul(mid, w_down)
    if has_prev:
        mixed = mixed + prevs[0][slot].astype(f32)
    og_out[slot] = mixed.astype(bf16)
    back = contract_last(gate_grad, w_gate) + contract_last(up_grad, w_up)
    if has_prev:
        back = back + prevs[1][slot, :, :width].astype(f32)
    og_grad[slot, :, :width] = back.astype(bf16)
    high = mix.astype(bf16).astype(f32)
    middle = (mix - high).astype(bf16).astype(f32)
    low = mix - high - middle
    spread = jnp.where(lane == mine, high, jnp.where(lane == mine + E, middle, jnp.where(lane == mine + 2 * E, low, 0.0)))
    if has_prev:
        spread = spread + prevs[1][slot, :, width:].astype(f32)
    og_grad[slot, :, width:] = spread.astype(bf16)
    for t in range(count):
        @pl.when(i == t)
        def _(t=t):
            for c in stores(t):
                c.start()

    @pl.when(i == count - 1)
    def _():
        for c in sum_stores():
            c.wait()
        for t in range(max(0, count - 2), count):
            for c in stores(t):
                c.wait()


def experts_call(place, expert, xs, cs, weights, own, prev, sums, last):
    tiles = [x if isinstance(x, (list, tuple)) else [x] for x in xs]
    cots = [c if isinstance(c, (list, tuple)) else [c] for c in cs]
    rows = sum(a.shape[0] for a in tiles[0])
    full = tiles[0][0].shape[1]
    packed = len(weights) == 1
    width, hidden = cots[0][0].shape[1], weights[0].shape[-1] if packed else weights[0].shape[1]
    anyspace = pl.BlockSpec(memory_space=pl.ANY)
    resident = lambda a: pl.BlockSpec(a.shape, lambda i: (0, 0), pipeline_mode=pl.Buffered(1))
    args, specs = [jnp.asarray(place, jnp.int32).reshape(1)], [pl.BlockSpec(memory_space=pltpu.SMEM)]
    for group in tiles + cots:
        args += group
        specs += [anyspace] * len(group)
    args += list(weights)
    specs += [anyspace] if packed else [resident(w) for w in weights]
    if prev is not None:
        for pair in prev:
            args += list(pair)
            specs += [anyspace] * 2
    if sums is not None:
        args += list(sums)
        specs += [anyspace] * 3
    shapes, out_specs = [], []
    for _ in tiles:
        shapes += [jax.ShapeDtypeStruct((rows, width), bf16), jax.ShapeDtypeStruct((rows, full), bf16)]
        out_specs += [anyspace] * 2
    sum_shapes = ((width, hidden), (width, hidden), (hidden, width))
    if packed and last:
        shapes.append(jax.ShapeDtypeStruct(weights[0].shape, bf16))
        out_specs.append(anyspace)
        sum_shapes = ()
    for shape in sum_shapes:
        shapes.append(jax.ShapeDtypeStruct(shape, bf16 if last else f32))
        out_specs.append(pl.BlockSpec(shape, lambda i: (0, 0), pipeline_mode=pl.Buffered(1)) if last else anyspace)
    scratch = [
        pltpu.VMEM((2, rows, full), bf16), pltpu.VMEM((2, rows, width), bf16),
        pltpu.VMEM((2, rows, width), bf16), pltpu.VMEM((2, rows, full), bf16),
    ]
    if prev is not None:
        scratch += [pltpu.VMEM((2, rows, width), bf16), pltpu.VMEM((2, rows, full), bf16)]
    scratch += [pltpu.VMEM((width, hidden), f32), pltpu.VMEM((width, hidden), f32), pltpu.VMEM((hidden, width), f32)]
    if packed:
        layers = weights[0].shape[0]
        low = hidden // (layers * GROUP)
        scratch += [
            pltpu.VMEM((layers, GROUP, own, hidden), bf16),
            pltpu.VMEM((layers, GROUP, own, hidden), bf16),
            pltpu.VMEM((layers, GROUP, low, width), bf16),
        ]
    if packed and last:
        scratch.append(pltpu.VMEM(weights[0].shape, bf16))
    scratch += [pltpu.SemaphoreType.DMA(shape) for shape in ((2, 6), (2, 2), (3,), (2 + width // hidden,))]
    out = pl.pallas_call(
        functools.partial(experts_kernel, [len(t) for t in tiles], [len(c) for c in cots], expert, packed,
                          prev is not None, sums is not None, last),
        grid=(len(tiles),),
        in_specs=specs,
        out_specs=out_specs,
        out_shape=shapes,
        scratch_shapes=scratch,
        compiler_params=pltpu.CompilerParams(vmem_limit_bytes=60 * 1024 * 1024),
        cost_estimate=small_cost(),
    )(*args)
    parts = [(out[2 * t], out[2 * t + 1]) for t in range(len(tiles))]
    return parts, tuple(out[2 * len(tiles) :])


def shards(device_count, hidden_in, lengths, routes, norm_attn, w_query, w_key, w_value, w_out,
           norm_moe, w_router, w_gate, w_up, w_down, cotangent):
    n = device_count
    layers = n // GROUP
    along = [[q + GROUP * j for j in range(layers)] for q in range(GROUP)]
    inside = [[GROUP * j + q for q in range(GROUP)] for j in range(layers)]
    me = lax.axis_index("fsdp")
    place, layer = me % GROUP, me // GROUP
    core = lambda value: swap(value, 1, n)
    rows, width = hidden_in.shape
    own_rows = w_query.shape[0]
    hidden = w_gate.shape[2]
    own_hidden = w_down.shape[1]
    split = own_rows % 16 == 0
    thirds = width // hidden
    members = jnp.arange(GROUP, dtype=jnp.int32) ^ place
    steps = jnp.arange(layers, dtype=jnp.int32)

    extras = jnp.concatenate(
        [w_router, norm_attn[:, None], norm_moe[:, None], jnp.zeros((own_rows, LANES - E - 2), bf16)],
        axis=1,
    )
    own_qkv = jnp.concatenate([w_query, w_key, w_value, extras], axis=1)

    down_rows = jnp.concatenate(
        [w_down[:, :, t * hidden : (t + 1) * hidden] for t in range(thirds)], axis=1
    )
    expert_rows = jnp.concatenate([w_gate, w_up, down_rows], axis=1)
    per_expert = expert_rows.shape[1]
    expert_rows = expert_rows.reshape(GROUP, PAIR_E, per_expert, hidden).transpose(1, 0, 2, 3)

    expert_rows = lax.all_to_all(expert_rows, "fsdp", 1, 1, tiled=True, axis_index_groups=inside)

    def over_all(block):
        return lax.all_gather(block, "fsdp", axis=0, axis_index_groups=along)

    aligned = own_rows % 16 == 0 and own_hidden % 16 == 0

    def expert_parts(gathered):
        if aligned:
            return (gathered,)
        gate = gathered[:, :, :own_rows].reshape(width, hidden)
        up = gathered[:, :, own_rows : 2 * own_rows].reshape(width, hidden)
        low = gathered[:, :, 2 * own_rows :].reshape(layers, GROUP, thirds, own_hidden, hidden)
        return gate, up, low.transpose(0, 1, 3, 2, 4).reshape(hidden, width)

    segment, position = layout(lengths[0], rows)
    cosine, sine_val = turn_tables(position)
    half = HK // 4
    c_low, c_high = cotangent[: rows // 2], cotangent[rows // 2 :]
    near = lambda block: (swap(block, 2, n), swap(block, 4, n))
    cores = lambda *values: [core(value) for value in values]
    if split:
        ring = list(range(layers))
        plan = [[(k, j) for j in ring] for k in range(6)]
        upper = (layers + 1) // 2
        plan += [[(k, j) for j in part] for k in (6, 7) for part in (ring[:upper], ring[upper:]) if part]
        cut = upper * own_rows
        blocks = ring_start(own_qkv, layers, n)
        column = joined_rows(ring_end(blocks, layers, n), ring)
        column, expert_rows, w_out = tie(column, expert_rows, w_out)

        def far_ways(pair):
            ways = [swap(pair[0][:cut], 4, n)]
            return ways + ([swap(pair[1][cut:], 2, n)] if layers > 1 else [])

        def in_order(own, other, near_two, far):
            return [own, other[0], near_two[0], other[1], near_two[1], other[2], *far, *cores(*far)]

        near_qkv = near(column)
        wo_blocks = ring_start(w_out, layers, n)
        near_qkv, wo_blocks, cosine, sine_val = tie(near_qkv, wo_blocks, cosine, sine_val)
        far = far_ways(near_qkv)
        other = cores(column, *near_qkv)
        other, wo_blocks = tie(other, wo_blocks)
        wo_column = joined_rows(ring_end(wo_blocks, layers, n), ring)
        far, other, wo_column = tie(far, other, wo_column)
        pieces = in_order(column, other, near_qkv, far)
        pieces, wo_column = tie(pieces, wo_column)
        wo_near, wo_other = near(wo_column), core(wo_column)
        table = own_rows * (GROUP * steps[None, :] + members[:, None])
        ring_table = own_rows * (GROUP * ((layer - steps[None, :]) % layers) + members[:, None])
    else:
        pieces = [lax.all_gather(own_qkv, "fsdp", axis=0, tiled=True)]
        plan = [[(0, 0)]]
        table = ring_table = jnp.zeros((1, 1), jnp.int32)
    table, ring_table = table.astype(jnp.int32), ring_table.astype(jnp.int32)

    gathered_first, gathered_second = over_all(expert_rows[0]), over_all(expert_rows[1])
    c_own = cores(c_low, c_high)
    w_qkv, normed, turned, *first_half = attend_forward(
        0, half, ring_table, plan, pieces, hidden_in, cosine, sine_val, segment
    )
    normed, c_low, c_own = tie(normed, c_low, c_own)
    if split:
        wo_near, wo_other, normed = tie(wo_near, wo_other, normed)
        wo_far = far_ways(wo_near)
    c_near_low = near(c_low)
    second_half = attend_forward(half, half, table, None, w_qkv, normed, cosine, sine_val, segment)
    attn_out = (first_half[3], second_half[3])
    if split:
        attn_out, c_high, wo_far, wo_near = tie(attn_out, c_high, wo_far, wo_near)
        out_pieces = in_order(wo_column, [wo_other, *cores(*wo_near)], wo_near, wo_far)
        out_pieces, c_high = tie(out_pieces, c_high)
    else:
        attn_out, c_high = tie(attn_out, c_high)
        out_pieces = [lax.all_gather(w_out, "fsdp", axis=0, tiled=True)]

    c_near_high = near(c_high)
    w_out_full, middle, inner, mix = to_middle(
        ring_table, plan, out_pieces, hidden_in, attn_out, w_qkv, routes
    )
    c_near_low, inner = tie(c_near_low, inner)
    c_core_low = cores(*c_near_low)

    def expert_sums(sums):
        if len(sums) == 1:
            return lax.psum_scatter(
                sums[0], "fsdp", scatter_dimension=0, tiled=True, axis_index_groups=along
            )[0]
        gate, up, low = sums
        low = low.reshape(layers, GROUP, own_hidden, thirds, hidden).transpose(0, 1, 3, 2, 4)
        joined = jnp.concatenate(
            [
                gate.reshape(layers, GROUP, own_rows, hidden),
                up.reshape(layers, GROUP, own_rows, hidden),
                low.reshape(layers, GROUP, thirds * own_hidden, hidden),
            ],
            axis=2,
        )
        return lax.psum_scatter(
            joined, "fsdp", scatter_dimension=0, tiled=True, axis_index_groups=along
        )[0]

    first = expert_parts(gathered_first)
    second = expert_parts(gathered_second)
    part = {}

    def run(expert, tiles, xs, cs, weights, sums, last):
        done, sums = experts_call(
            place, expert, xs, cs, weights, own_rows, [part[k] for k in tiles] if expert else None, sums, last
        )
        part.update(zip(tiles, done))
        return sums

    inner_near = gather_start(inner, n)
    inner_other = core(inner)
    inner_other, c_core_low = tie(inner_other, c_core_low)
    x_own, c_own = [[inner], [inner_other]], [[cotangent], c_own]
    sums = run(0, [0, 1], x_own, c_own, first, None, False)
    inner_near, c_near_high, sums = tie(inner_near, c_near_high, sums)
    c_core_high = cores(*c_near_high)
    inner_far = gather_far(*inner_near, n)
    cots_far = swap(c_near_low[0], 4, n), swap(c_near_high[1], 2, n)
    x_near = [[inner_near[0]], [core(inner_near[0])], [inner_near[1]], [core(inner_near[1])]]
    c_near = []
    for q in (0, 1):
        c_near += [[c_near_low[q], c_near_high[q]], [c_core_low[q], c_core_high[q]]]
    sums = run(0, [2, 3, 4, 5], x_near, c_near, first, sums, False)
    inner_far, cots_far = after((inner_far, cots_far), sums)
    x_far = [list(inner_far), [core(v) for v in inner_far]]
    c_far = [list(cots_far), [core(v) for v in cots_far]]
    sums0 = run(0, [6, 7], x_far, c_far, first, sums, True)
    shared0 = expert_sums(sums0)

    sums = run(1, [6, 7], x_far, c_far, second, None, False)
    both_ways = lambda low, high: (swap(low, 4, n), swap(high, 2, n))
    halves, out_halves = sums_for_far([(part[6][i], core(part[7][i])) for i in (1, 0)])
    x_near[0], halves, out_halves = tie(x_near[0], halves, out_halves)
    far_sums, out_far = both_ways(*halves), both_ways(*out_halves)
    sums = run(1, [2, 3, 4, 5], x_near, c_near, second, sums, False)
    done = [part[k] for k in (2, 3, 4, 5)]
    far_sums, out_far, sums, done = tie(far_sums, out_far, sums, done)
    part.update(zip((2, 3, 4, 5), done))
    near_sums = sums_for_near(part[2][1], core(part[3][1]), part[4][1], core(part[5][1]), *far_sums)
    x_own[0], near_sums, shared0 = tie(x_own[0], near_sums, shared0)
    ways = lambda two, four: [swap(two, 2, n), swap(four, 4, n)]
    inner_near = ways(*near_sums)
    out_core = [core(part[3][0]), core(part[5][0])]
    sums = run(1, [0, 1], x_own, c_own, second, sums, True)
    inner_near, out_core, sums, part[0], part[1] = tie(inner_near, out_core, sums, part[0], part[1])
    shared1 = expert_sums(sums)
    inner_other = core(part[1][1])
    out_blocks = (part[2][0], out_core[0], part[4][0], out_core[1])
    out_sums = half_for_near(0, *out_blocks, out_far[0])
    out_sums, inner_other = tie(out_sums, inner_other)
    out_low = ways(*out_sums)
    out_other = core(part[1][0])
    *out_grads, middle_grad, attn_grad0, attn_grad1 = middle_back(
        table, (part[0][1], inner_other, *inner_near), inner, mix, middle, cotangent, w_qkv, attn_out,
        w_out_full,
    )
    out_low, out_other, out_grads, middle_grad, attn_grad0, attn_grad1 = tie(
        out_low, out_other, out_grads, middle_grad, attn_grad0, attn_grad1
    )

    wide = lambda value: value.astype(f32)

    def chips_of(stacks):
        return sums_of_stack(stacks[0], core(stacks[1])) if split else [stacks[0]]

    def far_of(chips):
        return both_ways(*chips[3:]) if split else ()

    def near_of(*sets):
        if not split:
            return ()
        sum2, sum4 = stack_near([(*chips[1:3], *far) for chips, far in sets])
        return swap(sum2, 2, n), swap(sum4, 4, n)

    def back(base, steps, half_set, grads):
        return attend_backward(
            base, steps, table, turned, *half_set[:3], grads, half_set[4], cosine, sine_val, segment
        )

    wo_chips = chips_of(out_grads)
    out_sums = half_for_near(1, *tie(*out_blocks, middle_grad)[:4], out_far[1])
    attn_grad0, wo_chips, out_sums = tie(attn_grad0, wo_chips, out_sums)
    out_high = ways(*out_sums)
    wo_far = far_of(wo_chips)
    *stacks0, dq0, dk0, dv0 = back(0, half, first_half, attn_grad0)
    out_high, wo_far, stacks0, dq0, dk0, dv0 = tie(out_high, wo_far, stacks0, dq0, dk0, dv0)

    chips0 = chips_of(stacks0)
    attn_grad1, chips0 = tie(attn_grad1, chips0)
    wo_near, far0 = near_of((wo_chips, wo_far)), far_of(chips0)
    *stacks1, dq1, dk1, dv1 = back(0, half, second_half, attn_grad1)
    wo_near, far0, stacks1, dq1, dk1, dv1, shared1 = tie(wo_near, far0, stacks1, dq1, dk1, dv1, shared1)

    def to_owner(block):
        return lax.all_to_all(block, "fsdp", 0, 0, tiled=True, axis_index_groups=inside)

    def summed(group, near_sums):
        own = jnp.concatenate([chips[0] for chips in group], axis=1)
        return (wide(own) + wide(near_sums[0]) + wide(near_sums[1])).astype(bf16)

    chips1 = chips_of(stacks1)
    dq1, chips1 = tie(dq1, chips1)
    near0, far1 = near_of((chips0, far0)), far_of(chips1)
    if split:
        wo_shared = lax.psum_scatter(
            summed([wo_chips], wo_near), "fsdp", scatter_dimension=0, tiled=True, axis_index_groups=along
        )
    else:
        wo_shared = lax.psum_scatter(wo_chips[0], "fsdp", scatter_dimension=0, tiled=True)
    input_grad = to_input(hidden_in, middle_grad, w_qkv, (dq0, dk0, dv0, dq1, dk1, dv1))
    near0, far1, input_grad = tie(near0, far1, input_grad)
    near1 = near_of((chips1, far1))
    owned = to_owner(jnp.stack([shared0, after(shared1, near1)], axis=1))
    out_low, near1, wo_shared = tie(out_low, near1, wo_shared)
    mine_out = wide(wo_shared)
    out_total = wide(part[0][0]) + wide(out_other) + jnp.concatenate(
        [wide(out_low[0]) + wide(out_low[1]), wide(out_high[0]) + wide(out_high[1])], axis=0
    )
    mixed = (middle + resid_scale * out_total).astype(bf16)
    if split:
        total = jnp.concatenate([summed([chips0], near0), summed([chips1], near1)], axis=1)
        late, owned = tie(layer_start(total.reshape(layers, own_rows, -1), layer, layers, n), owned)
        late = layer_add(late)
    else:
        late = jnp.concatenate(
            [
                wide(lax.psum_scatter(chips[0], "fsdp", scatter_dimension=0, tiled=True))
                for chips in (chips0, chips1)
            ],
            axis=1,
        )
    unit = chips0[0].shape[1]
    mine = [late[:, :unit], late[:, unit:]]

    shared = owned.reshape(E, per_expert, hidden).astype(f32)
    grad_gate, grad_up = shared[:, :own_rows], shared[:, own_rows : 2 * own_rows]
    grad_down = jnp.concatenate(
        [
            shared[:, 2 * own_rows + t * own_hidden : 2 * own_rows + (t + 1) * own_hidden]
            for t in range(thirds)
        ],
        axis=2,
    )
    def joined(kind):
        pieces = []
        for part_grads in mine:
            unit = part_grads.shape[1] // 5
            start, wide = ((0, 3 * unit), (3 * unit, unit), (4 * unit, unit))[kind]
            pieces.append(part_grads[:, start : start + wide])
        return jnp.concatenate(pieces, axis=1)

    grad_query, grad_key, grad_value = joined(0), joined(1), joined(2)
    grad_router = mine_out[:, width : width + E]

    def row_sums(weight, grad):
        return jnp.sum(weight.astype(f32) * grad, axis=-1)

    grad_norm_attn = (
        row_sums(w_query, grad_query) + row_sums(w_key, grad_key) + row_sums(w_value, grad_value)
    ) / norm_attn.astype(f32)
    grad_norm_moe = (
        jnp.sum(row_sums(w_gate, grad_gate) + row_sums(w_up, grad_up), axis=0)
        + row_sums(w_router, grad_router)
    ) / norm_moe.astype(f32)
    return (
        mixed,
        input_grad,
        grad_norm_attn,
        grad_query,
        grad_key,
        grad_value,
        mine_out[:, :width],
        grad_norm_moe,
        grad_router,
        grad_gate,
        grad_up,
        grad_down,
    )


def solution(mesh):

    in_specs = (
        P("fsdp", None),
        P("fsdp", None),
        P("fsdp", None),
        P("fsdp"),
        P("fsdp", None),
        P("fsdp", None),
        P("fsdp", None),
        P("fsdp", None),
        P("fsdp"),
        P("fsdp", None),
        P(None, "fsdp", None),
        P(None, "fsdp", None),
        P(None, "fsdp", None),
        P("fsdp", None),
    )
    out_specs = (
        P("fsdp", None),
        P("fsdp", None),
        P("fsdp"),
        P("fsdp", None),
        P("fsdp", None),
        P("fsdp", None),
        P("fsdp", None),
        P("fsdp"),
        P("fsdp", None),
        P(None, "fsdp", None),
        P(None, "fsdp", None),
        P(None, "fsdp", None),
    )
    return jax.shard_map(
        functools.partial(shards, mesh.shape["fsdp"]),
        mesh=mesh,
        in_specs=in_specs,
        out_specs=out_specs,
        check_vma=False,
    )
```

```python
import functools
import math

import jax
import jax.numpy as jnp
from jax import lax
from jax.experimental import pallas as pl
from jax.experimental.pallas import tpu as pltpu
from jax.sharding import PartitionSpec as P

HQ = 24
HK = 8
HD = 64
E = 16
GROUP = 8
PAIR_E = E // GROUP
HEADS_STEP = 2 * HQ // HK
LANES = 128
ROW_TILES = 2
QW = HQ * HD
KW = HK * HD
QKV_WIDE = QW + 2 * KW + LANES
GAIN_ONE = E
GAIN_TWO = E + 1
VMEM_LIMIT = 58 * 1024 * 1024

norm_eps = 1e-06
resid_scale = 0.22
score_scale = 0.015625
rope_base = 10000.0
masked_score = -1e30

f32 = jnp.float32
bf16 = jnp.bfloat16


def matmul(left, right):
    return jnp.dot(left, right, preferred_element_type=f32)


def contract_rows(left, right):
    return lax.dot_general(left, right, (((0,), (0,)), ((), ())), preferred_element_type=f32)


def contract_last(left, right):
    return lax.dot_general(left, right, (((1,), (1,)), ((), ())), preferred_element_type=f32)


def layout(seq_lengths, row_count):
    seq_ends = jnp.cumsum(seq_lengths)
    starts = seq_ends - seq_lengths
    places = jnp.arange(row_count, dtype=jnp.int32)
    member = (places[:, None] >= starts[None, :]) & (places[:, None] < seq_ends[None, :])
    labels = jnp.arange(seq_lengths.shape[0], dtype=jnp.int32)
    segment = jnp.sum(jnp.where(member, labels[None, :], 0), axis=1)
    offset = jnp.sum(jnp.where(member, starts[None, :], 0), axis=1)
    return (segment, places - offset)


def turn_tables(position):
    half_dim = HD // 2
    inv_freq = jnp.exp(
        -(jnp.arange(half_dim, dtype=f32) * (2.0 / HD)) * math.log(rope_base)
    )
    angles = position.astype(f32)[:, None] * inv_freq[None, :]
    cosine, sine_val = jnp.cos(angles), jnp.sin(angles)
    return (
        jnp.concatenate([cosine] * 4, axis=1),
        jnp.concatenate([-sine_val, sine_val] * 2, axis=1),
    )


def swap(value, bit, device_count):
    return lax.ppermute(value, "fsdp", [(i, i ^ bit) for i in range(device_count)])


def shift(value, steps, device_count):
    moved = [(i, (i + GROUP * steps) % device_count) for i in range(device_count)]
    return lax.ppermute(value, "fsdp", moved)


def after(value, *needed):
    return lax.optimization_barrier((value, needed))[0]


def tie(*values):
    return lax.optimization_barrier(values)


def ring_start(own, layers, device_count):
    blocks = {0: own}
    ahead, behind = own, own
    for step in range(1, (layers - 1) // 2 + 1):
        ahead, behind = shift(ahead, 1, device_count), shift(behind, -1, device_count)
        blocks[step], blocks[layers - step] = ahead, behind
    return blocks


def ring_end(blocks, layers, device_count):
    if layers % 2 == 0:
        ahead, behind = blocks[layers // 2 - 1], blocks[(layers // 2 + 1) % layers]
        half = ahead.shape[1] // 2 // LANES * LANES
        blocks[layers // 2] = jnp.concatenate(
            [shift(ahead[:, :half], 1, device_count), shift(behind[:, half:], -1, device_count)], axis=1
        )
    return blocks


def joined_rows(blocks, places):
    return jnp.concatenate([blocks[j] for j in places], axis=0)


def gather_start(own, device_count):
    return swap(own, 2, device_count), swap(own, 4, device_count)


def gather_far(from2, from4, device_count):
    half = from2.shape[0] // 2
    return swap(from2[:half], 4, device_count), swap(from4[half:], 2, device_count)


def gather_cores(own, near, far, device_count):
    other = lambda value: swap(value, 1, device_count)
    return [
        [own], [other(own)], [near[0]], [other(near[0])], [near[1]], [other(near[1])],
        list(far), [other(far[0]), other(far[1])],
    ]


def layer_start(stacked, layer, layers, device_count):
    pick = lambda at: lax.dynamic_index_in_dim(stacked, at % layers, 0, keepdims=False)
    return [pick(layer)] + [shift(pick(layer + k), k, device_count) for k in range(1, layers)]


def layer_add(blocks):
    total = blocks[0].astype(f32)
    for block in blocks[1:]:
        total = total + block.astype(f32)
    return total


def turn(values, cosine, sine_val, low_half):
    shifted = jnp.where(low_half, pltpu.roll(values, LANES - 32, 1), pltpu.roll(values, 32, 1))
    return values * cosine + shifted * sine_val


def half_views(pair, scale):
    lane = lax.broadcasted_iota(jnp.int32, pair.shape, 1)
    scaled = pair.astype(f32) * scale
    low = lane < HD
    return jnp.where(low, scaled, 0.0).astype(bf16), jnp.where(low, 0.0, scaled).astype(bf16)


def head_tiles(tiles):
    return [
        tiles[head // 2] if head % 2 == head // 3 else pltpu.roll(tiles[head // 2], HD, 1)
        for head in range(HEADS_STEP)
    ]


def visible_keys(seg_col, seg_row, row_start, rows, keys):
    query_at = row_start + lax.broadcasted_iota(jnp.int32, (rows, keys), 0)
    key_at = lax.broadcasted_iota(jnp.int32, (rows, keys), 1)
    return (seg_col[row_start : row_start + rows, :] == seg_row[:, :keys]) & (key_at <= query_at)


def any_spec():
    return pl.BlockSpec(memory_space=pl.ANY)


def smem_spec():
    return pl.BlockSpec(memory_space=pltpu.SMEM)


def small_cost():
    return pl.CostEstimate(flops=1_000_000, bytes_accessed=100_000, transcendentals=0)


def extras_spec(width):
    return pl.BlockSpec((width, LANES), lambda *_: (0, (QW + 2 * KW) // LANES))


def params():
    return pltpu.CompilerParams(vmem_limit_bytes=VMEM_LIMIT)


def whole_spec(shape):
    zeros = (0,) * len(shape)
    return pl.BlockSpec(shape, lambda *_: zeros, pipeline_mode=pl.Buffered(1))


def gather_copies(plan, refs, table_ref, dst, sems):
    copies = []
    for ref, runs in zip(refs, plan):
        rows = ref.shape[0] // len(runs)
        for number, (member, step) in enumerate(runs):
            start = pl.multiple_of(table_ref[member, step], 16)
            copies.append(
                pltpu.make_async_copy(
                    ref.at[pl.ds(number * rows, rows)],
                    dst.at[pl.ds(start, rows)],
                    sems.at[len(copies)],
                )
            )
    return copies


def spread_copies(src, table_ref, refs, sems):
    copies = []
    members, blocks = table_ref.shape
    rows = src.shape[0] // (members * blocks)
    for member in range(members):
        for block in range(blocks):
            start = pl.multiple_of(table_ref[member, block], 16)
            to = (member // 2 * blocks + block) * rows
            copies.append(
                pltpu.make_async_copy(
                    src.at[pl.ds(start, rows)], refs[member % 2].at[pl.ds(to, rows)], sems.at[len(copies)]
                )
            )
    return copies


def stack_shapes(table, width, full):
    members = table.shape[0]
    stacks = min(members, 2)
    return [jax.ShapeDtypeStruct((width // stacks, full), bf16)] * stacks


def far_kernel(*refs):
    count = len(refs) // 4
    for q in range(count):
        left, right = refs[2 * q : 2 * q + 2]
        low, high = refs[2 * count + 2 * q : 2 * count + 2 * q + 2]
        total = (left[...].astype(f32) + right[...].astype(f32)).astype(bf16)
        low[...] = total[0]
        high[...] = total[1]


def sums_for_far(pairs):
    rows = pairs[0][0].shape[0]
    tile = rows // 8
    args, in_specs, out_specs, shapes = [], [], [], []
    for pair in pairs:
        width = pair[0].shape[1]
        args += [value.reshape(2, rows // 2, width) for value in pair]
        in_specs += [pl.BlockSpec((2, tile, width), lambda i: (0, i, 0))] * 2
        out_specs += [pl.BlockSpec((tile, width), lambda i: (i, 0))] * 2
        shapes += [jax.ShapeDtypeStruct((rows // 2, width), bf16)] * 2
    out = pl.pallas_call(
        far_kernel, grid=(4,), in_specs=in_specs, out_specs=out_specs, out_shape=shapes,
        compiler_params=params(), cost_estimate=small_cost(),
    )(*args)
    return [out[2 * q : 2 * q + 2] for q in range(len(pairs))]


def near_kernel(a2_ref, b2_ref, a4_ref, b4_ref, low_ref, high_ref, sum2_ref, sum4_ref):
    two = a2_ref[...].astype(f32) + b2_ref[...].astype(f32)
    four = a4_ref[...].astype(f32) + b4_ref[...].astype(f32)
    sum2_ref[0] = (two[0] + low_ref[...].astype(f32)).astype(bf16)
    sum2_ref[1] = two[1].astype(bf16)
    sum4_ref[0] = four[0].astype(bf16)
    sum4_ref[1] = (four[1] + high_ref[...].astype(f32)).astype(bf16)


def sums_for_near(a2, b2, a4, b4, low, high):
    rows, width = a2.shape
    tile = rows // 8
    pair = pl.BlockSpec((2, tile, width), lambda i: (0, i, 0))
    single = pl.BlockSpec((tile, width), lambda i: (i, 0))
    out = pl.pallas_call(
        near_kernel, grid=(4,), in_specs=[pair] * 4 + [single] * 2, out_specs=[pair] * 2,
        out_shape=[jax.ShapeDtypeStruct((2, rows // 2, width), bf16)] * 2,
        compiler_params=params(), cost_estimate=small_cost(),
    )(*[value.reshape(2, rows // 2, width) for value in (a2, b2, a4, b4)], low, high)
    return [value.reshape(rows, width) for value in out]


def half_kernel(more_for, a2_ref, b2_ref, a4_ref, b4_ref, more_ref, sum2_ref, sum4_ref):
    two = a2_ref[...].astype(f32) + b2_ref[...].astype(f32)
    four = a4_ref[...].astype(f32) + b4_ref[...].astype(f32)
    more = more_ref[...].astype(f32)
    sum2_ref[...] = (two + more if more_for == 2 else two).astype(bf16)
    sum4_ref[...] = (four + more if more_for == 4 else four).astype(bf16)


def half_for_near(which, a2, b2, a4, b4, more):
    rows, width = a2.shape
    tile = rows // 8
    picked = pl.BlockSpec((tile, width), lambda i: (4 * which + i, 0))
    single = pl.BlockSpec((tile, width), lambda i: (i, 0))
    return pl.pallas_call(
        functools.partial(half_kernel, (2, 4)[which]), grid=(4,), in_specs=[picked] * 4 + [single],
        out_specs=[single] * 2, out_shape=[jax.ShapeDtypeStruct((rows // 2, width), bf16)] * 2,
        compiler_params=params(), cost_estimate=small_cost(),
    )(a2, b2, a4, b4, more)


def stack_kernel(even_ref, odd_ref, own_ref, two_ref, four_ref, low_ref, high_ref):
    rows = own_ref.shape[0]
    half = rows // 2
    spots = ((own_ref, 0, rows), (two_ref, rows, rows), (four_ref, 2 * rows, rows), (low_ref, 3 * rows, half),
             (high_ref, 3 * rows + half, half))
    for ref, start, count in spots:
        at = slice(start, start + count)
        ref[...] = (even_ref[at].astype(f32) + odd_ref[at].astype(f32)).astype(bf16)


def sums_of_stack(even, odd):
    rows, width = even.shape[0] // 4, even.shape[1]
    vmem = pl.BlockSpec(memory_space=pltpu.VMEM)
    return pl.pallas_call(
        stack_kernel, in_specs=[vmem] * 2, out_specs=[vmem] * 5,
        out_shape=[jax.ShapeDtypeStruct((r, width), bf16) for r in (rows, rows, rows, rows // 2, rows // 2)],
        compiler_params=params(), cost_estimate=small_cost(),
    )(even, odd)


def stack_near_kernel(*refs):
    *sources, sum2_ref, sum4_ref = refs
    start = 0
    for q in range(0, len(sources), 4):
        two_ref, four_ref, low_ref, high_ref = sources[q : q + 4]
        half = low_ref.shape[0]
        at = slice(start, start + two_ref.shape[1])
        sum2_ref[:half, at] = (two_ref[:half].astype(f32) + low_ref[...].astype(f32)).astype(bf16)
        sum2_ref[half:, at] = two_ref[half:]
        sum4_ref[:half, at] = four_ref[:half]
        sum4_ref[half:, at] = (four_ref[half:].astype(f32) + high_ref[...].astype(f32)).astype(bf16)
        start += two_ref.shape[1]


def stack_near(sets):
    vmem = pl.BlockSpec(memory_space=pltpu.VMEM)
    shape = (sets[0][0].shape[0], sum(one[0].shape[1] for one in sets))
    return pl.pallas_call(
        stack_near_kernel, in_specs=[vmem] * (4 * len(sets)), out_specs=[vmem] * 2,
        out_shape=[jax.ShapeDtypeStruct(shape, bf16)] * 2,
        compiler_params=params(), cost_estimate=small_cost(),
    )(*[value for one in sets for value in one])


def attend_kernel(block, plan, table_ref, x_ref, cos_ref, sin_ref, segc_ref, segr_ref, *refs):
    pair = pl.program_id(0)
    rows_all, width = x_ref.shape
    at = lambda start, wide: pl.ds(pl.multiple_of(start, LANES), wide)
    if plan is None:
        wq_ref, wk_ref, wv_ref, q_ref, k_ref, v_ref, out_ref, lse_ref = refs
        normed_ref = x_ref
        w_q, w_k, w_v = wq_ref[...], wk_ref[...], wv_ref[...]
    else:
        sources = refs[: len(plan)]
        (w_out_ref, normed_ref, turned_ref, q_ref, k_ref, v_ref, out_ref, lse_ref,
         w_ref, sems, save_sem) = refs[len(plan) :]

        @pl.when(pair == 0)
        def _():
            copies = gather_copies(plan, sources, table_ref, w_ref, sems)
            for c in copies:
                c.start()
            x = x_ref[...].astype(f32)
            rinv = lax.rsqrt(jnp.mean(x * x, axis=-1, keepdims=True) + norm_eps)
            for c in copies:
                c.wait()
            pltpu.make_async_copy(w_ref, w_out_ref, save_sem).start()
            gains = w_ref[:, QW + 2 * KW :].astype(f32).T
            scaled = x * rinv * gains[GAIN_ONE : GAIN_ONE + 1, :]
            normed_ref[...] = scaled.astype(bf16)
            turned_ref[...] = scaled.T.astype(bf16)

        w_q = w_ref[:, at(pair * 3 * LANES, 3 * LANES)]
        w_k = w_ref[:, at(QW + pair * LANES, LANES)]
        w_v = w_ref[:, at(QW + KW + pair * LANES, LANES)]

    normed = normed_ref[...]
    lane = lax.broadcasted_iota(jnp.int32, (rows_all, LANES), 1)
    first = (lane % HD) < (HD // 2)
    cosine, sine_val = cos_ref[...], sin_ref[...]
    q_pre = matmul(normed, w_q)
    tiles = []
    for t in range(3):
        cols = slice(t * LANES, (t + 1) * LANES)
        tiles.append(turn(q_pre[:, cols], cosine, sine_val, first))
        q_ref[:, cols] = tiles[t].astype(bf16)
    heads = [tile.astype(bf16) for tile in head_tiles(tiles)]
    k_low = turn(matmul(normed, w_k), cosine, sine_val, first).astype(bf16)
    v_low = matmul(normed, w_v).astype(bf16)
    k_ref[...] = k_low
    v_ref[...] = v_low
    k_views = half_views(k_low, score_scale)
    v_views = half_views(v_low, 1.0)
    seg_col, seg_row = segc_ref[...], segr_ref[...]
    lane_b = lax.broadcasted_iota(jnp.int32, (block, LANES), 1)
    for start in range(0, rows_all, block):
        keys = start + block
        rows = slice(start, keys)
        visible = visible_keys(seg_col, seg_row, start, block, keys)
        norms = jnp.zeros((block, LANES), f32)
        outs = []
        for kv in range(2):
            q_rows = jnp.concatenate([heads[3 * kv + j][rows] for j in range(3)], axis=0)
            scores = contract_last(q_rows, k_views[kv][:keys]).reshape(3, block, keys)
            scores = jnp.where(visible[None], scores, masked_score)
            peak = jnp.max(scores, axis=-1, keepdims=True)
            expo = jnp.exp(scores - peak)
            mass = jnp.sum(expo, axis=-1, keepdims=True)
            probs = (expo * (1.0 / mass)).astype(bf16)
            total = matmul(probs.reshape(3 * block, keys), v_views[kv][:keys])
            norm = peak + jnp.log(mass)
            for j in range(3):
                outs.append(total[j * block : (j + 1) * block])
                norms = jnp.where(lane_b == 3 * kv + j, norm[j], norms)
        for t in range(3):
            low, high = outs[2 * t], outs[2 * t + 1]
            low = pltpu.roll(low, HD, 1) if t == 2 else low
            high = pltpu.roll(high, HD, 1) if t == 0 else high
            out_ref[rows, t * LANES : (t + 1) * LANES] = (low + high).astype(bf16)
        lse_ref[0, rows, :] = norms

    if plan is not None:
        @pl.when(pair == pl.num_programs(0) - 1)
        def _():
            pltpu.make_async_copy(w_ref, w_out_ref, save_sem).wait()


def attend_forward(base, steps, table, plan, weights, rows_in, cosine, sine_val, segment):
    rows, width = rows_in.shape
    wide = pl.BlockSpec((rows, 3 * LANES), lambda i: (0, i))
    thin = pl.BlockSpec((rows, LANES), lambda i: (0, i))
    in_specs = [
        smem_spec(),
        whole_spec((rows, width)),
        whole_spec((rows, LANES)),
        whole_spec((rows, LANES)),
        whole_spec((rows, 1)),
        whole_spec((1, rows)),
    ]
    out_specs = [wide, thin, thin, wide, pl.BlockSpec((1, rows, LANES), lambda i: (i, 0, 0))]
    out_shape = [
        jax.ShapeDtypeStruct((rows, 3 * LANES * steps), bf16),
        jax.ShapeDtypeStruct((rows, LANES * steps), bf16),
        jax.ShapeDtypeStruct((rows, LANES * steps), bf16),
        jax.ShapeDtypeStruct((rows, 3 * LANES * steps), bf16),
        jax.ShapeDtypeStruct((steps, rows, LANES), f32),
    ]
    if plan is None:
        in_specs += [
            pl.BlockSpec((width, 3 * LANES), lambda i: (0, base + i)),
            pl.BlockSpec((width, LANES), lambda i: (0, QW // LANES + base + i)),
            pl.BlockSpec((width, LANES), lambda i: (0, (QW + KW) // LANES + base + i)),
        ]
        weights = [weights] * 3
        scratch = []
    else:
        in_specs += [any_spec()] * len(weights)
        out_specs = [any_spec(), whole_spec((rows, width)), whole_spec((width, rows))] + out_specs
        out_shape = [
            jax.ShapeDtypeStruct((width, QKV_WIDE), bf16),
            jax.ShapeDtypeStruct((rows, width), bf16),
            jax.ShapeDtypeStruct((width, rows), bf16),
        ] + out_shape
        scratch = [
            pltpu.VMEM((width, QKV_WIDE), bf16),
            pltpu.SemaphoreType.DMA((sum(len(r) for r in plan),)),
            pltpu.SemaphoreType.DMA(()),
        ]
    return pl.pallas_call(
        functools.partial(attend_kernel, 128, plan),
        grid=(steps,),
        in_specs=in_specs,
        out_specs=out_specs,
        out_shape=out_shape,
        scratch_shapes=scratch,
        compiler_params=params(),
        cost_estimate=small_cost(),
    )(table, rows_in, cosine, sine_val, segment[:, None], segment[None, :], *weights)


def middle_kernel(plan, table_ref, x_ref, attn0_ref, attn1_ref, extras_ref, routes_ref, *refs):
    sources = refs[: len(plan)]
    w_out_ref, middle_ref, inner_ref, mix_ref, w_ref, gain_ref, sems, save_sem = refs[len(plan) :]
    step = pl.program_id(0)
    rows, width = x_ref.shape

    @pl.when(step == 0)
    def _():
        copies = gather_copies(plan, sources, table_ref, w_ref, sems)
        for c in copies:
            c.start()
        gain_ref[...] = extras_ref[...].astype(f32).T[GAIN_TWO : GAIN_TWO + 1, :]
        for c in copies:
            c.wait()
        pltpu.make_async_copy(w_ref, w_out_ref, save_sem).start()

    extras = extras_ref[...]
    half = attn0_ref.shape[1]
    product = matmul(attn0_ref[...], w_ref[:half]) + matmul(attn1_ref[...], w_ref[half:])
    middle = x_ref[...].astype(f32) + resid_scale * product
    middle_ref[...] = middle
    rinv = lax.rsqrt(jnp.mean(middle * middle, axis=-1, keepdims=True) + norm_eps)
    inner = (middle * rinv * gain_ref[...]).astype(bf16)
    inner_ref[:, :width] = inner
    logits = matmul(inner, extras)
    lane = lax.broadcasted_iota(jnp.int32, logits.shape, 1)
    routes = routes_ref[...]
    named = lane == routes[:, 0:1]
    for k in range(1, routes.shape[1]):
        named = named | (lane == routes[:, k : k + 1])
    chosen = jnp.where(named, logits, masked_score)
    peak = jnp.max(chosen, axis=-1, keepdims=True)
    expo = jnp.where(named, jnp.exp(chosen - peak), 0.0)
    mix = expo / jnp.sum(expo, axis=-1, keepdims=True)
    mix_ref[...] = mix
    high = mix.astype(bf16).astype(f32)
    rest = (mix - high).astype(bf16).astype(f32)
    low = mix - high - rest
    spread = high + pltpu.roll(rest, E, 1) + pltpu.roll(low, 2 * E, 1)
    inner_ref[:, width:] = spread.astype(bf16)

    @pl.when(step == pl.num_programs(0) - 1)
    def _():
        pltpu.make_async_copy(w_ref, w_out_ref, save_sem).wait()


def to_middle(table, plan, pieces, hidden_in, attn_out, extras, routes):
    rows, width = hidden_in.shape
    tall = functools.partial(row_tiles, rows)
    return pl.pallas_call(
        functools.partial(middle_kernel, plan),
        grid=(ROW_TILES,),
        in_specs=[smem_spec(), tall(width), tall(QW // 2), tall(QW // 2), extras_spec(width)]
        + [tall(routes.shape[1])]
        + [any_spec()] * len(pieces),
        out_specs=[any_spec(), tall(width), tall(width + LANES), tall(LANES)],
        out_shape=[
            jax.ShapeDtypeStruct((QW, width), bf16),
            jax.ShapeDtypeStruct((rows, width), f32),
            jax.ShapeDtypeStruct((rows, width + LANES), bf16),
            jax.ShapeDtypeStruct((rows, LANES), f32),
        ],
        scratch_shapes=[
            pltpu.VMEM((QW, width), bf16),
            pltpu.VMEM((1, width), f32),
            pltpu.SemaphoreType.DMA((sum(len(r) for r in plan),)),
            pltpu.SemaphoreType.DMA(()),
        ],
        compiler_params=params(),
        cost_estimate=small_cost(),
    )(table, hidden_in, *attn_out, extras, routes, *pieces)


def middle_back_kernel(blocks, table_ref, own0_ref, own1_ref, near2_ref, near4_ref, inner_ref, mix_ref, middle_ref,
                       cot_ref, extras_ref, attn0_src, attn1_src, w_src, *refs):
    dests = refs[:blocks]
    (grad_ref, attn_grad0_ref, attn_grad1_ref, wgrad_ref, attn0_ref, attn1_ref, w_ref, sems,
     load_sems) = refs[blocks:]
    rows, width = middle_ref.shape
    loads = [
        pltpu.make_async_copy(a, b, load_sems.at[q])
        for q, (a, b) in enumerate(((w_src, w_ref), (attn0_src, attn0_ref), (attn1_src, attn1_ref)))
    ]
    for c in loads:
        c.start()
    total = own0_ref[...].astype(f32) + own1_ref[...].astype(f32)
    total = total + near2_ref[...].astype(f32) + near4_ref[...].astype(f32)
    inner_grad, tail = total[:, :width], total[:, width:]
    lane = lax.broadcasted_iota(jnp.int32, tail.shape, 1)
    mix = mix_ref[...]
    mix_grad = tail + pltpu.roll(tail, LANES - E, 1) + pltpu.roll(tail, LANES - 2 * E, 1)
    mix_grad = jnp.where(lane < E, mix_grad, 0.0)
    logit_grad = mix_grad - mix * jnp.sum(mix_grad, axis=-1, keepdims=True)
    logit_grad = logit_grad.astype(bf16)
    extras = extras_ref[...]
    gain = extras.astype(f32).T[GAIN_TWO : GAIN_TWO + 1, :]
    inner_grad = inner_grad + contract_last(logit_grad, extras)
    middle = middle_ref[...]
    rinv = lax.rsqrt(jnp.mean(middle * middle, axis=-1, keepdims=True) + norm_eps)
    scaled = gain * inner_grad
    back = rinv * scaled - middle * (rinv * rinv * rinv * jnp.mean(scaled * middle, axis=-1, keepdims=True))
    middle_grad = cot_ref[...].astype(f32) + back
    grad_ref[...] = middle_grad
    proj_grad = (resid_scale * middle_grad).astype(bf16)
    half = attn0_ref.shape[1]
    for c in loads:
        c.wait()
    attn_grad0_ref[...] = contract_last(proj_grad, w_ref[:half]).astype(bf16)
    attn_grad1_ref[...] = contract_last(proj_grad, w_ref[half:]).astype(bf16)
    wgrad_ref[:half, :width] = contract_rows(attn0_ref[...], proj_grad).astype(bf16)
    wgrad_ref[half:, :width] = contract_rows(attn1_ref[...], proj_grad).astype(bf16)
    wgrad_ref[:, width:] = contract_rows(inner_ref[:, :width], logit_grad).astype(bf16)
    copies = spread_copies(wgrad_ref, table_ref, dests, sems)
    for c in copies:
        c.start()
    for c in copies:
        c.wait()


def middle_back(table, sums, inner, mix, middle, cotangent, extras, attn_out, w_out):
    rows, width = middle.shape
    members, layers = table.shape
    vmem = pl.BlockSpec(memory_space=pltpu.VMEM)
    full = width + LANES
    return pl.pallas_call(
        functools.partial(middle_back_kernel, min(members, 2)),
        grid=(1,),
        in_specs=[smem_spec()] + [vmem] * 8 + [extras_spec(width)] + [any_spec()] * 3,
        out_specs=[any_spec()] * min(members, 2) + [vmem] * 3,
        out_shape=stack_shapes(table, width, full)
        + [jax.ShapeDtypeStruct((rows, width), f32)]
        + [jax.ShapeDtypeStruct((rows, QW // 2), bf16)] * 2,
        scratch_shapes=[
            pltpu.VMEM((width, full), bf16),
            pltpu.VMEM((rows, QW // 2), bf16),
            pltpu.VMEM((rows, QW // 2), bf16),
            pltpu.VMEM(w_out.shape, bf16),
            pltpu.SemaphoreType.DMA((members * layers,)),
            pltpu.SemaphoreType.DMA((3,)),
        ],
        compiler_params=params(),
        cost_estimate=small_cost(),
    )(table, *sums, inner, mix, middle, cotangent, extras, *attn_out, w_out)


def attend_back_kernel(block, blocks, table_ref, turned_ref, q_ref, k_ref, v_ref, grad_ref, lse_ref,
                       cos_ref, sin_ref, segc_ref, segr_ref, *refs):
    dests = refs[:blocks]
    dq_ref, dk_ref, dv_ref, dkt_ref, dvt_ref, wgrad_ref, sems = refs[blocks:]
    step = pl.program_id(0)
    width, rows_all = turned_ref.shape
    lane = lax.broadcasted_iota(jnp.int32, (rows_all, LANES), 1)
    first = (lane % HD) < (HD // 2)
    k_views = half_views(k_ref[...], score_scale)
    v_views = half_views(v_ref[...], 1.0)
    tile_cols = [slice(t * LANES, (t + 1) * LANES) for t in range(3)]
    q_tiles = [q_ref[:, cols].astype(f32) for cols in tile_cols]
    g_tiles = [grad_ref[:, cols].astype(f32) for cols in tile_cols]
    q_heads = [tile.astype(bf16) for tile in head_tiles(q_tiles)]
    g_heads = [tile.astype(bf16) for tile in head_tiles(g_tiles)]

    def turned_heads(tiles):
        out = []
        for head in range(HEADS_STEP):
            tile = tiles[head // 2].T
            if head % 2 != head // 3:
                tile = jnp.concatenate([tile[HD:], tile[:HD]], axis=0)
            out.append(tile.astype(bf16))
        return out

    q_turned, g_turned = turned_heads(q_tiles), turned_heads(g_tiles)
    dkt_ref[...] = jnp.zeros_like(dkt_ref)
    dvt_ref[...] = jnp.zeros_like(dvt_ref)
    seg_col, seg_row = segc_ref[...], segr_ref[...]
    cosine, sine_val = cos_ref[...], -sin_ref[...]
    for start in range(0, rows_all, block):
        keys = start + block
        rows = slice(start, keys)
        visible = visible_keys(seg_col, seg_row, start, block, keys)
        norms = lse_ref[0, rows, :]
        parts = []
        for kv in range(2):
            three = [3 * kv + j for j in range(3)]
            q_rows = jnp.concatenate([q_heads[h][rows] for h in three], axis=0)
            g_rows = jnp.concatenate([g_heads[h][rows] for h in three], axis=0)
            norm = jnp.concatenate([norms[:, h : h + 1] for h in three], axis=0).reshape(3, block, 1)
            scores = contract_last(q_rows, k_views[kv][:keys]).reshape(3, block, keys)
            probs = jnp.where(visible[None], jnp.exp(scores - norm), 0.0)
            prob_grad = contract_last(g_rows, v_views[kv][:keys]).reshape(3, block, keys)
            centre = jnp.sum(probs * prob_grad, axis=-1, keepdims=True)
            score_grad = (probs * (prob_grad - centre)).astype(bf16).reshape(3 * block, keys)
            probs = probs.astype(bf16).reshape(3 * block, keys)
            dq = matmul(score_grad, k_views[kv][:keys])
            parts += [dq[j * block : (j + 1) * block] for j in range(3)]
            q_across = jnp.concatenate([q_turned[h][:, rows] for h in three], axis=1)
            g_across = jnp.concatenate([g_turned[h][:, rows] for h in three], axis=1)
            dkt_ref[kv, :, :keys] += matmul(q_across, score_grad)
            dvt_ref[kv, :, :keys] += matmul(g_across, probs)
        for t in range(3):
            low, high = parts[2 * t], parts[2 * t + 1]
            low = pltpu.roll(low, HD, 1) if t == 2 else low
            high = pltpu.roll(high, HD, 1) if t == 0 else high
            turned_back = turn(low + high, cosine[rows], sine_val[rows], first[rows])
            dq_ref[rows, tile_cols[t]] = turned_back.astype(bf16)

    def joined(ref):
        return jnp.where(lane < HD, ref[0].T, ref[1].T)

    dk_ref[...] = turn(joined(dkt_ref) * score_scale, cosine, sine_val, first).astype(bf16)
    dv_ref[...] = joined(dvt_ref).astype(bf16)
    at = lambda start, wide: pl.ds(pl.multiple_of(start, LANES), wide)
    normed_turned = turned_ref[...]
    count = wgrad_ref.shape[1] // (5 * LANES)
    wgrad_ref[:, at(step * 3 * LANES, 3 * LANES)] = matmul(normed_turned, dq_ref[...]).astype(bf16)
    wgrad_ref[:, at((3 * count + step) * LANES, LANES)] = matmul(normed_turned, dk_ref[...]).astype(bf16)
    wgrad_ref[:, at((4 * count + step) * LANES, LANES)] = matmul(normed_turned, dv_ref[...]).astype(bf16)

    @pl.when(step == pl.num_programs(0) - 1)
    def _():
        copies = spread_copies(wgrad_ref, table_ref, dests, sems)
        for c in copies:
            c.start()
        for c in copies:
            c.wait()


def attend_backward(base, steps, table, turned, queries, keys, values, grads, norms, cosine, sine_val,
                    segment):
    width, rows = turned.shape
    members, layers = table.shape
    full = 5 * steps * LANES
    wide = pl.BlockSpec((rows, 3 * LANES), lambda i: (0, base + i))
    thin = pl.BlockSpec((rows, LANES), lambda i: (0, base + i))
    out_wide = pl.BlockSpec((rows, 3 * LANES), lambda i: (0, i))
    out_thin = pl.BlockSpec((rows, LANES), lambda i: (0, i))
    return pl.pallas_call(
        functools.partial(attend_back_kernel, 128, min(members, 2)),
        grid=(steps,),
        in_specs=[
            smem_spec(),
            whole_spec((width, rows)),
            wide,
            thin,
            thin,
            wide,
            pl.BlockSpec((1, rows, LANES), lambda i: (base + i, 0, 0)),
            whole_spec((rows, LANES)),
            whole_spec((rows, LANES)),
            whole_spec((rows, 1)),
            whole_spec((1, rows)),
        ],
        out_specs=[any_spec()] * min(members, 2) + [out_wide, out_thin, out_thin],
        out_shape=stack_shapes(table, width, full)
        + [jax.ShapeDtypeStruct((rows, k * LANES * steps), bf16) for k in (3, 1, 1)],
        scratch_shapes=[
            pltpu.VMEM((2, LANES, rows), f32),
            pltpu.VMEM((2, LANES, rows), f32),
            pltpu.VMEM((width, full), bf16),
            pltpu.SemaphoreType.DMA((members * layers,)),
        ],
        compiler_params=params(),
        cost_estimate=small_cost(),
    )(table, turned, queries, keys, values, grads, norms, cosine, sine_val, segment[:, None],
      segment[None, :])


def input_kernel(x_ref, mgrad_ref, w_ref, *refs):
    *grads, out_ref, gain_ref = refs

    @pl.when(pl.program_id(0) == 0)
    def _():
        gain_ref[...] = w_ref[:, QW + 2 * KW :].astype(f32).T[GAIN_ONE : GAIN_ONE + 1, :]

    x = x_ref[...].astype(f32)
    rinv = lax.rsqrt(jnp.mean(x * x, axis=-1, keepdims=True) + norm_eps)
    gain = gain_ref[...]
    start = [0, QW, QW + KW]
    total = None
    for number, ref in enumerate(grads):
        wide = ref.shape[1]
        kind = number % 3
        product = contract_last(ref[...], w_ref[:, start[kind] : start[kind] + wide])
        start[kind] += wide
        total = product if total is None else total + product
    scaled = gain * total
    back = rinv * scaled - x * (rinv * rinv * rinv * jnp.mean(scaled * x, axis=-1, keepdims=True))
    out_ref[...] = mgrad_ref[...] + back


def row_tiles(rows, width):
    return pl.BlockSpec((rows // ROW_TILES, width), lambda i: (i, 0))


def to_input(hidden_in, middle_grad, w_qkv, grads):
    rows, width = hidden_in.shape
    tall = row_tiles(rows, width)
    return pl.pallas_call(
        input_kernel,
        grid=(ROW_TILES,),
        in_specs=[tall, tall, whole_spec(w_qkv.shape)] + [row_tiles(rows, g.shape[1]) for g in grads],
        out_specs=tall,
        out_shape=jax.ShapeDtypeStruct(hidden_in.shape, f32),
        scratch_shapes=[pltpu.VMEM((1, width), f32)],
        compiler_params=params(),
        cost_estimate=small_cost(),
    )(hidden_in, middle_grad, w_qkv, *grads)


def experts_kernel(x_counts, c_counts, expert, packed, has_prev, has_sums, last, *refs):
    refs = list(refs)
    take = lambda count: [refs.pop(0) for _ in range(count)]
    (place_ref,) = take(1)
    x_src = [take(c) for c in x_counts]
    c_src = [take(c) for c in c_counts]
    weights = take(1 if packed else 3)
    prev_src = [take(2) for _ in x_counts] if has_prev else None
    sums_src = take(3) if has_sums else None
    dest = [take(2) for _ in x_counts]
    sums_dst = take(1 if packed and last else 3)
    xs, cs, og_out, og_grad = take(4)
    prevs = take(2) if has_prev else None
    acc = take(3)
    held = take(3) if packed else weights
    (staged,) = take(1) if packed and last else (None,)
    sem_in, sem_out, sem_sum, sem_w = take(4)
    i = pl.program_id(0)
    count = len(x_counts)
    width = cs.shape[2]
    hidden = acc[0].shape[1]

    def weight_loads():
        own, low = held[0].shape[2], held[2].shape[2]
        src = weights[0]
        pairs = [(src.at[:, :, pl.ds(0, own)], held[0]), (src.at[:, :, pl.ds(own, own)], held[1])]
        for third in range(width // hidden):
            pairs.append(
                (
                    src.at[:, :, pl.ds(2 * own + third * low, low)],
                    held[2].at[:, :, :, pl.ds(third * hidden, hidden)],
                )
            )
        return [pltpu.make_async_copy(a, b, sem_w.at[q]) for q, (a, b) in enumerate(pairs)]

    def loads(t):
        out = []
        slot = t % 2
        number = 0
        for srcs, dst in ((x_src[t], xs), (c_src[t], cs)):
            row = 0
            for r in srcs:
                rows = r.shape[0]
                out.append(pltpu.make_async_copy(r, dst.at[slot, pl.ds(row, rows)], sem_in.at[slot, number]))
                row += rows
                number += 1
        return out

    def prev_loads(t):
        if not has_prev:
            return []
        slot = t % 2
        return [
            pltpu.make_async_copy(r, dst.at[slot], sem_in.at[slot, 6 + q])
            for q, (r, dst) in enumerate(zip(prev_src[t], prevs))
        ]

    def sum_stores():
        if last and packed:
            return [pltpu.make_async_copy(staged, sums_dst[0], sem_sum.at[0])]
        if last:
            return []
        return [pltpu.make_async_copy(a, d, sem_sum.at[q]) for q, (a, d) in enumerate(zip(acc, sums_dst))]

    def stores(t):
        slot = t % 2
        return [
            pltpu.make_async_copy(og_out.at[slot], dest[t][0], sem_out.at[slot, 0]),
            pltpu.make_async_copy(og_grad.at[slot], dest[t][1], sem_out.at[slot, 1]),
        ]

    def sum_loads():
        return [pltpu.make_async_copy(s, a, sem_sum.at[q]) for q, (s, a) in enumerate(zip(sums_src, acc))]

    @pl.when(i == 0)
    def _():
        for c in loads(0):
            c.start()
        if packed:
            for c in weight_loads():
                c.start()
        for c in prev_loads(0):
            c.start()
        if has_sums:
            for c in sum_loads():
                c.start()
        else:
            for a in acc:
                a[...] = jnp.zeros_like(a)
        if packed:
            for c in weight_loads():
                c.wait()

    for t in range(count):
        @pl.when(i == t)
        def _(t=t):
            for c in loads(t):
                c.wait()
            if t + 1 < count:
                for c in loads(t + 1) + prev_loads(t + 1):
                    c.start()
            if t >= 2:
                for c in stores(t - 2):
                    c.wait()

    slot = lax.rem(i, 2)
    rows_in = xs[slot, :, :width]
    extra = xs[slot, :, width:].astype(f32)
    lane = lax.broadcasted_iota(jnp.int32, extra.shape, 1)
    mine = place_ref[0] * PAIR_E + expert
    gate_row = jnp.sum(jnp.where((lane < 3 * E) & (lax.rem(lane, E) == mine), extra, 0.0), axis=-1, keepdims=True)
    cot_wide = cs[slot].astype(f32)
    w_gate = held[0][...].reshape(width, hidden)
    w_up = held[1][...].reshape(width, hidden)
    w_down = held[2][...].reshape(hidden, width)
    gate_proj = matmul(rows_in, w_gate)
    up_proj = matmul(rows_in, w_up)
    sigmoid_g = 1.0 / (1.0 + jnp.exp(-gate_proj))
    active = gate_proj * sigmoid_g
    mid = (active * up_proj).astype(bf16)
    out_grad = ((resid_scale * gate_row) * cot_wide).astype(bf16)
    mid_grad = contract_last(out_grad, w_down)
    gate_grad = (mid_grad * up_proj * sigmoid_g * (1.0 + gate_proj * (1.0 - sigmoid_g))).astype(bf16)
    up_grad = (mid_grad * active).astype(bf16)
    mix = jnp.sum(mid.astype(f32) * mid_grad, axis=-1, keepdims=True)
    if has_sums:
        @pl.when(i == 0)
        def _():
            for c in sum_loads():
                c.wait()
    acc[0][...] += contract_rows(rows_in, gate_grad)
    acc[1][...] += contract_rows(rows_in, up_grad)
    acc[2][...] += contract_rows(mid, out_grad)

    @pl.when(i == count - 1)
    def _():
        if last and packed:
            layers, members, own, _ = held[0].shape
            low = held[2].shape[2]
            staged[:, :, :own] = acc[0][...].astype(bf16).reshape(layers, members, own, hidden)
            staged[:, :, own : 2 * own] = acc[1][...].astype(bf16).reshape(layers, members, own, hidden)
            for third in range(width // hidden):
                piece = acc[2][:, third * hidden : (third + 1) * hidden].astype(bf16)
                start = 2 * own + third * low
                staged[:, :, start : start + low] = piece.reshape(layers, members, low, hidden)
        elif last:
            for a, d in zip(acc, sums_dst):
                d[...] = a[...].astype(bf16)
        for c in sum_stores():
            c.start()

    if has_prev:
        for t in range(count):
            @pl.when(i == t)
            def _(t=t):
                for c in prev_loads(t):
                    c.wait()
    mixed = gate_row * matmul(mid, w_down)
    if has_prev:
        mixed = mixed + prevs[0][slot].astype(f32)
    og_out[slot] = mixed.astype(bf16)
    back = contract_last(gate_grad, w_gate) + contract_last(up_grad, w_up)
    if has_prev:
        back = back + prevs[1][slot, :, :width].astype(f32)
    og_grad[slot, :, :width] = back.astype(bf16)
    high = mix.astype(bf16).astype(f32)
    middle = (mix - high).astype(bf16).astype(f32)
    low = mix - high - middle
    spread = jnp.where(lane == mine, high, jnp.where(lane == mine + E, middle, jnp.where(lane == mine + 2 * E, low, 0.0)))
    if has_prev:
        spread = spread + prevs[1][slot, :, width:].astype(f32)
    og_grad[slot, :, width:] = spread.astype(bf16)
    for t in range(count):
        @pl.when(i == t)
        def _(t=t):
            for c in stores(t):
                c.start()

    @pl.when(i == count - 1)
    def _():
        for c in sum_stores():
            c.wait()
        for t in range(max(0, count - 2), count):
            for c in stores(t):
                c.wait()


def experts_call(place, expert, xs, cs, weights, own, prev, sums, last):
    tiles = [x if isinstance(x, (list, tuple)) else [x] for x in xs]
    cots = [c if isinstance(c, (list, tuple)) else [c] for c in cs]
    rows = sum(a.shape[0] for a in tiles[0])
    full = tiles[0][0].shape[1]
    packed = len(weights) == 1
    width, hidden = cots[0][0].shape[1], weights[0].shape[-1] if packed else weights[0].shape[1]
    anyspace = pl.BlockSpec(memory_space=pl.ANY)
    resident = lambda a: pl.BlockSpec(a.shape, lambda i: (0, 0), pipeline_mode=pl.Buffered(1))
    args, specs = [jnp.asarray(place, jnp.int32).reshape(1)], [pl.BlockSpec(memory_space=pltpu.SMEM)]
    for group in tiles + cots:
        args += group
        specs += [anyspace] * len(group)
    args += list(weights)
    specs += [anyspace] if packed else [resident(w) for w in weights]
    if prev is not None:
        for pair in prev:
            args += list(pair)
            specs += [anyspace] * 2
    if sums is not None:
        args += list(sums)
        specs += [anyspace] * 3
    shapes, out_specs = [], []
    for _ in tiles:
        shapes += [jax.ShapeDtypeStruct((rows, width), bf16), jax.ShapeDtypeStruct((rows, full), bf16)]
        out_specs += [anyspace] * 2
    sum_shapes = ((width, hidden), (width, hidden), (hidden, width))
    if packed and last:
        shapes.append(jax.ShapeDtypeStruct(weights[0].shape, bf16))
        out_specs.append(anyspace)
        sum_shapes = ()
    for shape in sum_shapes:
        shapes.append(jax.ShapeDtypeStruct(shape, bf16 if last else f32))
        out_specs.append(pl.BlockSpec(shape, lambda i: (0, 0), pipeline_mode=pl.Buffered(1)) if last else anyspace)
    scratch = [
        pltpu.VMEM((2, rows, full), bf16), pltpu.VMEM((2, rows, width), bf16),
        pltpu.VMEM((2, rows, width), bf16), pltpu.VMEM((2, rows, full), bf16),
    ]
    if prev is not None:
        scratch += [pltpu.VMEM((2, rows, width), bf16), pltpu.VMEM((2, rows, full), bf16)]
    scratch += [pltpu.VMEM((width, hidden), f32), pltpu.VMEM((width, hidden), f32), pltpu.VMEM((hidden, width), f32)]
    if packed:
        layers = weights[0].shape[0]
        low = hidden // (layers * GROUP)
        scratch += [
            pltpu.VMEM((layers, GROUP, own, hidden), bf16),
            pltpu.VMEM((layers, GROUP, own, hidden), bf16),
            pltpu.VMEM((layers, GROUP, low, width), bf16),
        ]
    if packed and last:
        scratch.append(pltpu.VMEM(weights[0].shape, bf16))
    scratch += [pltpu.SemaphoreType.DMA(shape) for shape in ((2, 8), (2, 2), (3,), (2 + width // hidden,))]
    out = pl.pallas_call(
        functools.partial(experts_kernel, [len(t) for t in tiles], [len(c) for c in cots], expert, packed,
                          prev is not None, sums is not None, last),
        grid=(len(tiles),),
        in_specs=specs,
        out_specs=out_specs,
        out_shape=shapes,
        scratch_shapes=scratch,
        compiler_params=pltpu.CompilerParams(vmem_limit_bytes=60 * 1024 * 1024),
        cost_estimate=small_cost(),
    )(*args)
    parts = [(out[2 * t], out[2 * t + 1]) for t in range(len(tiles))]
    return parts, tuple(out[2 * len(tiles) :])


def shards(device_count, hidden_in, lengths, routes, norm_attn, w_query, w_key, w_value, w_out,
           norm_moe, w_router, w_gate, w_up, w_down, cotangent):
    n = device_count
    layers = n // GROUP
    along = [[q + GROUP * j for j in range(layers)] for q in range(GROUP)]
    inside = [[GROUP * j + q for q in range(GROUP)] for j in range(layers)]
    me = lax.axis_index("fsdp")
    place, layer = me % GROUP, me // GROUP
    core = lambda value: swap(value, 1, n)
    rows, width = hidden_in.shape
    own_rows = w_query.shape[0]
    hidden = w_gate.shape[2]
    own_hidden = w_down.shape[1]
    split = own_rows % 16 == 0
    thirds = width // hidden
    members = jnp.arange(GROUP, dtype=jnp.int32) ^ place
    steps = jnp.arange(layers, dtype=jnp.int32)

    extras = jnp.concatenate(
        [w_router, norm_attn[:, None], norm_moe[:, None], jnp.zeros((own_rows, LANES - E - 2), bf16)],
        axis=1,
    )
    own_qkv = jnp.concatenate([w_query, w_key, w_value, extras], axis=1)

    down_rows = jnp.concatenate(
        [w_down[:, :, t * hidden : (t + 1) * hidden] for t in range(thirds)], axis=1
    )
    expert_rows = jnp.concatenate([w_gate, w_up, down_rows], axis=1)
    per_expert = expert_rows.shape[1]
    expert_rows = expert_rows.reshape(GROUP, PAIR_E, per_expert, hidden).transpose(1, 0, 2, 3)

    expert_rows = lax.all_to_all(expert_rows, "fsdp", 1, 1, tiled=True, axis_index_groups=inside)

    def over_all(block):
        return lax.all_gather(block, "fsdp", axis=0, axis_index_groups=along)

    aligned = own_rows % 16 == 0 and own_hidden % 16 == 0

    def expert_parts(gathered):
        if aligned:
            return (gathered,)
        gate = gathered[:, :, :own_rows].reshape(width, hidden)
        up = gathered[:, :, own_rows : 2 * own_rows].reshape(width, hidden)
        low = gathered[:, :, 2 * own_rows :].reshape(layers, GROUP, thirds, own_hidden, hidden)
        return gate, up, low.transpose(0, 1, 3, 2, 4).reshape(hidden, width)

    segment, position = layout(lengths[0], rows)
    cosine, sine_val = turn_tables(position)
    half = HK // 4
    c_parts = [cotangent[: rows // 4], cotangent[rows // 4 : rows // 2], cotangent[rows // 2 :]]
    c_own = core(cotangent)
    near = lambda block: (swap(block, 2, n), swap(block, 4, n))
    cores = lambda *values: [core(value) for value in values]
    if split:
        ring = list(range(layers))
        plan = [[(k, j) for j in ring] for k in range(6)]
        upper = (layers + 1) // 2
        plan += [[(k, j) for j in part] for k in (6, 7) for part in (ring[:upper], ring[upper:]) if part]
        cut = upper * own_rows
        blocks = ring_start(own_qkv, layers, n)
        column = joined_rows(ring_end(blocks, layers, n), ring)
        column, expert_rows, w_out = tie(column, expert_rows, w_out)

        def far_ways(pair):
            ways = [swap(pair[0][:cut], 4, n)]
            return ways + ([swap(pair[1][cut:], 2, n)] if layers > 1 else [])

        def in_order(own, other, near_two, far):
            return [own, other[0], near_two[0], other[1], near_two[1], other[2], *far, *cores(*far)]

        near_qkv = near(column)
        wo_blocks = ring_start(w_out, layers, n)
        near_qkv, wo_blocks, cosine, sine_val, c_own, c_parts = tie(
            near_qkv, wo_blocks, cosine, sine_val, c_own, c_parts
        )
        far = far_ways(near_qkv)
        other = cores(column, *near_qkv)
        other, wo_blocks = tie(other, wo_blocks)
        wo_column = joined_rows(ring_end(wo_blocks, layers, n), ring)
        far, other, wo_column = tie(far, other, wo_column)
        pieces = in_order(column, other, near_qkv, far)
        pieces, wo_column, c_parts = tie(pieces, wo_column, c_parts)
        wo_near, wo_other = near(wo_column), core(wo_column)
        table = own_rows * (GROUP * steps[None, :] + members[:, None])
        ring_table = own_rows * (GROUP * ((layer - steps[None, :]) % layers) + members[:, None])
    else:
        pieces = [lax.all_gather(own_qkv, "fsdp", axis=0, tiled=True)]
        plan = [[(0, 0)]]
        table = ring_table = jnp.zeros((1, 1), jnp.int32)
    table, ring_table = table.astype(jnp.int32), ring_table.astype(jnp.int32)

    gathered_first, gathered_second = over_all(expert_rows[0]), over_all(expert_rows[1])
    c_near = [near(c_parts[0])]
    w_qkv, normed, turned, *first_half = attend_forward(
        0, half, ring_table, plan, pieces, hidden_in, cosine, sine_val, segment
    )
    normed, c_near, c_parts = tie(normed, c_near, c_parts)
    if split:
        wo_near, wo_other, normed = tie(wo_near, wo_other, normed)
        wo_far = far_ways(wo_near)
    c_near.append(near(c_parts[1]))
    second_half = attend_forward(half, half, table, None, w_qkv, normed, cosine, sine_val, segment)
    attn_out = (first_half[3], second_half[3])
    if split:
        attn_out, c_parts, wo_far, wo_near, c_near = tie(attn_out, c_parts, wo_far, wo_near, c_near)
        out_pieces = in_order(wo_column, [wo_other, *cores(*wo_near)], wo_near, wo_far)
    else:
        attn_out, c_parts, c_near = tie(attn_out, c_parts, c_near)
        out_pieces = [lax.all_gather(w_out, "fsdp", axis=0, tiled=True)]

    c_near.append(near(c_parts[2]))
    w_out_full, middle, inner, mix = to_middle(
        ring_table, plan, out_pieces, hidden_in, attn_out, w_qkv, routes
    )
    inner_near = gather_start(inner, n)
    inner_other = core(inner)
    c_core = [cores(*pair) for pair in c_near[:2]]
    inner_here, c_near[2] = tie(inner, c_near[2])
    c_core.append(cores(*c_near[2]))
    inner_here, inner_other, c_core[:2] = tie(inner_here, inner_other, c_core[:2])

    def expert_sums(sums):
        if len(sums) == 1:
            return lax.psum_scatter(
                sums[0], "fsdp", scatter_dimension=0, tiled=True, axis_index_groups=along
            )[0]
        gate, up, low = sums
        low = low.reshape(layers, GROUP, own_hidden, thirds, hidden).transpose(0, 1, 3, 2, 4)
        joined = jnp.concatenate(
            [
                gate.reshape(layers, GROUP, own_rows, hidden),
                up.reshape(layers, GROUP, own_rows, hidden),
                low.reshape(layers, GROUP, thirds * own_hidden, hidden),
            ],
            axis=2,
        )
        return lax.psum_scatter(
            joined, "fsdp", scatter_dimension=0, tiled=True, axis_index_groups=along
        )[0]

    first = expert_parts(gathered_first)
    second = expert_parts(gathered_second)
    part = {}

    def run(expert, tiles, xs, cs, weights, sums, last):
        done, sums = experts_call(
            place, expert, xs, cs, weights, own_rows, [part[k] for k in tiles] if expert else None, sums, last
        )
        part.update(zip(tiles, done))
        return sums

    x_own, c_own = [[inner_here], [inner_other]], [[cotangent], [c_own]]
    sums = run(0, [0, 1], x_own, c_own, first, None, False)
    inner_near, c_core[2], sums = tie(inner_near, c_core[2], sums)
    inner_far = gather_far(*inner_near, n)
    cots_far = swap(c_near[0][0], 4, n), swap(c_near[1][0], 4, n), swap(c_near[2][1], 2, n)
    x_near = [[inner_near[0]], [core(inner_near[0])], [inner_near[1]], [core(inner_near[1])]]
    c_all = []
    for q in (0, 1):
        c_all += [[pair[q] for pair in c_near], [pair[q] for pair in c_core]]
    sums = run(0, [2, 3, 4, 5], x_near, c_all, first, sums, False)
    inner_far, cots_far = after((inner_far, cots_far), sums)
    x_far = [list(inner_far), [core(v) for v in inner_far]]
    c_far = [list(cots_far), [core(v) for v in cots_far]]
    sums0 = run(0, [6, 7], x_far, c_far, first, sums, True)
    shared0 = expert_sums(sums0)

    sums = run(1, [6, 7], x_far, c_far, second, None, False)
    both_ways = lambda low, high: (swap(low, 4, n), swap(high, 2, n))
    halves, out_halves = sums_for_far([(part[6][i], core(part[7][i])) for i in (1, 0)])
    x_near[0], halves, out_halves = tie(x_near[0], halves, out_halves)
    far_sums, out_far = both_ways(*halves), both_ways(*out_halves)
    sums = run(1, [2, 3, 4, 5], x_near, c_all, second, sums, False)
    done = [part[k] for k in (2, 3, 4, 5)]
    far_sums, out_far, sums, done = tie(far_sums, out_far, sums, done)
    part.update(zip((2, 3, 4, 5), done))
    near_sums = sums_for_near(part[2][1], core(part[3][1]), part[4][1], core(part[5][1]), *far_sums)
    x_own[0], near_sums, shared0 = tie(x_own[0], near_sums, shared0)
    ways = lambda two, four: [swap(two, 2, n), swap(four, 4, n)]
    inner_near = ways(*near_sums)
    out_core = [core(part[3][0]), core(part[5][0])]
    sums = run(1, [0, 1], x_own, c_own, second, sums, True)
    inner_near, out_core, sums, part[0], part[1] = tie(inner_near, out_core, sums, part[0], part[1])
    shared1 = expert_sums(sums)
    inner_other = core(part[1][1])
    out_blocks = (part[2][0], out_core[0], part[4][0], out_core[1])
    out_sums = half_for_near(0, *out_blocks, out_far[0])
    out_sums, inner_other = tie(out_sums, inner_other)
    out_low = ways(*out_sums)
    def to_owner(block):
        return lax.all_to_all(block, "fsdp", 0, 0, tiled=True, axis_index_groups=inside)

    owned0 = to_owner(shared0)
    out_other = core(part[1][0])
    *out_grads, middle_grad, attn_grad0, attn_grad1 = middle_back(
        table, (part[0][1], inner_other, *inner_near), inner, mix, middle, cotangent, w_qkv, attn_out,
        w_out_full,
    )
    out_low, out_other, owned0, out_grads, middle_grad, attn_grad0, attn_grad1 = tie(
        out_low, out_other, owned0, out_grads, middle_grad, attn_grad0, attn_grad1
    )

    wide = lambda value: value.astype(f32)

    def chips_of(stacks):
        return sums_of_stack(stacks[0], core(stacks[1])) if split else [stacks[0]]

    def far_of(chips):
        return both_ways(*chips[3:]) if split else ()

    def near_sums_of(chips, far):
        return stack_near([(*chips[1:3], *far)]) if split else ()

    def near_of(chips, far):
        return [swap(value, bit, n) for value, bit in zip(near_sums_of(chips, far), (2, 4))]

    def back(base, steps, half_set, grads):
        return attend_backward(
            base, steps, table, turned, *half_set[:3], grads, half_set[4], cosine, sine_val, segment
        )

    wo_chips = chips_of(out_grads)
    out_sums = half_for_near(1, *tie(*out_blocks, middle_grad)[:4], out_far[1])
    attn_grad0, wo_chips, out_sums = tie(attn_grad0, wo_chips, out_sums)
    out_high = ways(*out_sums)
    wo_far = far_of(wo_chips)
    *stacks0, dq0, dk0, dv0 = back(0, half, first_half, attn_grad0)
    out_high, wo_far, stacks0, dq0, dk0, dv0 = tie(out_high, wo_far, stacks0, dq0, dk0, dv0)

    chips0 = chips_of(stacks0)
    attn_grad1, chips0 = tie(attn_grad1, chips0)
    wo_near, far0 = near_of(wo_chips, wo_far), far_of(chips0)
    *stacks1, dq1, dk1, dv1 = back(0, half, second_half, attn_grad1)
    wo_near, far0, stacks1, dq1, dk1, dv1, shared1 = tie(wo_near, far0, stacks1, dq1, dk1, dv1, shared1)

    def summed(group, near_sums):
        own = jnp.concatenate([chips[0] for chips in group], axis=1)
        return (wide(own) + wide(near_sums[0]) + wide(near_sums[1])).astype(bf16)

    chips1 = chips_of(stacks1)
    dq1, chips1 = tie(dq1, chips1)
    near0, far1 = near_of(chips0, far0), far_of(chips1)
    if split:
        wo_shared = lax.psum_scatter(
            summed([wo_chips], wo_near), "fsdp", scatter_dimension=0, tiled=True, axis_index_groups=along
        )
    else:
        wo_shared = lax.psum_scatter(wo_chips[0], "fsdp", scatter_dimension=0, tiled=True)
    input_grad = to_input(hidden_in, middle_grad, w_qkv, (dq0, dk0, dv0, dq1, dk1, dv1))
    near0, far1, input_grad = tie(near0, far1, input_grad)
    near1, near0 = tie(near_sums_of(chips1, far1), near0)
    near1 = [swap(value, bit, n) for value, bit in zip(near1, (2, 4))]

    def over_layers(chips, near_sums):
        if not split:
            return [lax.psum_scatter(chips[0], "fsdp", scatter_dimension=0, tiled=True)]
        total = summed([chips], near_sums)
        return layer_start(total.reshape(layers, own_rows, -1), layer, layers, n)

    late0 = over_layers(chips0, near0)
    owned1 = to_owner(after(shared1, near1))
    out_low, near1, wo_shared, late0 = tie(out_low, near1, wo_shared, late0)
    mine_out = wide(wo_shared)
    out_total = wide(part[0][0]) + wide(out_other) + jnp.concatenate(
        [wide(out_low[0]) + wide(out_low[1]), wide(out_high[0]) + wide(out_high[1])], axis=0
    )
    mixed = (middle + resid_scale * out_total).astype(bf16)
    late1, owned1 = tie(over_layers(chips1, near1), owned1)
    mine = [layer_add(late0), layer_add(late1)]

    shared = jnp.stack([owned0, owned1], axis=1).reshape(E, per_expert, hidden).astype(f32)
    grad_gate, grad_up = shared[:, :own_rows], shared[:, own_rows : 2 * own_rows]
    grad_down = jnp.concatenate(
        [
            shared[:, 2 * own_rows + t * own_hidden : 2 * own_rows + (t + 1) * own_hidden]
            for t in range(thirds)
        ],
        axis=2,
    )
    def joined(kind):
        pieces = []
        for part_grads in mine:
            unit = part_grads.shape[1] // 5
            start, wide = ((0, 3 * unit), (3 * unit, unit), (4 * unit, unit))[kind]
            pieces.append(part_grads[:, start : start + wide])
        return jnp.concatenate(pieces, axis=1)

    grad_query, grad_key, grad_value = joined(0), joined(1), joined(2)
    grad_router = mine_out[:, width : width + E]

    def row_sums(weight, grad):
        return jnp.sum(weight.astype(f32) * grad, axis=-1)

    grad_norm_attn = (
        row_sums(w_query, grad_query) + row_sums(w_key, grad_key) + row_sums(w_value, grad_value)
    ) / norm_attn.astype(f32)
    grad_norm_moe = (
        jnp.sum(row_sums(w_gate, grad_gate) + row_sums(w_up, grad_up), axis=0)
        + row_sums(w_router, grad_router)
    ) / norm_moe.astype(f32)
    return (
        mixed,
        input_grad,
        grad_norm_attn,
        grad_query,
        grad_key,
        grad_value,
        mine_out[:, :width],
        grad_norm_moe,
        grad_router,
        grad_gate,
        grad_up,
        grad_down,
    )


def solution(mesh):

    in_specs = (
        P("fsdp", None),
        P("fsdp", None),
        P("fsdp", None),
        P("fsdp"),
        P("fsdp", None),
        P("fsdp", None),
        P("fsdp", None),
        P("fsdp", None),
        P("fsdp"),
        P("fsdp", None),
        P(None, "fsdp", None),
        P(None, "fsdp", None),
        P(None, "fsdp", None),
        P("fsdp", None),
    )
    out_specs = (
        P("fsdp", None),
        P("fsdp", None),
        P("fsdp"),
        P("fsdp", None),
        P("fsdp", None),
        P("fsdp", None),
        P("fsdp", None),
        P("fsdp"),
        P("fsdp", None),
        P(None, "fsdp", None),
        P(None, "fsdp", None),
        P(None, "fsdp", None),
    )
    return jax.shard_map(
        functools.partial(shards, mesh.shape["fsdp"]),
        mesh=mesh,
        in_specs=in_specs,
        out_specs=out_specs,
        check_vma=False,
    )
```

```python
import functools
import math

import jax
import jax.numpy as jnp
from jax import lax
from jax.experimental import pallas as pl
from jax.experimental.pallas import tpu as pltpu
from jax.sharding import PartitionSpec as P

HQ = 24
HK = 8
HD = 64
E = 16
GROUP = 8
PAIR_E = E // GROUP
HEADS_STEP = 2 * HQ // HK
LANES = 128
ROW_TILES = 2
QW = HQ * HD
KW = HK * HD
QKV_WIDE = QW + 2 * KW + LANES
GAIN_ONE = E
GAIN_TWO = E + 1
VMEM_LIMIT = 58 * 1024 * 1024

norm_eps = 1e-06
resid_scale = 0.22
score_scale = 0.015625
rope_base = 10000.0
masked_score = -1e30

f32 = jnp.float32
bf16 = jnp.bfloat16


def matmul(left, right):
    return jnp.dot(left, right, preferred_element_type=f32)


def contract_rows(left, right):
    return lax.dot_general(left, right, (((0,), (0,)), ((), ())), preferred_element_type=f32)


def contract_last(left, right):
    return lax.dot_general(left, right, (((1,), (1,)), ((), ())), preferred_element_type=f32)


def layout(seq_lengths, row_count):
    seq_ends = jnp.cumsum(seq_lengths)
    starts = seq_ends - seq_lengths
    places = jnp.arange(row_count, dtype=jnp.int32)
    member = (places[:, None] >= starts[None, :]) & (places[:, None] < seq_ends[None, :])
    labels = jnp.arange(seq_lengths.shape[0], dtype=jnp.int32)
    segment = jnp.sum(jnp.where(member, labels[None, :], 0), axis=1)
    offset = jnp.sum(jnp.where(member, starts[None, :], 0), axis=1)
    return (segment, places - offset)


def turn_tables(position):
    half_dim = HD // 2
    inv_freq = jnp.exp(
        -(jnp.arange(half_dim, dtype=f32) * (2.0 / HD)) * math.log(rope_base)
    )
    angles = position.astype(f32)[:, None] * inv_freq[None, :]
    cosine, sine_val = jnp.cos(angles), jnp.sin(angles)
    return (
        jnp.concatenate([cosine] * 4, axis=1),
        jnp.concatenate([-sine_val, sine_val] * 2, axis=1),
    )


def swap(value, bit, device_count):
    return lax.ppermute(value, "fsdp", [(i, i ^ bit) for i in range(device_count)])


def shift(value, steps, device_count):
    moved = [(i, (i + GROUP * steps) % device_count) for i in range(device_count)]
    return lax.ppermute(value, "fsdp", moved)


def after(value, *needed):
    return lax.optimization_barrier((value, needed))[0]


def tie(*values):
    return lax.optimization_barrier(values)


def ring_start(own, layers, device_count):
    blocks = {0: own}
    ahead, behind = own, own
    for step in range(1, (layers - 1) // 2 + 1):
        ahead, behind = shift(ahead, 1, device_count), shift(behind, -1, device_count)
        blocks[step], blocks[layers - step] = ahead, behind
    return blocks


def ring_end(blocks, layers, device_count):
    if layers % 2 == 0:
        ahead, behind = blocks[layers // 2 - 1], blocks[(layers // 2 + 1) % layers]
        half = ahead.shape[1] // 2 // LANES * LANES
        blocks[layers // 2] = jnp.concatenate(
            [shift(ahead[:, :half], 1, device_count), shift(behind[:, half:], -1, device_count)], axis=1
        )
    return blocks


def joined_rows(blocks, places):
    return jnp.concatenate([blocks[j] for j in places], axis=0)


def gather_start(own, device_count):
    return swap(own, 2, device_count), swap(own, 4, device_count)


def gather_far(from2, from4, device_count):
    half = from2.shape[0] // 2
    return swap(from2[:half], 4, device_count), swap(from4[half:], 2, device_count)


def gather_cores(own, near, far, device_count):
    other = lambda value: swap(value, 1, device_count)
    return [
        [own], [other(own)], [near[0]], [other(near[0])], [near[1]], [other(near[1])],
        list(far), [other(far[0]), other(far[1])],
    ]


def layer_start(stacked, layer, layers, device_count):
    pick = lambda at: lax.dynamic_index_in_dim(stacked, at % layers, 0, keepdims=False)
    return [pick(layer)] + [shift(pick(layer + k), k, device_count) for k in range(1, layers)]


def layer_add(blocks):
    total = blocks[0].astype(f32)
    for block in blocks[1:]:
        total = total + block.astype(f32)
    return total


def turn(values, cosine, sine_val, low_half):
    shifted = jnp.where(low_half, pltpu.roll(values, LANES - 32, 1), pltpu.roll(values, 32, 1))
    return values * cosine + shifted * sine_val


def half_views(pair, scale):
    lane = lax.broadcasted_iota(jnp.int32, pair.shape, 1)
    scaled = pair.astype(f32) * scale
    low = lane < HD
    return jnp.where(low, scaled, 0.0).astype(bf16), jnp.where(low, 0.0, scaled).astype(bf16)


def head_tiles(tiles):
    return [
        tiles[head // 2] if head % 2 == head // 3 else pltpu.roll(tiles[head // 2], HD, 1)
        for head in range(HEADS_STEP)
    ]


def visible_keys(seg_col, seg_row, row_start, rows, keys):
    query_at = row_start + lax.broadcasted_iota(jnp.int32, (rows, keys), 0)
    key_at = lax.broadcasted_iota(jnp.int32, (rows, keys), 1)
    return (seg_col[row_start : row_start + rows, :] == seg_row[:, :keys]) & (key_at <= query_at)


def any_spec():
    return pl.BlockSpec(memory_space=pl.ANY)


def smem_spec():
    return pl.BlockSpec(memory_space=pltpu.SMEM)


def small_cost():
    return pl.CostEstimate(flops=1_000_000, bytes_accessed=100_000, transcendentals=0)


def extras_spec(width):
    return pl.BlockSpec((width, LANES), lambda *_: (0, (QW + 2 * KW) // LANES))


def params():
    return pltpu.CompilerParams(vmem_limit_bytes=VMEM_LIMIT)


def whole_spec(shape):
    zeros = (0,) * len(shape)
    return pl.BlockSpec(shape, lambda *_: zeros, pipeline_mode=pl.Buffered(1))


def gather_copies(plan, refs, table_ref, dst, sems):
    copies = []
    for ref, runs in zip(refs, plan):
        rows = ref.shape[0] // len(runs)
        for number, (member, step) in enumerate(runs):
            start = pl.multiple_of(table_ref[member, step], 16)
            copies.append(
                pltpu.make_async_copy(
                    ref.at[pl.ds(number * rows, rows)],
                    dst.at[pl.ds(start, rows)],
                    sems.at[len(copies)],
                )
            )
    return copies


def spread_copies(src, table_ref, refs, sems):
    copies = []
    members, blocks = table_ref.shape
    rows = src.shape[0] // (members * blocks)
    for member in range(members):
        for block in range(blocks):
            start = pl.multiple_of(table_ref[member, block], 16)
            to = (member // 2 * blocks + block) * rows
            copies.append(
                pltpu.make_async_copy(
                    src.at[pl.ds(start, rows)], refs[member % 2].at[pl.ds(to, rows)], sems.at[len(copies)]
                )
            )
    return copies


def stack_shapes(table, width, full):
    members = table.shape[0]
    stacks = min(members, 2)
    return [jax.ShapeDtypeStruct((width // stacks, full), bf16)] * stacks


def far_kernel(*refs):
    count = len(refs) // 4
    for q in range(count):
        left, right = refs[2 * q : 2 * q + 2]
        low, high = refs[2 * count + 2 * q : 2 * count + 2 * q + 2]
        total = (left[...].astype(f32) + right[...].astype(f32)).astype(bf16)
        low[...] = total[0]
        high[...] = total[1]


def sums_for_far(pairs):
    rows = pairs[0][0].shape[0]
    tile = rows // 8
    args, in_specs, out_specs, shapes = [], [], [], []
    for pair in pairs:
        width = pair[0].shape[1]
        args += [value.reshape(2, rows // 2, width) for value in pair]
        in_specs += [pl.BlockSpec((2, tile, width), lambda i: (0, i, 0))] * 2
        out_specs += [pl.BlockSpec((tile, width), lambda i: (i, 0))] * 2
        shapes += [jax.ShapeDtypeStruct((rows // 2, width), bf16)] * 2
    out = pl.pallas_call(
        far_kernel, grid=(4,), in_specs=in_specs, out_specs=out_specs, out_shape=shapes,
        compiler_params=params(), cost_estimate=small_cost(),
    )(*args)
    return [out[2 * q : 2 * q + 2] for q in range(len(pairs))]


def near_kernel(a2_ref, b2_ref, a4_ref, b4_ref, low_ref, high_ref, sum2_ref, sum4_ref):
    two = a2_ref[...].astype(f32) + b2_ref[...].astype(f32)
    four = a4_ref[...].astype(f32) + b4_ref[...].astype(f32)
    sum2_ref[0] = (two[0] + low_ref[...].astype(f32)).astype(bf16)
    sum2_ref[1] = two[1].astype(bf16)
    sum4_ref[0] = four[0].astype(bf16)
    sum4_ref[1] = (four[1] + high_ref[...].astype(f32)).astype(bf16)


def sums_for_near(a2, b2, a4, b4, low, high):
    rows, width = a2.shape
    tile = rows // 8
    pair = pl.BlockSpec((2, tile, width), lambda i: (0, i, 0))
    single = pl.BlockSpec((tile, width), lambda i: (i, 0))
    out = pl.pallas_call(
        near_kernel, grid=(4,), in_specs=[pair] * 4 + [single] * 2, out_specs=[pair] * 2,
        out_shape=[jax.ShapeDtypeStruct((2, rows // 2, width), bf16)] * 2,
        compiler_params=params(), cost_estimate=small_cost(),
    )(*[value.reshape(2, rows // 2, width) for value in (a2, b2, a4, b4)], low, high)
    return [value.reshape(rows, width) for value in out]


def half_kernel(more_for, a2_ref, b2_ref, a4_ref, b4_ref, more_ref, sum2_ref, sum4_ref):
    two = a2_ref[...].astype(f32) + b2_ref[...].astype(f32)
    four = a4_ref[...].astype(f32) + b4_ref[...].astype(f32)
    more = more_ref[...].astype(f32)
    sum2_ref[...] = (two + more if more_for == 2 else two).astype(bf16)
    sum4_ref[...] = (four + more if more_for == 4 else four).astype(bf16)


def half_for_near(which, a2, b2, a4, b4, more):
    rows, width = a2.shape
    tile = rows // 8
    picked = pl.BlockSpec((tile, width), lambda i: (4 * which + i, 0))
    single = pl.BlockSpec((tile, width), lambda i: (i, 0))
    return pl.pallas_call(
        functools.partial(half_kernel, (2, 4)[which]), grid=(4,), in_specs=[picked] * 4 + [single],
        out_specs=[single] * 2, out_shape=[jax.ShapeDtypeStruct((rows // 2, width), bf16)] * 2,
        compiler_params=params(), cost_estimate=small_cost(),
    )(a2, b2, a4, b4, more)


def stack_kernel(even_ref, odd_ref, own_ref, two_ref, four_ref, low_ref, high_ref):
    rows = own_ref.shape[0]
    half = rows // 2
    spots = ((own_ref, 0, rows), (two_ref, rows, rows), (four_ref, 2 * rows, rows), (low_ref, 3 * rows, half),
             (high_ref, 3 * rows + half, half))
    for ref, start, count in spots:
        at = slice(start, start + count)
        ref[...] = (even_ref[at].astype(f32) + odd_ref[at].astype(f32)).astype(bf16)


def sums_of_stack(even, odd):
    rows, width = even.shape[0] // 4, even.shape[1]
    vmem = pl.BlockSpec(memory_space=pltpu.VMEM)
    return pl.pallas_call(
        stack_kernel, in_specs=[vmem] * 2, out_specs=[vmem] * 5,
        out_shape=[jax.ShapeDtypeStruct((r, width), bf16) for r in (rows, rows, rows, rows // 2, rows // 2)],
        compiler_params=params(), cost_estimate=small_cost(),
    )(even, odd)


def stack_near_kernel(*refs):
    *sources, sum2_ref, sum4_ref = refs
    start = 0
    for q in range(0, len(sources), 4):
        two_ref, four_ref, low_ref, high_ref = sources[q : q + 4]
        half = low_ref.shape[0]
        at = slice(start, start + two_ref.shape[1])
        sum2_ref[:half, at] = (two_ref[:half].astype(f32) + low_ref[...].astype(f32)).astype(bf16)
        sum2_ref[half:, at] = two_ref[half:]
        sum4_ref[:half, at] = four_ref[:half]
        sum4_ref[half:, at] = (four_ref[half:].astype(f32) + high_ref[...].astype(f32)).astype(bf16)
        start += two_ref.shape[1]


def stack_near(sets):
    vmem = pl.BlockSpec(memory_space=pltpu.VMEM)
    shape = (sets[0][0].shape[0], sum(one[0].shape[1] for one in sets))
    return pl.pallas_call(
        stack_near_kernel, in_specs=[vmem] * (4 * len(sets)), out_specs=[vmem] * 2,
        out_shape=[jax.ShapeDtypeStruct(shape, bf16)] * 2,
        compiler_params=params(), cost_estimate=small_cost(),
    )(*[value for one in sets for value in one])


def attend_kernel(block, plan, table_ref, x_ref, cos_ref, sin_ref, segc_ref, segr_ref, *refs):
    pair = pl.program_id(0)
    rows_all, width = x_ref.shape
    at = lambda start, wide: pl.ds(pl.multiple_of(start, LANES), wide)
    if plan is None:
        wq_ref, wk_ref, wv_ref, q_ref, k_ref, v_ref, out_ref, lse_ref = refs
        normed_ref = x_ref
        w_q, w_k, w_v = wq_ref[...], wk_ref[...], wv_ref[...]
    else:
        sources = refs[: len(plan)]
        (w_out_ref, normed_ref, turned_ref, q_ref, k_ref, v_ref, out_ref, lse_ref,
         w_ref, sems, save_sem) = refs[len(plan) :]

        @pl.when(pair == 0)
        def _():
            copies = gather_copies(plan, sources, table_ref, w_ref, sems)
            for c in copies:
                c.start()
            x = x_ref[...].astype(f32)
            rinv = lax.rsqrt(jnp.mean(x * x, axis=-1, keepdims=True) + norm_eps)
            for c in copies:
                c.wait()
            pltpu.make_async_copy(w_ref, w_out_ref, save_sem).start()
            gains = w_ref[:, QW + 2 * KW :].astype(f32).T
            scaled = x * rinv * gains[GAIN_ONE : GAIN_ONE + 1, :]
            normed_ref[...] = scaled.astype(bf16)
            turned_ref[...] = scaled.T.astype(bf16)

        w_q = w_ref[:, at(pair * 3 * LANES, 3 * LANES)]
        w_k = w_ref[:, at(QW + pair * LANES, LANES)]
        w_v = w_ref[:, at(QW + KW + pair * LANES, LANES)]

    normed = normed_ref[...]
    lane = lax.broadcasted_iota(jnp.int32, (rows_all, LANES), 1)
    first = (lane % HD) < (HD // 2)
    cosine, sine_val = cos_ref[...], sin_ref[...]
    q_pre = matmul(normed, w_q)
    tiles = []
    for t in range(3):
        cols = slice(t * LANES, (t + 1) * LANES)
        tiles.append(turn(q_pre[:, cols], cosine, sine_val, first))
        q_ref[:, cols] = tiles[t].astype(bf16)
    heads = [tile.astype(bf16) for tile in head_tiles(tiles)]
    k_low = turn(matmul(normed, w_k), cosine, sine_val, first).astype(bf16)
    v_low = matmul(normed, w_v).astype(bf16)
    k_ref[...] = k_low
    v_ref[...] = v_low
    k_views = half_views(k_low, score_scale)
    v_views = half_views(v_low, 1.0)
    seg_col, seg_row = segc_ref[...], segr_ref[...]
    lane_b = lax.broadcasted_iota(jnp.int32, (block, LANES), 1)
    for start in range(0, rows_all, block):
        keys = start + block
        rows = slice(start, keys)
        visible = visible_keys(seg_col, seg_row, start, block, keys)
        norms = jnp.zeros((block, LANES), f32)
        outs = []
        for kv in range(2):
            q_rows = jnp.concatenate([heads[3 * kv + j][rows] for j in range(3)], axis=0)
            scores = contract_last(q_rows, k_views[kv][:keys]).reshape(3, block, keys)
            scores = jnp.where(visible[None], scores, masked_score)
            peak = jnp.max(scores, axis=-1, keepdims=True)
            expo = jnp.exp(scores - peak)
            mass = jnp.sum(expo, axis=-1, keepdims=True)
            probs = (expo * (1.0 / mass)).astype(bf16)
            total = matmul(probs.reshape(3 * block, keys), v_views[kv][:keys])
            norm = peak + jnp.log(mass)
            for j in range(3):
                outs.append(total[j * block : (j + 1) * block])
                norms = jnp.where(lane_b == 3 * kv + j, norm[j], norms)
        for t in range(3):
            low, high = outs[2 * t], outs[2 * t + 1]
            low = pltpu.roll(low, HD, 1) if t == 2 else low
            high = pltpu.roll(high, HD, 1) if t == 0 else high
            out_ref[rows, t * LANES : (t + 1) * LANES] = (low + high).astype(bf16)
        lse_ref[0, rows, :] = norms

    if plan is not None:
        @pl.when(pair == pl.num_programs(0) - 1)
        def _():
            pltpu.make_async_copy(w_ref, w_out_ref, save_sem).wait()


def attend_forward(base, steps, table, plan, weights, rows_in, cosine, sine_val, segment):
    rows, width = rows_in.shape
    wide = pl.BlockSpec((rows, 3 * LANES), lambda i: (0, i))
    thin = pl.BlockSpec((rows, LANES), lambda i: (0, i))
    in_specs = [
        smem_spec(),
        whole_spec((rows, width)),
        whole_spec((rows, LANES)),
        whole_spec((rows, LANES)),
        whole_spec((rows, 1)),
        whole_spec((1, rows)),
    ]
    out_specs = [wide, thin, thin, wide, pl.BlockSpec((1, rows, LANES), lambda i: (i, 0, 0))]
    out_shape = [
        jax.ShapeDtypeStruct((rows, 3 * LANES * steps), bf16),
        jax.ShapeDtypeStruct((rows, LANES * steps), bf16),
        jax.ShapeDtypeStruct((rows, LANES * steps), bf16),
        jax.ShapeDtypeStruct((rows, 3 * LANES * steps), bf16),
        jax.ShapeDtypeStruct((steps, rows, LANES), f32),
    ]
    if plan is None:
        in_specs += [
            pl.BlockSpec((width, 3 * LANES), lambda i: (0, base + i)),
            pl.BlockSpec((width, LANES), lambda i: (0, QW // LANES + base + i)),
            pl.BlockSpec((width, LANES), lambda i: (0, (QW + KW) // LANES + base + i)),
        ]
        weights = [weights] * 3
        scratch = []
    else:
        in_specs += [any_spec()] * len(weights)
        out_specs = [any_spec(), whole_spec((rows, width)), whole_spec((width, rows))] + out_specs
        out_shape = [
            jax.ShapeDtypeStruct((width, QKV_WIDE), bf16),
            jax.ShapeDtypeStruct((rows, width), bf16),
            jax.ShapeDtypeStruct((width, rows), bf16),
        ] + out_shape
        scratch = [
            pltpu.VMEM((width, QKV_WIDE), bf16),
            pltpu.SemaphoreType.DMA((sum(len(r) for r in plan),)),
            pltpu.SemaphoreType.DMA(()),
        ]
    return pl.pallas_call(
        functools.partial(attend_kernel, 128, plan),
        grid=(steps,),
        in_specs=in_specs,
        out_specs=out_specs,
        out_shape=out_shape,
        scratch_shapes=scratch,
        compiler_params=params(),
        cost_estimate=small_cost(),
    )(table, rows_in, cosine, sine_val, segment[:, None], segment[None, :], *weights)


def middle_kernel(plan, table_ref, x_ref, attn0_ref, attn1_ref, extras_ref, routes_ref, *refs):
    sources = refs[: len(plan)]
    w_out_ref, middle_ref, inner_ref, mix_ref, w_ref, gain_ref, sems, save_sem = refs[len(plan) :]
    step = pl.program_id(0)
    rows, width = x_ref.shape

    @pl.when(step == 0)
    def _():
        copies = gather_copies(plan, sources, table_ref, w_ref, sems)
        for c in copies:
            c.start()
        gain_ref[...] = extras_ref[...].astype(f32).T[GAIN_TWO : GAIN_TWO + 1, :]
        for c in copies:
            c.wait()
        pltpu.make_async_copy(w_ref, w_out_ref, save_sem).start()

    extras = extras_ref[...]
    half = attn0_ref.shape[1]
    product = matmul(attn0_ref[...], w_ref[:half]) + matmul(attn1_ref[...], w_ref[half:])
    middle = x_ref[...].astype(f32) + resid_scale * product
    middle_ref[...] = middle
    rinv = lax.rsqrt(jnp.mean(middle * middle, axis=-1, keepdims=True) + norm_eps)
    inner = (middle * rinv * gain_ref[...]).astype(bf16)
    inner_ref[:, :width] = inner
    logits = matmul(inner, extras)
    lane = lax.broadcasted_iota(jnp.int32, logits.shape, 1)
    routes = routes_ref[...]
    named = lane == routes[:, 0:1]
    for k in range(1, routes.shape[1]):
        named = named | (lane == routes[:, k : k + 1])
    chosen = jnp.where(named, logits, masked_score)
    peak = jnp.max(chosen, axis=-1, keepdims=True)
    expo = jnp.where(named, jnp.exp(chosen - peak), 0.0)
    mix = expo / jnp.sum(expo, axis=-1, keepdims=True)
    mix_ref[...] = mix
    high = mix.astype(bf16).astype(f32)
    rest = (mix - high).astype(bf16).astype(f32)
    low = mix - high - rest
    spread = high + pltpu.roll(rest, E, 1) + pltpu.roll(low, 2 * E, 1)
    inner_ref[:, width:] = spread.astype(bf16)

    @pl.when(step == pl.num_programs(0) - 1)
    def _():
        pltpu.make_async_copy(w_ref, w_out_ref, save_sem).wait()


def to_middle(table, plan, pieces, hidden_in, attn_out, extras, routes):
    rows, width = hidden_in.shape
    tall = functools.partial(row_tiles, rows)
    return pl.pallas_call(
        functools.partial(middle_kernel, plan),
        grid=(ROW_TILES,),
        in_specs=[smem_spec(), tall(width), tall(QW // 2), tall(QW // 2), extras_spec(width)]
        + [tall(routes.shape[1])]
        + [any_spec()] * len(pieces),
        out_specs=[any_spec(), tall(width), tall(width + LANES), tall(LANES)],
        out_shape=[
            jax.ShapeDtypeStruct((QW, width), bf16),
            jax.ShapeDtypeStruct((rows, width), f32),
            jax.ShapeDtypeStruct((rows, width + LANES), bf16),
            jax.ShapeDtypeStruct((rows, LANES), f32),
        ],
        scratch_shapes=[
            pltpu.VMEM((QW, width), bf16),
            pltpu.VMEM((1, width), f32),
            pltpu.SemaphoreType.DMA((sum(len(r) for r in plan),)),
            pltpu.SemaphoreType.DMA(()),
        ],
        compiler_params=params(),
        cost_estimate=small_cost(),
    )(table, hidden_in, *attn_out, extras, routes, *pieces)


def middle_back_kernel(blocks, table_ref, own0_ref, own1_ref, near2_ref, near4_ref, inner_ref, mix_ref, middle_ref,
                       cot_ref, extras_ref, attn0_src, attn1_src, w_src, *refs):
    dests = refs[:blocks]
    (grad_ref, attn_grad0_ref, attn_grad1_ref, wgrad_ref, attn0_ref, attn1_ref, w_ref, sems,
     load_sems) = refs[blocks:]
    rows, width = middle_ref.shape
    loads = [
        pltpu.make_async_copy(a, b, load_sems.at[q])
        for q, (a, b) in enumerate(((w_src, w_ref), (attn0_src, attn0_ref), (attn1_src, attn1_ref)))
    ]
    for c in loads:
        c.start()
    total = own0_ref[...].astype(f32) + own1_ref[...].astype(f32)
    total = total + near2_ref[...].astype(f32) + near4_ref[...].astype(f32)
    inner_grad, tail = total[:, :width], total[:, width:]
    lane = lax.broadcasted_iota(jnp.int32, tail.shape, 1)
    mix = mix_ref[...]
    mix_grad = tail + pltpu.roll(tail, LANES - E, 1) + pltpu.roll(tail, LANES - 2 * E, 1)
    mix_grad = jnp.where(lane < E, mix_grad, 0.0)
    logit_grad = mix_grad - mix * jnp.sum(mix_grad, axis=-1, keepdims=True)
    logit_grad = logit_grad.astype(bf16)
    extras = extras_ref[...]
    gain = extras.astype(f32).T[GAIN_TWO : GAIN_TWO + 1, :]
    inner_grad = inner_grad + contract_last(logit_grad, extras)
    middle = middle_ref[...]
    rinv = lax.rsqrt(jnp.mean(middle * middle, axis=-1, keepdims=True) + norm_eps)
    scaled = gain * inner_grad
    back = rinv * scaled - middle * (rinv * rinv * rinv * jnp.mean(scaled * middle, axis=-1, keepdims=True))
    middle_grad = cot_ref[...].astype(f32) + back
    grad_ref[...] = middle_grad
    proj_grad = (resid_scale * middle_grad).astype(bf16)
    half = attn0_ref.shape[1]
    for c in loads:
        c.wait()
    attn_grad0_ref[...] = contract_last(proj_grad, w_ref[:half]).astype(bf16)
    attn_grad1_ref[...] = contract_last(proj_grad, w_ref[half:]).astype(bf16)
    wgrad_ref[:half, :width] = contract_rows(attn0_ref[...], proj_grad).astype(bf16)
    wgrad_ref[half:, :width] = contract_rows(attn1_ref[...], proj_grad).astype(bf16)
    wgrad_ref[:, width:] = contract_rows(inner_ref[:, :width], logit_grad).astype(bf16)
    copies = spread_copies(wgrad_ref, table_ref, dests, sems)
    for c in copies:
        c.start()
    for c in copies:
        c.wait()


def middle_back(table, sums, inner, mix, middle, cotangent, extras, attn_out, w_out):
    rows, width = middle.shape
    members, layers = table.shape
    vmem = pl.BlockSpec(memory_space=pltpu.VMEM)
    full = width + LANES
    return pl.pallas_call(
        functools.partial(middle_back_kernel, min(members, 2)),
        grid=(1,),
        in_specs=[smem_spec()] + [vmem] * 8 + [extras_spec(width)] + [any_spec()] * 3,
        out_specs=[any_spec()] * min(members, 2) + [vmem] * 3,
        out_shape=stack_shapes(table, width, full)
        + [jax.ShapeDtypeStruct((rows, width), f32)]
        + [jax.ShapeDtypeStruct((rows, QW // 2), bf16)] * 2,
        scratch_shapes=[
            pltpu.VMEM((width, full), bf16),
            pltpu.VMEM((rows, QW // 2), bf16),
            pltpu.VMEM((rows, QW // 2), bf16),
            pltpu.VMEM(w_out.shape, bf16),
            pltpu.SemaphoreType.DMA((members * layers,)),
            pltpu.SemaphoreType.DMA((3,)),
        ],
        compiler_params=params(),
        cost_estimate=small_cost(),
    )(table, *sums, inner, mix, middle, cotangent, extras, *attn_out, w_out)


def attend_back_kernel(block, blocks, table_ref, turned_ref, q_ref, k_ref, v_ref, grad_ref, lse_ref,
                       cos_ref, sin_ref, segc_ref, segr_ref, *refs):
    dests = refs[:blocks]
    dq_ref, dk_ref, dv_ref, dkt_ref, dvt_ref, wgrad_ref, sems = refs[blocks:]
    step = pl.program_id(0)
    width, rows_all = turned_ref.shape
    lane = lax.broadcasted_iota(jnp.int32, (rows_all, LANES), 1)
    first = (lane % HD) < (HD // 2)
    k_views = half_views(k_ref[...], score_scale)
    v_views = half_views(v_ref[...], 1.0)
    tile_cols = [slice(t * LANES, (t + 1) * LANES) for t in range(3)]
    q_tiles = [q_ref[:, cols].astype(f32) for cols in tile_cols]
    g_tiles = [grad_ref[:, cols].astype(f32) for cols in tile_cols]
    q_heads = [tile.astype(bf16) for tile in head_tiles(q_tiles)]
    g_heads = [tile.astype(bf16) for tile in head_tiles(g_tiles)]

    def turned_heads(tiles):
        out = []
        for head in range(HEADS_STEP):
            tile = tiles[head // 2].T
            if head % 2 != head // 3:
                tile = jnp.concatenate([tile[HD:], tile[:HD]], axis=0)
            out.append(tile.astype(bf16))
        return out

    q_turned, g_turned = turned_heads(q_tiles), turned_heads(g_tiles)
    dkt_ref[...] = jnp.zeros_like(dkt_ref)
    dvt_ref[...] = jnp.zeros_like(dvt_ref)
    seg_col, seg_row = segc_ref[...], segr_ref[...]
    cosine, sine_val = cos_ref[...], -sin_ref[...]
    for start in range(0, rows_all, block):
        keys = start + block
        rows = slice(start, keys)
        visible = visible_keys(seg_col, seg_row, start, block, keys)
        norms = lse_ref[0, rows, :]
        parts = []
        for kv in range(2):
            three = [3 * kv + j for j in range(3)]
            q_rows = jnp.concatenate([q_heads[h][rows] for h in three], axis=0)
            g_rows = jnp.concatenate([g_heads[h][rows] for h in three], axis=0)
            norm = jnp.concatenate([norms[:, h : h + 1] for h in three], axis=0).reshape(3, block, 1)
            scores = contract_last(q_rows, k_views[kv][:keys]).reshape(3, block, keys)
            probs = jnp.where(visible[None], jnp.exp(scores - norm), 0.0)
            prob_grad = contract_last(g_rows, v_views[kv][:keys]).reshape(3, block, keys)
            centre = jnp.sum(probs * prob_grad, axis=-1, keepdims=True)
            score_grad = (probs * (prob_grad - centre)).astype(bf16).reshape(3 * block, keys)
            probs = probs.astype(bf16).reshape(3 * block, keys)
            dq = matmul(score_grad, k_views[kv][:keys])
            parts += [dq[j * block : (j + 1) * block] for j in range(3)]
            q_across = jnp.concatenate([q_turned[h][:, rows] for h in three], axis=1)
            g_across = jnp.concatenate([g_turned[h][:, rows] for h in three], axis=1)
            dkt_ref[kv, :, :keys] += matmul(q_across, score_grad)
            dvt_ref[kv, :, :keys] += matmul(g_across, probs)
        for t in range(3):
            low, high = parts[2 * t], parts[2 * t + 1]
            low = pltpu.roll(low, HD, 1) if t == 2 else low
            high = pltpu.roll(high, HD, 1) if t == 0 else high
            turned_back = turn(low + high, cosine[rows], sine_val[rows], first[rows])
            dq_ref[rows, tile_cols[t]] = turned_back.astype(bf16)

    def joined(ref):
        return jnp.where(lane < HD, ref[0].T, ref[1].T)

    dk_ref[...] = turn(joined(dkt_ref) * score_scale, cosine, sine_val, first).astype(bf16)
    dv_ref[...] = joined(dvt_ref).astype(bf16)
    at = lambda start, wide: pl.ds(pl.multiple_of(start, LANES), wide)
    normed_turned = turned_ref[...]
    count = wgrad_ref.shape[1] // (5 * LANES)
    wgrad_ref[:, at(step * 3 * LANES, 3 * LANES)] = matmul(normed_turned, dq_ref[...]).astype(bf16)
    wgrad_ref[:, at((3 * count + step) * LANES, LANES)] = matmul(normed_turned, dk_ref[...]).astype(bf16)
    wgrad_ref[:, at((4 * count + step) * LANES, LANES)] = matmul(normed_turned, dv_ref[...]).astype(bf16)

    @pl.when(step == pl.num_programs(0) - 1)
    def _():
        copies = spread_copies(wgrad_ref, table_ref, dests, sems)
        for c in copies:
            c.start()
        for c in copies:
            c.wait()


def attend_backward(base, steps, table, turned, queries, keys, values, grads, norms, cosine, sine_val,
                    segment):
    width, rows = turned.shape
    members, layers = table.shape
    full = 5 * steps * LANES
    wide = pl.BlockSpec((rows, 3 * LANES), lambda i: (0, base + i))
    thin = pl.BlockSpec((rows, LANES), lambda i: (0, base + i))
    out_wide = pl.BlockSpec((rows, 3 * LANES), lambda i: (0, i))
    out_thin = pl.BlockSpec((rows, LANES), lambda i: (0, i))
    return pl.pallas_call(
        functools.partial(attend_back_kernel, 128, min(members, 2)),
        grid=(steps,),
        in_specs=[
            smem_spec(),
            whole_spec((width, rows)),
            wide,
            thin,
            thin,
            wide,
            pl.BlockSpec((1, rows, LANES), lambda i: (base + i, 0, 0)),
            whole_spec((rows, LANES)),
            whole_spec((rows, LANES)),
            whole_spec((rows, 1)),
            whole_spec((1, rows)),
        ],
        out_specs=[any_spec()] * min(members, 2) + [out_wide, out_thin, out_thin],
        out_shape=stack_shapes(table, width, full)
        + [jax.ShapeDtypeStruct((rows, k * LANES * steps), bf16) for k in (3, 1, 1)],
        scratch_shapes=[
            pltpu.VMEM((2, LANES, rows), f32),
            pltpu.VMEM((2, LANES, rows), f32),
            pltpu.VMEM((width, full), bf16),
            pltpu.SemaphoreType.DMA((members * layers,)),
        ],
        compiler_params=params(),
        cost_estimate=small_cost(),
    )(table, turned, queries, keys, values, grads, norms, cosine, sine_val, segment[:, None],
      segment[None, :])


def input_kernel(x_ref, mgrad_ref, w_ref, *refs):
    *grads, out_ref, gain_ref = refs

    @pl.when(pl.program_id(0) == 0)
    def _():
        gain_ref[...] = w_ref[:, QW + 2 * KW :].astype(f32).T[GAIN_ONE : GAIN_ONE + 1, :]

    x = x_ref[...].astype(f32)
    rinv = lax.rsqrt(jnp.mean(x * x, axis=-1, keepdims=True) + norm_eps)
    gain = gain_ref[...]
    start = [0, QW, QW + KW]
    total = None
    for number, ref in enumerate(grads):
        wide = ref.shape[1]
        kind = number % 3
        product = contract_last(ref[...], w_ref[:, start[kind] : start[kind] + wide])
        start[kind] += wide
        total = product if total is None else total + product
    scaled = gain * total
    back = rinv * scaled - x * (rinv * rinv * rinv * jnp.mean(scaled * x, axis=-1, keepdims=True))
    out_ref[...] = mgrad_ref[...] + back


def row_tiles(rows, width):
    return pl.BlockSpec((rows // ROW_TILES, width), lambda i: (i, 0))


def to_input(hidden_in, middle_grad, w_qkv, grads):
    rows, width = hidden_in.shape
    tall = row_tiles(rows, width)
    return pl.pallas_call(
        input_kernel,
        grid=(ROW_TILES,),
        in_specs=[tall, tall, whole_spec(w_qkv.shape)] + [row_tiles(rows, g.shape[1]) for g in grads],
        out_specs=tall,
        out_shape=jax.ShapeDtypeStruct(hidden_in.shape, f32),
        scratch_shapes=[pltpu.VMEM((1, width), f32)],
        compiler_params=params(),
        cost_estimate=small_cost(),
    )(hidden_in, middle_grad, w_qkv, *grads)


def experts_kernel(x_counts, c_counts, expert, packed, has_prev, has_sums, last, *refs):
    refs = list(refs)
    take = lambda count: [refs.pop(0) for _ in range(count)]
    (place_ref,) = take(1)
    x_src = [take(c) for c in x_counts]
    c_src = [take(c) for c in c_counts]
    weights = take(1 if packed else 3)
    prev_src = [take(2) for _ in x_counts] if has_prev else None
    sums_src = take(3) if has_sums else None
    dest = [take(2) for _ in x_counts]
    sums_dst = take(1 if packed and last else 3)
    xs, cs, og_out, og_grad = take(4)
    prevs = take(2) if has_prev else None
    acc = take(3)
    held = take(3) if packed else weights
    (staged,) = take(1) if packed and last else (None,)
    sem_in, sem_out, sem_sum, sem_w = take(4)
    i = pl.program_id(0)
    count = len(x_counts)
    width = cs.shape[2]
    hidden = acc[0].shape[1]

    def weight_loads():
        own, low = held[0].shape[2], held[2].shape[2]
        src = weights[0]
        pairs = [(src.at[:, :, pl.ds(0, own)], held[0]), (src.at[:, :, pl.ds(own, own)], held[1])]
        for third in range(width // hidden):
            pairs.append(
                (
                    src.at[:, :, pl.ds(2 * own + third * low, low)],
                    held[2].at[:, :, :, pl.ds(third * hidden, hidden)],
                )
            )
        return [pltpu.make_async_copy(a, b, sem_w.at[q]) for q, (a, b) in enumerate(pairs)]

    def loads(t):
        out = []
        slot = t % 2
        number = 0
        for srcs, dst in ((x_src[t], xs), (c_src[t], cs)):
            row = 0
            for r in srcs:
                rows = r.shape[0]
                out.append(pltpu.make_async_copy(r, dst.at[slot, pl.ds(row, rows)], sem_in.at[slot, number]))
                row += rows
                number += 1
        return out

    def prev_loads(t):
        if not has_prev:
            return []
        slot = t % 2
        return [
            pltpu.make_async_copy(r, dst.at[slot], sem_in.at[slot, 6 + q])
            for q, (r, dst) in enumerate(zip(prev_src[t], prevs))
        ]

    def sum_stores():
        if last and packed:
            return [pltpu.make_async_copy(staged, sums_dst[0], sem_sum.at[0])]
        if last:
            return []
        return [pltpu.make_async_copy(a, d, sem_sum.at[q]) for q, (a, d) in enumerate(zip(acc, sums_dst))]

    def stores(t):
        slot = t % 2
        return [
            pltpu.make_async_copy(og_out.at[slot], dest[t][0], sem_out.at[slot, 0]),
            pltpu.make_async_copy(og_grad.at[slot], dest[t][1], sem_out.at[slot, 1]),
        ]

    def sum_loads():
        return [pltpu.make_async_copy(s, a, sem_sum.at[q]) for q, (s, a) in enumerate(zip(sums_src, acc))]

    @pl.when(i == 0)
    def _():
        for c in loads(0):
            c.start()
        if packed:
            for c in weight_loads():
                c.start()
        for c in prev_loads(0):
            c.start()
        if has_sums:
            for c in sum_loads():
                c.start()
        else:
            for a in acc:
                a[...] = jnp.zeros_like(a)
        if packed:
            for c in weight_loads():
                c.wait()

    for t in range(count):
        @pl.when(i == t)
        def _(t=t):
            for c in loads(t):
                c.wait()
            if t + 1 < count:
                for c in loads(t + 1) + prev_loads(t + 1):
                    c.start()
            if t >= 2:
                for c in stores(t - 2):
                    c.wait()

    slot = lax.rem(i, 2)
    rows_in = xs[slot, :, :width]
    extra = xs[slot, :, width:].astype(f32)
    lane = lax.broadcasted_iota(jnp.int32, extra.shape, 1)
    mine = place_ref[0] * PAIR_E + expert
    gate_row = jnp.sum(jnp.where((lane < 3 * E) & (lax.rem(lane, E) == mine), extra, 0.0), axis=-1, keepdims=True)
    cot_wide = cs[slot].astype(f32)
    w_gate = held[0][...].reshape(width, hidden)
    w_up = held[1][...].reshape(width, hidden)
    w_down = held[2][...].reshape(hidden, width)
    gate_proj = matmul(rows_in, w_gate)
    up_proj = matmul(rows_in, w_up)
    sigmoid_g = 1.0 / (1.0 + jnp.exp(-gate_proj))
    active = gate_proj * sigmoid_g
    mid = (active * up_proj).astype(bf16)
    out_grad = ((resid_scale * gate_row) * cot_wide).astype(bf16)
    mid_grad = contract_last(out_grad, w_down)
    gate_grad = (mid_grad * up_proj * sigmoid_g * (1.0 + gate_proj * (1.0 - sigmoid_g))).astype(bf16)
    up_grad = (mid_grad * active).astype(bf16)
    mix = jnp.sum(mid.astype(f32) * mid_grad, axis=-1, keepdims=True)
    if has_sums:
        @pl.when(i == 0)
        def _():
            for c in sum_loads():
                c.wait()
    acc[0][...] += contract_rows(rows_in, gate_grad)
    acc[1][...] += contract_rows(rows_in, up_grad)
    acc[2][...] += contract_rows(mid, out_grad)

    @pl.when(i == count - 1)
    def _():
        if last and packed:
            layers, members, own, _ = held[0].shape
            low = held[2].shape[2]
            staged[:, :, :own] = acc[0][...].astype(bf16).reshape(layers, members, own, hidden)
            staged[:, :, own : 2 * own] = acc[1][...].astype(bf16).reshape(layers, members, own, hidden)
            for third in range(width // hidden):
                piece = acc[2][:, third * hidden : (third + 1) * hidden].astype(bf16)
                start = 2 * own + third * low
                staged[:, :, start : start + low] = piece.reshape(layers, members, low, hidden)
        elif last:
            for a, d in zip(acc, sums_dst):
                d[...] = a[...].astype(bf16)
        for c in sum_stores():
            c.start()

    if has_prev:
        for t in range(count):
            @pl.when(i == t)
            def _(t=t):
                for c in prev_loads(t):
                    c.wait()
    mixed = gate_row * matmul(mid, w_down)
    if has_prev:
        mixed = mixed + prevs[0][slot].astype(f32)
    og_out[slot] = mixed.astype(bf16)
    back = contract_last(gate_grad, w_gate) + contract_last(up_grad, w_up)
    if has_prev:
        back = back + prevs[1][slot, :, :width].astype(f32)
    og_grad[slot, :, :width] = back.astype(bf16)
    high = mix.astype(bf16).astype(f32)
    middle = (mix - high).astype(bf16).astype(f32)
    low = mix - high - middle
    spread = jnp.where(lane == mine, high, jnp.where(lane == mine + E, middle, jnp.where(lane == mine + 2 * E, low, 0.0)))
    if has_prev:
        spread = spread + prevs[1][slot, :, width:].astype(f32)
    og_grad[slot, :, width:] = spread.astype(bf16)
    for t in range(count):
        @pl.when(i == t)
        def _(t=t):
            for c in stores(t):
                c.start()

    @pl.when(i == count - 1)
    def _():
        for c in sum_stores():
            c.wait()
        for t in range(max(0, count - 2), count):
            for c in stores(t):
                c.wait()


def experts_call(place, expert, xs, cs, weights, own, prev, sums, last):
    tiles = [x if isinstance(x, (list, tuple)) else [x] for x in xs]
    cots = [c if isinstance(c, (list, tuple)) else [c] for c in cs]
    rows = sum(a.shape[0] for a in tiles[0])
    full = tiles[0][0].shape[1]
    packed = len(weights) == 1
    width, hidden = cots[0][0].shape[1], weights[0].shape[-1] if packed else weights[0].shape[1]
    anyspace = pl.BlockSpec(memory_space=pl.ANY)
    resident = lambda a: pl.BlockSpec(a.shape, lambda i: (0, 0), pipeline_mode=pl.Buffered(1))
    args, specs = [jnp.asarray(place, jnp.int32).reshape(1)], [pl.BlockSpec(memory_space=pltpu.SMEM)]
    for group in tiles + cots:
        args += group
        specs += [anyspace] * len(group)
    args += list(weights)
    specs += [anyspace] if packed else [resident(w) for w in weights]
    if prev is not None:
        for pair in prev:
            args += list(pair)
            specs += [anyspace] * 2
    if sums is not None:
        args += list(sums)
        specs += [anyspace] * 3
    shapes, out_specs = [], []
    for _ in tiles:
        shapes += [jax.ShapeDtypeStruct((rows, width), bf16), jax.ShapeDtypeStruct((rows, full), bf16)]
        out_specs += [anyspace] * 2
    sum_shapes = ((width, hidden), (width, hidden), (hidden, width))
    if packed and last:
        shapes.append(jax.ShapeDtypeStruct(weights[0].shape, bf16))
        out_specs.append(anyspace)
        sum_shapes = ()
    for shape in sum_shapes:
        shapes.append(jax.ShapeDtypeStruct(shape, bf16 if last else f32))
        out_specs.append(pl.BlockSpec(shape, lambda i: (0, 0), pipeline_mode=pl.Buffered(1)) if last else anyspace)
    scratch = [
        pltpu.VMEM((2, rows, full), bf16), pltpu.VMEM((2, rows, width), bf16),
        pltpu.VMEM((2, rows, width), bf16), pltpu.VMEM((2, rows, full), bf16),
    ]
    if prev is not None:
        scratch += [pltpu.VMEM((2, rows, width), bf16), pltpu.VMEM((2, rows, full), bf16)]
    scratch += [pltpu.VMEM((width, hidden), f32), pltpu.VMEM((width, hidden), f32), pltpu.VMEM((hidden, width), f32)]
    if packed:
        layers = weights[0].shape[0]
        low = hidden // (layers * GROUP)
        scratch += [
            pltpu.VMEM((layers, GROUP, own, hidden), bf16),
            pltpu.VMEM((layers, GROUP, own, hidden), bf16),
            pltpu.VMEM((layers, GROUP, low, width), bf16),
        ]
    if packed and last:
        scratch.append(pltpu.VMEM(weights[0].shape, bf16))
    scratch += [pltpu.SemaphoreType.DMA(shape) for shape in ((2, 8), (2, 2), (3,), (2 + width // hidden,))]
    out = pl.pallas_call(
        functools.partial(experts_kernel, [len(t) for t in tiles], [len(c) for c in cots], expert, packed,
                          prev is not None, sums is not None, last),
        grid=(len(tiles),),
        in_specs=specs,
        out_specs=out_specs,
        out_shape=shapes,
        scratch_shapes=scratch,
        compiler_params=pltpu.CompilerParams(vmem_limit_bytes=60 * 1024 * 1024),
        cost_estimate=small_cost(),
    )(*args)
    parts = [(out[2 * t], out[2 * t + 1]) for t in range(len(tiles))]
    return parts, tuple(out[2 * len(tiles) :])


def shards(device_count, hidden_in, lengths, routes, norm_attn, w_query, w_key, w_value, w_out,
           norm_moe, w_router, w_gate, w_up, w_down, cotangent):
    n = device_count
    layers = n // GROUP
    along = [[q + GROUP * j for j in range(layers)] for q in range(GROUP)]
    inside = [[GROUP * j + q for q in range(GROUP)] for j in range(layers)]
    me = lax.axis_index("fsdp")
    place, layer = me % GROUP, me // GROUP
    core = lambda value: swap(value, 1, n)
    rows, width = hidden_in.shape
    own_rows = w_query.shape[0]
    hidden = w_gate.shape[2]
    own_hidden = w_down.shape[1]
    split = own_rows % 16 == 0
    thirds = width // hidden
    members = jnp.arange(GROUP, dtype=jnp.int32) ^ place
    steps = jnp.arange(layers, dtype=jnp.int32)

    extras = jnp.concatenate(
        [w_router, norm_attn[:, None], norm_moe[:, None], jnp.zeros((own_rows, LANES - E - 2), bf16)],
        axis=1,
    )
    own_qkv = jnp.concatenate([w_query, w_key, w_value, extras], axis=1)

    down_rows = jnp.concatenate(
        [w_down[:, :, t * hidden : (t + 1) * hidden] for t in range(thirds)], axis=1
    )
    expert_rows = jnp.concatenate([w_gate, w_up, down_rows], axis=1)
    per_expert = expert_rows.shape[1]
    expert_rows = expert_rows.reshape(GROUP, PAIR_E, per_expert, hidden).transpose(1, 0, 2, 3)

    c_own, expert_rows = tie(core(cotangent), expert_rows)
    expert_rows = lax.all_to_all(expert_rows, "fsdp", 1, 1, tiled=True, axis_index_groups=inside)

    def over_all(block):
        return lax.all_gather(block, "fsdp", axis=0, axis_index_groups=along)

    aligned = own_rows % 16 == 0 and own_hidden % 16 == 0

    def expert_parts(gathered):
        if aligned:
            return (gathered,)
        gate = gathered[:, :, :own_rows].reshape(width, hidden)
        up = gathered[:, :, own_rows : 2 * own_rows].reshape(width, hidden)
        low = gathered[:, :, 2 * own_rows :].reshape(layers, GROUP, thirds, own_hidden, hidden)
        return gate, up, low.transpose(0, 1, 3, 2, 4).reshape(hidden, width)

    segment, position = layout(lengths[0], rows)
    cosine, sine_val = turn_tables(position)
    half = HK // 4
    c_parts = [cotangent[: rows // 4], cotangent[rows // 4 : rows // 2], cotangent[rows // 2 :]]
    near = lambda block: (swap(block, 2, n), swap(block, 4, n))
    cores = lambda *values: [core(value) for value in values]
    if split:
        ring = list(range(layers))
        plan = [[(k, j) for j in ring] for k in range(6)]
        upper = (layers + 1) // 2
        plan += [[(k, j) for j in part] for k in (6, 7) for part in (ring[:upper], ring[upper:]) if part]
        cut = upper * own_rows
        blocks = ring_start(own_qkv, layers, n)
        column = joined_rows(ring_end(blocks, layers, n), ring)
        column, w_out = tie(column, w_out)

        def far_ways(pair):
            ways = [swap(pair[0][:cut], 4, n)]
            return ways + ([swap(pair[1][cut:], 2, n)] if layers > 1 else [])

        def in_order(own, other, near_two, far):
            return [own, other[0], near_two[0], other[1], near_two[1], other[2], *far, *cores(*far)]

        near_qkv = near(column)
        wo_blocks = ring_start(w_out, layers, n)
        near_qkv, wo_blocks, cosine, sine_val, expert_rows, c_parts = tie(
            near_qkv, wo_blocks, cosine, sine_val, expert_rows, c_parts
        )
        far = far_ways(near_qkv)
        other = cores(column, *near_qkv)
        other, wo_blocks = tie(other, wo_blocks)
        wo_column = joined_rows(ring_end(wo_blocks, layers, n), ring)
        far, other, wo_column = tie(far, other, wo_column)
        pieces = in_order(column, other, near_qkv, far)
        pieces, wo_column, c_parts = tie(pieces, wo_column, c_parts)
        wo_near, wo_other = near(wo_column), core(wo_column)
        table = own_rows * (GROUP * steps[None, :] + members[:, None])
        ring_table = own_rows * (GROUP * ((layer - steps[None, :]) % layers) + members[:, None])
    else:
        pieces = [lax.all_gather(own_qkv, "fsdp", axis=0, tiled=True)]
        plan = [[(0, 0)]]
        table = ring_table = jnp.zeros((1, 1), jnp.int32)
    table, ring_table = table.astype(jnp.int32), ring_table.astype(jnp.int32)

    gathered_first, gathered_second = over_all(expert_rows[0]), over_all(expert_rows[1])
    c_near = [near(c_parts[0])]
    w_qkv, normed, turned, *first_half = attend_forward(
        0, half, ring_table, plan, pieces, hidden_in, cosine, sine_val, segment
    )
    normed, c_near, c_parts = tie(normed, c_near, c_parts)
    if split:
        wo_near, wo_other, normed = tie(wo_near, wo_other, normed)
        wo_far = far_ways(wo_near)
    c_near.append(near(c_parts[1]))
    second_half = attend_forward(half, half, table, None, w_qkv, normed, cosine, sine_val, segment)
    attn_out = (first_half[3], second_half[3])
    if split:
        attn_out, c_parts, wo_far, wo_near, c_near = tie(attn_out, c_parts, wo_far, wo_near, c_near)
        out_pieces = in_order(wo_column, [wo_other, *cores(*wo_near)], wo_near, wo_far)
    else:
        attn_out, c_parts, c_near = tie(attn_out, c_parts, c_near)
        out_pieces = [lax.all_gather(w_out, "fsdp", axis=0, tiled=True)]

    c_near.append(near(c_parts[2]))
    w_out_full, middle, inner, mix = to_middle(
        ring_table, plan, out_pieces, hidden_in, attn_out, w_qkv, routes
    )
    inner_near = gather_start(inner, n)
    inner_other = core(inner)
    c_core = [cores(*pair) for pair in c_near[:2]]
    inner_here, c_near[2] = tie(inner, c_near[2])
    c_core.append(cores(*c_near[2]))
    inner_here, inner_other, c_core[:2] = tie(inner_here, inner_other, c_core[:2])

    def expert_sums(sums):
        if len(sums) == 1:
            return lax.psum_scatter(
                sums[0], "fsdp", scatter_dimension=0, tiled=True, axis_index_groups=along
            )[0]
        gate, up, low = sums
        low = low.reshape(layers, GROUP, own_hidden, thirds, hidden).transpose(0, 1, 3, 2, 4)
        joined = jnp.concatenate(
            [
                gate.reshape(layers, GROUP, own_rows, hidden),
                up.reshape(layers, GROUP, own_rows, hidden),
                low.reshape(layers, GROUP, thirds * own_hidden, hidden),
            ],
            axis=2,
        )
        return lax.psum_scatter(
            joined, "fsdp", scatter_dimension=0, tiled=True, axis_index_groups=along
        )[0]

    first = expert_parts(gathered_first)
    second = expert_parts(gathered_second)
    part = {}

    def run(expert, tiles, xs, cs, weights, sums, last):
        done, sums = experts_call(
            place, expert, xs, cs, weights, own_rows, [part[k] for k in tiles] if expert else None, sums, last
        )
        part.update(zip(tiles, done))
        return sums

    x_own, c_own = [[inner_here], [inner_other]], [[cotangent], [c_own]]
    sums = run(0, [0, 1], x_own, c_own, first, None, False)
    inner_near, c_core[2], sums = tie(inner_near, c_core[2], sums)
    inner_far = gather_far(*inner_near, n)
    cots_far = swap(c_near[0][0], 4, n), swap(c_near[1][0], 4, n), swap(c_near[2][1], 2, n)
    x_near = [[inner_near[0]], [core(inner_near[0])], [inner_near[1]], [core(inner_near[1])]]
    c_all = []
    for q in (0, 1):
        c_all += [[pair[q] for pair in c_near], [pair[q] for pair in c_core]]
    sums = run(0, [2, 3, 4, 5], x_near, c_all, first, sums, False)
    inner_far, cots_far = after((inner_far, cots_far), sums)
    x_far = [list(inner_far), [core(v) for v in inner_far]]
    c_far = [list(cots_far), [core(v) for v in cots_far]]
    sums0 = run(0, [6, 7], x_far, c_far, first, sums, True)
    shared0 = expert_sums(sums0)

    sums = run(1, [6, 7], x_far, c_far, second, None, False)
    both_ways = lambda low, high: (swap(low, 4, n), swap(high, 2, n))
    halves, out_halves = sums_for_far([(part[6][i], core(part[7][i])) for i in (1, 0)])
    x_near[0], halves, out_halves = tie(x_near[0], halves, out_halves)
    far_sums, out_far = both_ways(*halves), both_ways(*out_halves)
    sums = run(1, [2, 3, 4, 5], x_near, c_all, second, sums, False)
    done = [part[k] for k in (2, 3, 4, 5)]
    far_sums, out_far, sums, done = tie(far_sums, out_far, sums, done)
    part.update(zip((2, 3, 4, 5), done))
    near_sums = sums_for_near(part[2][1], core(part[3][1]), part[4][1], core(part[5][1]), *far_sums)
    x_own[0], near_sums, shared0 = tie(x_own[0], near_sums, shared0)
    ways = lambda two, four: [swap(two, 2, n), swap(four, 4, n)]
    inner_near = ways(*near_sums)
    out_core = [core(part[3][0]), core(part[5][0])]
    sums = run(1, [0, 1], x_own, c_own, second, sums, True)
    inner_near, out_core, sums, part[0], part[1] = tie(inner_near, out_core, sums, part[0], part[1])
    shared1 = expert_sums(sums)
    inner_other = core(part[1][1])
    out_blocks = (part[2][0], out_core[0], part[4][0], out_core[1])
    out_sums = half_for_near(0, *out_blocks, out_far[0])
    out_sums, inner_other = tie(out_sums, inner_other)
    out_low = ways(*out_sums)
    def to_owner(block):
        return lax.all_to_all(block, "fsdp", 0, 0, tiled=True, axis_index_groups=inside)

    owned0 = to_owner(shared0)
    out_other = core(part[1][0])
    *out_grads, middle_grad, attn_grad0, attn_grad1 = middle_back(
        table, (part[0][1], inner_other, *inner_near), inner, mix, middle, cotangent, w_qkv, attn_out,
        w_out_full,
    )
    out_low, out_other, owned0, out_grads, middle_grad, attn_grad0, attn_grad1 = tie(
        out_low, out_other, owned0, out_grads, middle_grad, attn_grad0, attn_grad1
    )

    wide = lambda value: value.astype(f32)

    def chips_of(stacks):
        return sums_of_stack(stacks[0], core(stacks[1])) if split else [stacks[0]]

    def far_of(chips):
        return both_ways(*chips[3:]) if split else ()

    def near_sums_of(chips, far):
        return stack_near([(*chips[1:3], *far)]) if split else ()

    def near_of(chips, far):
        return [swap(value, bit, n) for value, bit in zip(near_sums_of(chips, far), (2, 4))]

    def back(base, steps, half_set, grads):
        return attend_backward(
            base, steps, table, turned, *half_set[:3], grads, half_set[4], cosine, sine_val, segment
        )

    wo_chips = chips_of(out_grads)
    out_sums = half_for_near(1, *tie(*out_blocks, middle_grad)[:4], out_far[1])
    attn_grad0, wo_chips, out_sums = tie(attn_grad0, wo_chips, out_sums)
    out_high = ways(*out_sums)
    wo_far = far_of(wo_chips)
    *stacks0, dq0, dk0, dv0 = back(0, half, first_half, attn_grad0)
    out_high, wo_far, stacks0, dq0, dk0, dv0 = tie(out_high, wo_far, stacks0, dq0, dk0, dv0)

    chips0 = chips_of(stacks0)
    attn_grad1, chips0 = tie(attn_grad1, chips0)
    wo_near, far0 = near_of(wo_chips, wo_far), far_of(chips0)
    *stacks1, dq1, dk1, dv1 = back(0, half, second_half, attn_grad1)
    wo_near, far0, stacks1, dq1, dk1, dv1, shared1 = tie(wo_near, far0, stacks1, dq1, dk1, dv1, shared1)

    def summed(group, near_sums):
        own = jnp.concatenate([chips[0] for chips in group], axis=1)
        return (wide(own) + wide(near_sums[0]) + wide(near_sums[1])).astype(bf16)

    chips1 = chips_of(stacks1)
    dq1, chips1 = tie(dq1, chips1)
    near0, far1 = near_of(chips0, far0), far_of(chips1)
    if split:
        wo_shared = lax.psum_scatter(
            summed([wo_chips], wo_near), "fsdp", scatter_dimension=0, tiled=True, axis_index_groups=along
        )
    else:
        wo_shared = lax.psum_scatter(wo_chips[0], "fsdp", scatter_dimension=0, tiled=True)
    input_grad = to_input(hidden_in, middle_grad, w_qkv, (dq0, dk0, dv0, dq1, dk1, dv1))
    near0, far1, input_grad = tie(near0, far1, input_grad)
    near1, near0 = tie(near_sums_of(chips1, far1), near0)
    near1 = [swap(value, bit, n) for value, bit in zip(near1, (2, 4))]

    def over_layers(chips, near_sums):
        if not split:
            return [lax.psum_scatter(chips[0], "fsdp", scatter_dimension=0, tiled=True)]
        total = summed([chips], near_sums)
        return layer_start(total.reshape(layers, own_rows, -1), layer, layers, n)

    late0 = over_layers(chips0, near0)
    owned1 = to_owner(after(shared1, near1))
    out_low, near1, wo_shared, late0 = tie(out_low, near1, wo_shared, late0)
    mine_out = wide(wo_shared)
    out_total = wide(part[0][0]) + wide(out_other) + jnp.concatenate(
        [wide(out_low[0]) + wide(out_low[1]), wide(out_high[0]) + wide(out_high[1])], axis=0
    )
    mixed = (middle + resid_scale * out_total).astype(bf16)
    late1, owned1 = tie(over_layers(chips1, near1), owned1)
    mine = [layer_add(late0), layer_add(late1)]

    shared = jnp.stack([owned0, owned1], axis=1).reshape(E, per_expert, hidden).astype(f32)
    grad_gate, grad_up = shared[:, :own_rows], shared[:, own_rows : 2 * own_rows]
    grad_down = jnp.concatenate(
        [
            shared[:, 2 * own_rows + t * own_hidden : 2 * own_rows + (t + 1) * own_hidden]
            for t in range(thirds)
        ],
        axis=2,
    )
    def joined(kind):
        pieces = []
        for part_grads in mine:
            unit = part_grads.shape[1] // 5
            start, wide = ((0, 3 * unit), (3 * unit, unit), (4 * unit, unit))[kind]
            pieces.append(part_grads[:, start : start + wide])
        return jnp.concatenate(pieces, axis=1)

    grad_query, grad_key, grad_value = joined(0), joined(1), joined(2)
    grad_router = mine_out[:, width : width + E]

    def row_sums(weight, grad):
        return jnp.sum(weight.astype(f32) * grad, axis=-1)

    grad_norm_attn = (
        row_sums(w_query, grad_query) + row_sums(w_key, grad_key) + row_sums(w_value, grad_value)
    ) / norm_attn.astype(f32)
    grad_norm_moe = (
        jnp.sum(row_sums(w_gate, grad_gate) + row_sums(w_up, grad_up), axis=0)
        + row_sums(w_router, grad_router)
    ) / norm_moe.astype(f32)
    return (
        mixed,
        input_grad,
        grad_norm_attn,
        grad_query,
        grad_key,
        grad_value,
        mine_out[:, :width],
        grad_norm_moe,
        grad_router,
        grad_gate,
        grad_up,
        grad_down,
    )


def solution(mesh):

    in_specs = (
        P("fsdp", None),
        P("fsdp", None),
        P("fsdp", None),
        P("fsdp"),
        P("fsdp", None),
        P("fsdp", None),
        P("fsdp", None),
        P("fsdp", None),
        P("fsdp"),
        P("fsdp", None),
        P(None, "fsdp", None),
        P(None, "fsdp", None),
        P(None, "fsdp", None),
        P("fsdp", None),
    )
    out_specs = (
        P("fsdp", None),
        P("fsdp", None),
        P("fsdp"),
        P("fsdp", None),
        P("fsdp", None),
        P("fsdp", None),
        P("fsdp", None),
        P("fsdp"),
        P("fsdp", None),
        P(None, "fsdp", None),
        P(None, "fsdp", None),
        P(None, "fsdp", None),
    )
    return jax.shard_map(
        functools.partial(shards, mesh.shape["fsdp"]),
        mesh=mesh,
        in_specs=in_specs,
        out_specs=out_specs,
        check_vma=False,
    )
```
